32 devices in a mesh: dp: 4 (over z), expert: 2 (over y), tensor: 4 (over x, core).
Axes of the slice: x: 2, y: 2, z: 4, core: 2. Of those that a mesh axis runs over, the one named last changes fastest.
Arguments:
- tokens: bfloat16 [2, 4096, 768], P(None, ('dp', 'expert', 'tensor')), may hold values from -6 to 6
- cotangent: bfloat16 [2, 4096, 768], P(None, ('dp', 'expert', 'tensor')), may hold values from -6 to 6
- row_order: int32 [2, 8, 512], P(None, ('dp', 'expert')), may hold values from 0 to 511, each once within a row
- lengths: int32 [2, 8, 3], P(None, ('dp', 'expert')), may hold values from 1 to 341, 512 in all within a row
- routes: int32 [2, 2, 4096, 2], P(None, None, ('dp', 'expert', 'tensor')), may hold values from 0 to 5, all different within a row; in each aligned block of 128 rows (0 to 127, 128 to 255, ..., all dimensions but the last counted through in order) at most 48 rows name the same one
- norm_gains: float32 [2, 2, 768], replicated, may hold values from 0.25 to 1.75
- w_qkv: bfloat16 [2, 3, 768, 768], P(None, None, None, 'tensor'), may hold values from -0.21875 to 0.21875
- w_out: bfloat16 [2, 768, 768], P(None, 'tensor'), may hold values from -3 to 3
- w_gate_up: bfloat16 [2, 2, 2, 768, 2048], P(None, 'expert', None, None, 'tensor'), may hold values from -0.21875 to 0.21875
- w_down: bfloat16 [2, 2, 2048, 768], P(None, 'expert', 'tensor'), may hold values from -0.25 to 0.25
- w_router: float32 [2, 768, 6], replicated, may hold values from -0.15 to 0.15
- const_proj: float32 [2, 768, 4], replicated, may hold values from -0.2 to 0.2
- const_vec: float32 [2, 2, 768], replicated, may hold values from -6 to 6
Outputs:
- block_out: bfloat16 [2, 4096, 768], P(None, ('dp', 'expert', 'tensor'))
- grad_tokens: float32 [2, 4096, 768], P(None, ('dp', 'expert', 'tensor'))
- grad_gains: float32 [2, 768], replicated
- grad_moe_gains: float32 [2, 768], replicated
- grad_qkv: float32 [2, 3, 768, 768], P(None, None, ('dp', 'expert'), 'tensor')
- grad_out_proj: float32 [2, 768, 768], P(None, 'tensor', ('dp', 'expert'))
- grad_gate_up: float32 [2, 2, 2, 768, 2048], P(None, 'expert', None, 'dp', 'tensor')
- grad_down: float32 [2, 2, 2048, 768], P(None, 'expert', 'tensor', 'dp')
- grad_router: float32 [2, 768, 6], replicated
- grad_const_proj: float32 [2, 768, 4], replicated
- grad_const_vec: float32 [2, 2, 768], replicated
The draws below stay inside these ranges and needn't reach their ends.
Inputs may be any that keep to these rules, and one draw needn't show every extreme that they name: Each pack's row_order holds every position of the pack once. Each pack has 3 documents whose lengths sum to 512; the longest has exactly 341 tokens. A token's two routes differ. Routes below 2 are feed-forward experts, 2 is the zero expert, 3 the copy expert, 4 and 5 the constant experts. Among the rows of one device in one layer and micro-batch no route is named by more than 48 rows, a bound that some block reaches.
All inputs are finite; a program needn't handle non-finite values.
Results may differ from the reference program's by a relative error of at most 0.03.
The reference program's roundings to bfloat16 on the way count: a program that leaves them out, or rounds other values in their place, can miss the bound.
Values may be sent and summed in bfloat16 or wider, within the bound.
No kernel may reach another device: no remote copies, remote signals or barrier semaphores. Data moves between devices by JAX's collectives and lax.ppermute only.
A program may use at most 192 MiB of HBM per device.

```python
import math
import jax
import jax.numpy as jnp
import numpy as np
from jax import lax

D = 768
HEADS = 12
HDIM = 64
FF = 2048
LAYERS = 2
MB = 2
SEGS = 3
SEQ = 512
EXPERTS = 2
ROUTES = 6
PACKS = 8
TOKENS = 4096
QROWS = 128
CAP = 48
LONGEST = 341


def level_of(own_key, extent, pieces, smallest, high):
    level = 1.0
    for axis_at, parts in pieces:
        heights = jax.random.uniform(jax.random.fold_in(jax.random.fold_in(own_key, 6), axis_at), (parts,), jnp.float32, smallest / len(pieces), high / len(pieces))
        level = level * jnp.repeat(jnp.exp(heights), extent[axis_at] // parts).reshape((-1,) + (1,) * (len(extent) - 1 - axis_at))
    return level


def length_profile(amount, total, bound, lean):
    weights = [(1 << 20) // math.isqrt(standing ** lean) + 1 for standing in range(2, amount + 1)]
    rest, counts = total - bound - (amount - 1), [1] * (amount - 1)
    while rest > 0:
        movable = [i for i in range(amount - 1) if counts[i] < bound]
        mass, budget = sum([weights[i] for i in movable]), rest
        for i in movable:
            addition = min(bound - counts[i], max(1, budget * weights[i] // mass), rest)
            counts[i] = counts[i] + addition
            rest = rest - addition
    return np.array([bound] + counts)


def ragged(own_key, amount, total, most, skew):
    if amount == 2:
        one = jax.random.randint(own_key, (), max(1, total - most), min(most, total - 1) + 1)
        return jnp.stack([one, total - one])
    tallies = jnp.asarray(length_profile(amount, total, most, skew), jnp.int32)
    pairs = (amount - 1) // 2
    giver, sink = tallies[1:1 + 2 * pairs:2], tallies[2:2 + 2 * pairs:2]
    slack = jnp.minimum(giver - 1, most - sink)
    passed = jax.random.randint(jax.random.fold_in(own_key, 1), (pairs,), 0, 1 << 20) % (slack + 1)
    tallies = tallies.at[1:1 + 2 * pairs:2].set(giver - passed).at[2:2 + 2 * pairs:2].set(sink + passed)
    return tallies[jax.random.permutation(jax.random.fold_in(own_key, 2), amount)]


def shared_out(key, own, number, rows, count, top, most, skew):
    order = jax.random.permutation(key, count)
    crowded, usual = load_shares(count, rows * top, most, skew, True), load_shares(count, rows * top, most, skew, False)
    places = jnp.arange(count)

    def named(tallies, turn):
        used = int((tallies > 0).sum())
        fixed = max(1, used // 4)
        passed = fixed + (places - fixed + turn * (used - fixed)) % max(1, count - fixed)
        return jnp.zeros((count,), jnp.int32).at[order[jnp.where(places < fixed, places, passed)]].set(jnp.asarray(tallies, jnp.int32))

    tallies = jnp.where(number % 4 == 0, named(crowded, number // 4), named(usual, number - number // 4 - 1))
    mixed = jax.random.permutation(jax.random.fold_in(own, 3), count)
    source_of, receiver = mixed[0:count // 2 * 2:2], mixed[1:count // 2 * 2:2]
    slack = jnp.minimum(tallies[source_of] - 1, most - tallies[receiver]) // 2
    slack = jnp.where((source_of == order[0]) | (receiver == order[0]) | (tallies[receiver] == 0), 0, jnp.maximum(slack, 0))
    passed = jax.random.randint(jax.random.fold_in(own, 4), (count // 2,), 0, 1 << 20) % (slack + 1)
    tallies = tallies.at[source_of].add(-passed).at[receiver].add(passed)
    members = jnp.searchsorted(jnp.cumsum(tallies), jnp.arange(rows * top), side="right").astype(jnp.int32)
    grid = members.reshape(top, rows).T
    grid = grid[jax.random.permutation(jax.random.fold_in(own, 1), rows)]
    turn = jax.random.randint(jax.random.fold_in(own, 2), (rows, 1), 0, top)
    return jnp.take_along_axis(grid, (jnp.arange(top)[None, :] + turn) % top, axis=1)


def load_shares(number_of, total, reach, lean, full):
    portions = [(1 << 20) // math.isqrt(grade ** lean) + 1 for grade in range(1, number_of + 1)]
    largest = reach if full else min(reach, max(-(-total // number_of), total * portions[0] // sum(portions)))
    least = 1 if total - largest >= number_of - 1 else 0
    given, spare = [largest] + [least] * (number_of - 1), total - largest - least * (number_of - 1)
    while spare > 0:
        movable = [i for i in range(1, number_of) if given[i] < largest] or [i for i in range(1, number_of) if given[i] < reach]
        mass, remaining = sum([portions[i] for i in movable]), spare
        for i in movable:
            addition = min(reach - given[i], max(1, remaining * portions[i] // mass), spare)
            given[i] = given[i] + addition
            spare = spare - addition
    return np.array(given)


def bell_draw(own_key, extent, width, most, pieces=(), kind=jnp.bfloat16):
    values = width * jax.random.normal(own_key, extent, jnp.float32)
    if pieces:
        values = values * level_of(own_key, extent, pieces, -0.22, 0.18)
    return jnp.clip(values, -most, most).astype(kind)


def setup_inputs(seed: int = 0) -> dict:
    arg_keys = jax.random.split(jax.random.key(seed), 14)
    tokens = bell_draw(arg_keys[0], (MB, TOKENS, D), 1.0, 6.0, ((1, 32),))
    cotangent = bell_draw(arg_keys[1], (MB, TOKENS, D), 1.0, 6.0, ((1, 32),))
    row_order = jax.vmap(lambda own: jax.random.permutation(own, SEQ))(jax.random.split(arg_keys[2], MB * PACKS)).reshape((MB, PACKS, SEQ)).astype(jnp.int32)
    lengths = jax.vmap(lambda own: ragged(own, SEGS, SEQ, LONGEST, 0))(jax.random.split(arg_keys[3], MB * PACKS)).reshape((MB, PACKS, SEGS)).astype(jnp.int32)
    routes_keys = jax.random.split(jax.random.fold_in(arg_keys[4], 1), LAYERS * MB * TOKENS // QROWS)
    routes_turns = jax.random.permutation(jax.random.fold_in(arg_keys[4], 3), LAYERS * MB * TOKENS // QROWS)
    routes = jax.vmap(lambda own, number: shared_out(jax.random.fold_in(arg_keys[4], 2), own, number, QROWS, ROUTES, 2, CAP, 1))(routes_keys, routes_turns).reshape((LAYERS, MB, TOKENS, 2))
    norm_gains = jnp.clip(1.0 + 0.15 * jax.random.normal(arg_keys[5], (LAYERS, 2, D), jnp.float32), 0.25, 1.75)
    w_qkv = bell_draw(arg_keys[6], (LAYERS, 3, D, D), D ** -0.5, 0.21875, ((3, 4),))
    w_out = bell_draw(arg_keys[7], (LAYERS, D, D), 4 ** -0.5, 3.0, ((1, 4),))
    w_gate_up = bell_draw(arg_keys[8], (LAYERS, EXPERTS, 2, D, FF), D ** -0.5, 0.21875, ((1, 2), (4, 4)))
    w_down = bell_draw(arg_keys[9], (LAYERS, EXPERTS, FF, D), (FF // 4) ** -0.5, 0.25, ((1, 2), (2, 4)))
    w_router = bell_draw(arg_keys[10], (LAYERS, D, ROUTES), 0.025, 0.15, (), jnp.float32)
    const_proj = bell_draw(arg_keys[11], (LAYERS, D, 4), 0.036, 0.2, (), jnp.float32)
    const_vec = bell_draw(arg_keys[12], (LAYERS, 2, D), 1.0, 6.0, (), jnp.float32)
    return {"tokens": tokens, "cotangent": cotangent, "row_order": row_order, "lengths": lengths, "routes": routes, "norm_gains": norm_gains, "w_qkv": w_qkv, "w_out": w_out, "w_gate_up": w_gate_up, "w_down": w_down, "w_router": w_router, "const_proj": const_proj, "const_vec": const_vec}


@jax.custom_vjp
def low(v):
    return lax.optimization_barrier(v.astype(jnp.bfloat16)).astype(jnp.float32)

@jax.custom_vjp
def low_back(v):
    return v

def low_keep(v):
    return (low(v), None)

def low_pass(kept, grad):
    return (grad,)

def back_keep(v):
    return (v, None)

def back_low(kept, grad):
    return (low(grad),)
low.defvjp(low_keep, low_pass)
low_back.defvjp(back_keep, back_low)
epsilon = 1e-06
score_scale = 0.125
masked_value = -1e+30
highest = lax.Precision.HIGHEST

def positions(order_row, lengths_row):
    starts = jnp.cumsum(lengths_row, dtype=jnp.int32) - lengths_row
    reached = order_row[:, None] >= starts[None, :]
    segment = lax.optimization_barrier(jnp.sum(reached.astype(jnp.int32), axis=1, dtype=jnp.int32))
    offset = lax.optimization_barrier(jnp.max(jnp.where(reached, starts[None, :], 0), axis=1))
    return (segment, order_row - offset)

def rope_tables(relative):
    half_dim = HDIM // 2
    frequency = jnp.exp(-math.log(10000.0) * jnp.arange(half_dim, dtype=jnp.float32) / half_dim)
    angles = relative.astype(jnp.float32)[:, None] * frequency[None, :]
    return (jnp.cos(angles), jnp.sin(angles))

def rotate(values, cosine, sine_table):
    half_dim = values.shape[-1] // 2
    first_half = values[..., :half_dim]
    second_half = values[..., half_dim:]
    cos_part = cosine[:, None, :]
    sin_part = sine_table[:, None, :]
    return jnp.concatenate([first_half * cos_part - second_half * sin_part, second_half * cos_part + first_half * sin_part], axis=-1)

def attend_pack(packed):
    query_raw, key_raw, value_rows, order_row, lengths_row = packed
    segment, relative = positions(order_row, lengths_row)
    cosine, sine_table = rope_tables(relative)
    queries = low(rotate(query_raw, cosine, sine_table))
    key_rows = low(rotate(key_raw, cosine, sine_table))
    allowed = (segment[:, None] == segment[None, :]) & (order_row[None, :] <= order_row[:, None])
    scores = low_back(jnp.einsum('qhd,khd->hqk', queries, key_rows, precision=highest) * score_scale)
    scores = jnp.where(allowed[None], scores, masked_value)
    row_peak = lax.optimization_barrier(jnp.max(scores, axis=-1, keepdims=True))
    exponent = jnp.exp(scores - row_peak)
    attention = low(exponent / lax.optimization_barrier(jnp.sum(exponent, axis=-1, keepdims=True)))
    return jnp.einsum('hqk,khd->qhd', attention, value_rows, precision=highest)

def norm_rows(stream, gain):
    return stream * lax.rsqrt(lax.optimization_barrier(jnp.mean(stream * stream, axis=-1, keepdims=True)) + epsilon) * gain

def expert_branch(h_moe, gate_up, down_proj):
    gate_up_pre = low_back(jnp.einsum('td,cdf->ctf', h_moe, gate_up, precision=highest))
    hidden = low(jax.nn.silu(gate_up_pre[0]) * gate_up_pre[1])
    return low_back(jnp.dot(hidden, down_proj, precision=highest))

def layer_forward(stream, previous, routes_now, order_now, lengths_now, weights):
    gains_layer, qkv_layer, out_layer, gate_up_layer, down_layer, router_layer, proj_layer, vec_layer = weights
    token_count = stream.shape[0]
    h_attn = low(norm_rows(stream, gains_layer[0]))
    projected = low_back(jnp.einsum('td,cdf->ctf', h_attn, qkv_layer, precision=highest))
    shaped = projected.reshape(3, PACKS, SEQ, HEADS, HDIM)
    value_rows = low(shaped[2])
    mixed = lax.map(jax.checkpoint(attend_pack), (shaped[0], shaped[1], value_rows, order_now, lengths_now))
    mixed = low(low_back(mixed.reshape(token_count, D)))
    stream = stream + low_back(jnp.dot(mixed, out_layer, precision=highest))
    h_moe = low(norm_rows(stream, gains_layer[1]))
    logits = jnp.dot(h_moe, router_layer, precision=highest) + previous
    chosen = (routes_now[:, :, None] == jnp.arange(ROUTES, dtype=jnp.int32)[None, None, :]).astype(jnp.float32)
    picked = jnp.einsum('tkr,tr->tk', chosen, logits, precision=highest)
    gate_exp = jnp.exp(picked - lax.optimization_barrier(jnp.max(picked, axis=-1, keepdims=True)))
    gate_weights = gate_exp / lax.optimization_barrier(jnp.sum(gate_exp, axis=-1, keepdims=True))
    route_weight = jnp.einsum('tk,tkr->tr', gate_weights, chosen, precision=highest)
    const_logits = jnp.dot(h_moe, proj_layer, precision=highest).reshape(token_count, 2, 2)
    const_exp = jnp.exp(const_logits - lax.optimization_barrier(jnp.max(const_logits, axis=-1, keepdims=True)))
    mixing = const_exp / lax.optimization_barrier(jnp.sum(const_exp, axis=-1, keepdims=True))
    moe_sum = route_weight[:, EXPERTS + 1:EXPERTS + 2] * h_moe
    for const_index in range(2):
        const_out = mixing[:, const_index, 0:1] * h_moe + mixing[:, const_index, 1:2] * vec_layer[const_index][None, :]
        moe_sum = moe_sum + route_weight[:, EXPERTS + 2 + const_index:EXPERTS + 3 + const_index] * const_out
    branch = jax.checkpoint(expert_branch)
    for expert_index in range(EXPERTS):
        moe_sum = moe_sum + route_weight[:, expert_index:expert_index + 1] * branch(h_moe, gate_up_layer[expert_index], down_layer[expert_index])
    return (stream + moe_sum, logits)

def reference(tokens, cotangent, row_order, lengths, routes, norm_gains, w_qkv, w_out, w_gate_up, w_down, w_router, const_proj, const_vec):
    params = tuple((weight.astype(jnp.float32) for weight in (norm_gains, w_qkv, w_out, w_gate_up, w_down, w_router, const_proj, const_vec)))

    def forward(stream_in, gains_all, qkv_all, out_all, gate_up_all, down_all, router_all, proj_all, vec_all):
        finals = []
        for micro_index in range(MB):
            stream = stream_in[micro_index]
            previous = jnp.zeros((TOKENS, ROUTES), jnp.float32)
            for layer_index in range(LAYERS):
                weights = (gains_all[layer_index], qkv_all[layer_index], out_all[layer_index], gate_up_all[layer_index], down_all[layer_index], router_all[layer_index], proj_all[layer_index], vec_all[layer_index])
                stream, previous = layer_forward(stream, previous, routes[layer_index, micro_index], row_order[micro_index], lengths[micro_index], weights)
            finals.append(stream)
        return jnp.stack(finals)
    result, pullback = jax.vjp(forward, tokens.astype(jnp.float32), *params)
    gradients = pullback(cotangent.astype(jnp.float32))
    gain_grads = gradients[1]
    return (result.astype(jnp.bfloat16), gradients[0], gain_grads[:, 0], gain_grads[:, 1], gradients[2], gradients[3], gradients[4], gradients[5], gradients[6], gradients[7], gradients[8])
```

```python
import functools
import math

import jax
import jax.numpy as jnp
from jax import lax
from jax.experimental import pallas as pl
from jax.experimental.pallas import tpu as pltpu
from jax.sharding import PartitionSpec as P

HDIM = 64
epsilon = 1e-06
masked_value = -1e30
highest = lax.Precision.HIGHEST
low = jnp.bfloat16
full = jnp.float32
MIB = 1 << 20


def shape_of(shape, dtype):
    return jax.ShapeDtypeStruct(shape, dtype)


def run_kernel(body, outs, ins, name, limit, flops=0, scratch=()):
    in_bytes = sum(a.size * a.dtype.itemsize for a in ins)
    out_bytes = sum(math.prod(o.shape) * jnp.dtype(o.dtype).itemsize for o in outs)
    vmem = pl.BlockSpec(memory_space=pltpu.VMEM)
    return pl.pallas_call(
        body,
        out_shape=tuple(outs),
        in_specs=[vmem] * len(ins),
        out_specs=tuple([vmem] * len(outs)),
        scratch_shapes=list(scratch),
        compiler_params=pltpu.CompilerParams(vmem_limit_bytes=limit * MIB),
        cost_estimate=pl.CostEstimate(
            flops=flops, bytes_accessed=in_bytes + out_bytes, transcendentals=0
        ),
        name=name,
    )(*ins)


def dot(a, b):
    return jnp.dot(a, b, preferred_element_type=full)


def dot_nt(a, b):
    return lax.dot_general(a, b, (((1,), (1,)), ((), ())), preferred_element_type=full)


def dot_tn(a, b):
    return lax.dot_general(a, b, (((0,), (0,)), ((), ())), preferred_element_type=full)


def lanes(rows, width=128):
    return lax.broadcasted_iota(jnp.int32, (rows, width), 1)


def stack_rows(refs):
    if refs[0].shape[0] % 16:
        return jnp.concatenate([r[...].astype(full) for r in refs], axis=0).astype(low)
    return jnp.concatenate([r[...] for r in refs], axis=0)


def rms_scale(rows):
    return lax.rsqrt(jnp.mean(rows * rows, axis=-1, keepdims=True) + epsilon)


def split2(rows):
    top = rows.astype(low)
    return top, (rows - top.astype(full)).astype(low)


def norm_kernel(stream, gain, out):
    rows = stream[...].astype(full)
    out[...] = (rows * rms_scale(rows) * gain[...]).astype(low)


def half_masks():
    lane = lanes(1)
    return (lane < HDIM).astype(full).astype(low), (lane >= HDIM).astype(full).astype(low)


def swap_halves(rows):
    lane = lanes(rows.shape[0])
    half = HDIM // 2
    return jnp.where(
        lane % HDIM < half, pltpu.roll(rows, 128 - half, 1), pltpu.roll(rows, half, 1)
    )


def attn_fwd_kernel(blocks, *refs):
    heads = refs[:blocks]
    w, wo, cos, sin, bias, keep, far, send, saved, mixed, logsum = refs[blocks:]
    rows_n = keep.shape[0]
    width = 128
    h = stack_rows(heads)
    proj = dot(h, w[...])
    c = cos[...]
    s = sin[...]
    lane = lanes(proj.shape[0])

    def turn(chunk):
        return chunk * c + swap_halves(chunk) * s

    saved[:, 0:128] = (turn(proj[:, 0:128]) * 0.125).astype(low)
    saved[:, 128:256] = turn(proj[:, 128:256]).astype(low)
    saved[:, 256:384] = proj[:, 256:384].astype(low)
    third = turn(proj[:, 384:512])
    saved[:, 384:512] = jnp.where(lane < HDIM, third * 0.125, 0.0).astype(low)
    saved[:, 512:640] = jnp.where(lane < HDIM, pltpu.roll(third, HDIM, 1), 0.0).astype(low)
    saved[:, 640:768] = proj[:, 512:640].astype(low)
    first, second = half_masks()
    lane = lanes(rows_n)
    for i in range(blocks):
        part = slice(i * rows_n, (i + 1) * rows_n)
        shift = bias[part, :].astype(full)
        q01 = saved[part, 0:128]
        q2 = saved[part, 384:512]
        results = []
        sums = []
        for query, keys, values in (
            (q01 * first, slice(128, 256), slice(256, 384)),
            (q01 * second, slice(128, 256), slice(256, 384)),
            (q2, slice(512, 640), slice(640, 768)),
        ):
            scores = dot_nt(query, saved[:, keys]) + shift
            peak = jnp.max(scores, axis=-1, keepdims=True)
            exponent = jnp.exp(scores - peak)
            total = jnp.sum(exponent, axis=-1, keepdims=True)
            probs = (exponent * (1.0 / total)).astype(low)
            results.append(dot(probs, saved[:, values]))
            sums.append(peak + jnp.log(total))
        logsum[part, :] = jnp.where(lane == 0, sums[0], jnp.where(lane == 1, sums[1], sums[2]))
        mix = jnp.concatenate(
            [jnp.where(lane < HDIM, results[0], results[1]), results[2]], axis=1
        ).astype(low)
        mixed[part, :] = mix
        value = dot(mix, wo[...]).astype(low)
        if i == 0:
            keep[...] = value
        elif i == 2:
            far[...] = value
        else:
            at = (i // 2) * rows_n
            send[at : at + rows_n, :] = value


def attn_bwd_kernel(blocks, *refs):
    grads = refs[:blocks]
    (w, wo, cos, sin, bias, saved, logsum, keep, far, send, dqkv, probs_s, dscore_s, dq_s) = refs[
        blocks:
    ]
    rows_n = keep.shape[0]
    c = cos[...]
    s = sin[...]
    dattn = stack_rows(grads)
    dmix = dot_nt(dattn, wo[...]).astype(low)
    d01 = dmix[:, 0:128]
    d2 = dmix[:, 128:256]
    first, second = half_masks()
    q01 = saved[:, 0:128]
    k01 = saved[:, 128:256]
    v01 = saved[:, 256:384]
    q2 = saved[:, 384:512]
    k2 = saved[:, 512:640]
    v2 = saved[:, 640:768]
    heads = (
        (q01 * first, k01 * first, v01, d01 * first),
        (q01 * second, k01 * second, v01, d01 * second),
        (q2, k2, v2, d2),
    )
    dks = []
    dvs = []
    for n, (query, keys, values, dout) in enumerate(heads):
        for i in range(blocks):
            part = slice(i * rows_n, (i + 1) * rows_n)
            scores = dot_nt(query[part], keys) + bias[part, :].astype(full)
            probs = jnp.exp(scores - logsum[part, n : n + 1])
            dprobs = dot_nt(dout[part], values)
            inner = jnp.sum(probs * dprobs, axis=-1, keepdims=True)
            dscores = (probs * (dprobs - inner)).astype(low)
            probs_s[part, :] = probs.astype(low)
            dscore_s[part, :] = dscores
            dq = dot(dscores, keys)
            if n == 1:
                dq_s[part, 0:128] += dq
            else:
                at = 128 * (n // 2)
                dq_s[part, at : at + 128] = dq
        dks.append(dot_tn(dscore_s[...], query))
        dvs.append(dot_tn(probs_s[...], dout))

    def turn_back(chunk):
        return chunk * c - swap_halves(chunk) * s

    dqkv[:, 0:128] = turn_back(dq_s[:, 0:128] * 0.125).astype(low)
    dqkv[:, 128:256] = turn_back(dks[0] + dks[1]).astype(low)
    dqkv[:, 256:384] = (dvs[0] + dvs[1]).astype(low)
    dqkv[:, 384:512] = turn_back(
        dq_s[:, 128:256] * 0.125 + pltpu.roll(dks[2], HDIM, 1)
    ).astype(low)
    dqkv[:, 512:640] = dvs[2].astype(low)
    dh = dot_nt(dqkv[...], w[...]).astype(low)
    keep[...] = dh[0:rows_n]
    far[...] = dh[2 * rows_n : 3 * rows_n]
    send[0:rows_n, :] = dh[rows_n : 2 * rows_n]
    send[rows_n : 2 * rows_n, :] = dh[3 * rows_n : 4 * rows_n]


def attn_weights_kernel(blocks, micro, *refs):
    out = refs[-1]
    refs = refs[:-1]
    per = 2 * blocks + 2
    for m in range(micro):
        mine = refs[m * per : (m + 1) * per]
        h = stack_rows(mine[:blocks])
        d = stack_rows(mine[blocks : 2 * blocks])
        dqkv, mixed = mine[2 * blocks :]
        qkv_part = dot_tn(h, dqkv[...])
        out_part = dot_tn(d, mixed[...])
        if m:
            qkv_total = qkv_total + qkv_part
            out_total = out_total + out_part
        else:
            qkv_total, out_total = qkv_part, out_part
    out[:, 0:512] = qkv_total[:, 0:512].astype(low)
    out[:, 512:640] = (qkv_total[:, 512:640] + pltpu.roll(out_total[:, 128:256], HDIM, 1)).astype(
        low
    )
    out[:, 640:768] = out_total[:, 0:128].astype(low)


def add_far_kernel(far, arrived, out):
    rows_n = far.shape[0]
    out[...] = (far[...].astype(full) + arrived[rows_n : 2 * rows_n, :].astype(full)).astype(low)


def add_back_kernel(keep, arrived, *outs):
    total = keep[...].astype(full) + arrived[...].astype(full)
    rows_n = outs[0].shape[0]
    for i, out in enumerate(outs):
        out[...] = total[i * rows_n : (i + 1) * rows_n].astype(low)


def mid_kernel(
    experts_n,
    routes_n,
    keep,
    arrived,
    across,
    stream,
    gain,
    router,
    routes_col,
    routes_row,
    previous,
    mid,
    h_moe,
    logits_out,
    aux,
    pick,
    *bufs,
):
    rows_n = keep.shape[0]
    capacity = bufs[0].shape[0]
    rows = (
        stream[...].astype(full)
        + keep[...].astype(full)
        + arrived[0:rows_n, :].astype(full)
        + across[...].astype(full)
    )
    mid[...] = rows
    h = (rows * rms_scale(rows) * gain[...]).astype(low)
    h_moe[...] = h
    parts = dot(h, router[...])
    raw = parts[:, 0:128] + parts[:, 128:256] + parts[:, 256:384]
    lane = lanes(rows_n)
    logits = raw + previous[...]
    logits_out[...] = jnp.where(lane < routes_n, logits, 0.0)
    picked = [
        jnp.sum(jnp.where(lane == routes_col[:, k : k + 1], logits, 0.0), axis=-1, keepdims=True)
        for k in range(2)
    ]
    peak = jnp.maximum(picked[0], picked[1])
    gate = [jnp.exp(p - peak) for p in picked]
    both = gate[0] + gate[1]
    columns = [gate[0] / both, gate[1] / both]
    for j in range(2):
        pair = [raw[:, routes_n + 2 * j + i : routes_n + 2 * j + i + 1] for i in range(2)]
        peak = jnp.maximum(pair[0], pair[1])
        power = [jnp.exp(p - peak) for p in pair]
        both = power[0] + power[1]
        columns += [power[0] / both, power[1] / both]
    value = jnp.zeros((rows_n, 128), full)
    for i, column in enumerate(columns):
        value = jnp.where(lane == i, column, value)
    aux[...] = value
    index_rows = max(16, experts_n)
    expert = lax.broadcasted_iota(jnp.int32, (index_rows, rows_n), 0)
    first = routes_row[0:1, :]
    second = routes_row[1:2, :]
    member = ((first == expert) | (second == expert)).astype(full).astype(low)
    before = (
        lax.broadcasted_iota(jnp.int32, (rows_n, rows_n), 0)
        < lax.broadcasted_iota(jnp.int32, (rows_n, rows_n), 1)
    )
    rank = dot(member, before.astype(full).astype(low))
    slot = lax.broadcasted_iota(jnp.int32, (capacity, rows_n), 0).astype(full)
    picks = []
    for route in (first, second):
        picks.append(
            jnp.concatenate(
                [
                    ((slot == rank[k : k + 1, :]) & (route == k)).astype(full)
                    for k in range(experts_n)
                ],
                axis=0,
            )
        )
    pick[:, 0:rows_n] = picks[0].astype(low)
    pick[:, rows_n : 2 * rows_n] = picks[1].astype(low)
    sent = dot((picks[0] + picks[1]).astype(low), h)
    for k, buf in enumerate(bufs):
        buf[...] = sent[k * capacity : (k + 1) * capacity].astype(low)


def route_values(experts_n, pick, arrivals, aux, routes_col, h, vec):
    rows_n = h.shape[0]
    twice = jnp.concatenate([pick[...], pick[...]], axis=0)
    both = dot_tn(twice, stack_rows(arrivals))
    values = []
    for k in range(2):
        route = routes_col[:, k : k + 1]
        scale = (route == experts_n + 1).astype(full)
        value = both[k * rows_n : (k + 1) * rows_n]
        for j in range(2):
            here = (route == experts_n + 2 + j).astype(full)
            scale = scale + here * aux[:, 2 + 2 * j : 3 + 2 * j]
            value = value + (here * aux[:, 3 + 2 * j : 4 + 2 * j]) * vec[j : j + 1, :]
        values.append(value + scale * h)
    return values


def combine_kernel(experts_n, arrivals_n, last, *refs):
    arrivals = refs[:arrivals_n]
    pick, aux, routes_col, h_moe, mid, vec = refs[arrivals_n : arrivals_n + 6]
    values = route_values(
        experts_n, pick, arrivals, aux, routes_col, h_moe[...].astype(full), vec
    )
    rows = mid[...] + aux[:, 0:1] * values[0] + aux[:, 1:2] * values[1]
    if last:
        refs[-1][...] = rows.astype(low)
    else:
        gain, stream, h_next = refs[arrivals_n + 6 :]
        stream[...] = rows
        h_next[...] = (rows * rms_scale(rows) * gain[...]).astype(low)


def route_back(
    experts_n, routes_n, dstream, arrivals, pick, aux, routes_col, h_moe, vec, router_back, dnext,
    dlogits_out, dlocal, small, bufs,
):
    rows_n = dstream.shape[0]
    lane = lanes(rows_n)
    h_low = h_moe[...]
    h = h_low.astype(full)
    values = route_values(experts_n, pick, arrivals, aux, routes_col, h, vec)
    gates = [aux[:, k : k + 1] for k in range(2)]
    dgate = [jnp.sum(dstream * v, axis=-1, keepdims=True) for v in values]
    mean = gates[0] * dgate[0] + gates[1] * dgate[1]
    dlogits = dnext
    for k in range(2):
        dlogits = dlogits + jnp.where(
            lane == routes_col[:, k : k + 1], gates[k] * (dgate[k] - mean), 0.0
        )
    dlogits_out[...] = dlogits

    def gate_of(route):
        return sum(
            (routes_col[:, k : k + 1] == route).astype(full) * gates[k] for k in range(2)
        )

    along_h = jnp.sum(dstream * h, axis=-1, keepdims=True)
    scale = gate_of(experts_n + 1)
    both = dlogits
    for j in range(2):
        share = gate_of(experts_n + 2 + j)
        mix = [aux[:, 2 + 2 * j + i : 3 + 2 * j + i] for i in range(2)]
        along_v = jnp.sum(dstream * vec[j : j + 1, :], axis=-1, keepdims=True)
        dm = [share * along_h, share * along_v]
        inner = mix[0] * dm[0] + mix[1] * dm[1]
        for i in range(2):
            both = jnp.where(lane == routes_n + 2 * j + i, mix[i] * (dm[i] - inner), both)
        scale = scale + mix[0] * share
        small[24 + j : 25 + j, :] = jnp.sum((mix[1] * share) * dstream, axis=0, keepdims=True)
    dlocal[...] = scale * dstream + jnp.dot(
        both, router_back[...], precision=highest, preferred_element_type=full
    )
    top, rest = split2(both)
    small[0:24, :] = (dot_tn(top, h_low) + dot_tn(rest, h_low))[0:24]
    rows_n = h.shape[0]
    sent = dot(pick[:, 0:rows_n], (gates[0] * dstream).astype(low)) + dot(
        pick[:, rows_n : 2 * rows_n], (gates[1] * dstream).astype(low)
    )
    capacity = bufs[0].shape[0]
    for k, buf in enumerate(bufs):
        buf[...] = sent[k * capacity : (k + 1) * capacity].astype(low)


def last_back_kernel(experts_n, routes_n, arrivals_n, *refs):
    arrivals = refs[:arrivals_n]
    cotangent, pick, aux, routes_col, h_moe, vec, router_back = refs[arrivals_n : arrivals_n + 7]
    dlogits, dlocal, small, *bufs = refs[arrivals_n + 7 :]
    dstream = cotangent[...].astype(full)
    small[24:32, :] = jnp.zeros((8, small.shape[1]), full)
    route_back(
        experts_n, routes_n, dstream, arrivals, pick, aux, routes_col, h_moe, vec, router_back,
        jnp.zeros((dstream.shape[0], 128), full), dlogits, dlocal, small, bufs,
    )


def attn_norm_back(keep, arrived, across, stream, gain, dmid, dgain):
    rows_n = keep.shape[0]
    dh = (
        keep[...].astype(full)
        + arrived[0:rows_n, :].astype(full)
        + across[...].astype(full)
    )
    rows = stream[...].astype(full)
    scale = rms_scale(rows)
    unit = rows * scale
    dgain[...] = jnp.broadcast_to(jnp.sum(dh * unit, axis=0, keepdims=True), dgain.shape)
    dn = dh * gain[...]
    return dmid[...] + scale * (dn - unit * jnp.mean(dn * unit, axis=-1, keepdims=True))


def input_back_kernel(keep, arrived, across, stream, gain, dmid, dgain, out):
    out[...] = attn_norm_back(keep, arrived, across, stream, gain, dmid, dgain)


def next_back_kernel(experts_n, routes_n, arrivals_n, *refs):
    arrivals = refs[:arrivals_n]
    (keep, arrived, across, stream, gain, dmid, pick, aux, routes_col, h_moe, vec, router_back,
     dnext) = refs[arrivals_n : arrivals_n + 13]
    dgain, dstream_out, dlogits, dlocal, small, *bufs = refs[arrivals_n + 13 :]
    dstream = attn_norm_back(keep, arrived, across, stream, gain, dmid, dgain)
    dstream_out[...] = dstream
    small[24:32, :] = jnp.zeros((8, small.shape[1]), full)
    route_back(
        experts_n, routes_n, dstream, arrivals, pick, aux, routes_col, h_moe, vec, router_back,
        dnext[...], dlogits, dlocal, small, bufs,
    )


def expert_fwd_kernel(rows_in, *refs):
    blocks = refs[:rows_in]
    gate_up, down, keep, send = refs[rows_in:]
    rows = stack_rows(blocks)
    g = dot(rows, gate_up[0])
    u = dot(rows, gate_up[1])
    hidden = (g * jax.nn.sigmoid(g) * u).astype(low)
    value = dot(hidden, down[...]).astype(low)
    half = keep.shape[0]
    keep[...] = value[0:half]
    send[...] = value[half:]


def expert_bwd_kernel(rows_in, *refs):
    rows = stack_rows(refs[:rows_in])
    grads = stack_rows(refs[rows_in : 2 * rows_in])
    gate_up, down, keep, send, hidden_out, dgu_out = refs[2 * rows_in :]
    g = dot(rows, gate_up[0])
    u = dot(rows, gate_up[1])
    dhidden = dot_nt(grads, down[...])
    s = jax.nn.sigmoid(g)
    silu = g * s
    hidden_out[...] = (silu * u).astype(low)
    dg = (dhidden * u * s * (1.0 + g * (1.0 - s))).astype(low)
    du = (dhidden * silu).astype(low)
    width = g.shape[1]
    dgu_out[:, 0:width] = dg
    dgu_out[:, width : 2 * width] = du
    value = (dot_nt(dg, gate_up[0]) + dot_nt(du, gate_up[1])).astype(low)
    half = keep.shape[0]
    keep[...] = value[0:half]
    send[...] = value[half:]


def expert_weights_kernel(rows_in, micro, *refs):
    out = refs[-1]
    per = 2 * rows_in + 2
    groups = [refs[m * per : (m + 1) * per] for m in range(micro)]
    rows = jnp.concatenate([stack_rows(g[:rows_in]) for g in groups], axis=0)
    grads = jnp.concatenate([stack_rows(g[rows_in : 2 * rows_in]) for g in groups], axis=0)
    hidden = jnp.concatenate([g[2 * rows_in][...] for g in groups], axis=0)
    dgu = jnp.concatenate([g[2 * rows_in + 1][...] for g in groups], axis=0)
    width = dgu.shape[1]
    out[:, 0:width] = dot_tn(rows, dgu).astype(low)
    out[:, width : width + hidden.shape[1]] = dot_tn(grads, hidden).astype(low)


def expert_norm_back_kernel(arrivals_n, *refs):
    arrivals = refs[:arrivals_n]
    pick, dlocal, mid, gain, dstream, dmid, dattn, dgain = refs[arrivals_n:]
    rows_n = mid.shape[0]
    both = pick[:, 0:rows_n] + pick[:, rows_n : 2 * rows_n]
    twice = jnp.concatenate([both, both], axis=0)
    dh = dlocal[...] + dot_tn(twice, stack_rows(arrivals))
    rows = mid[...]
    scale = rms_scale(rows)
    unit = rows * scale
    dgain[...] = jnp.broadcast_to(jnp.sum(dh * unit, axis=0, keepdims=True), dgain.shape)
    dn = dh * gain[...]
    value = dstream[...].astype(full) + scale * (
        dn - unit * jnp.mean(dn * unit, axis=-1, keepdims=True)
    )
    dmid[...] = value
    dattn[...] = value.astype(low)


def swap(x, axis, k):
    n = lax.axis_size(axis)
    return lax.ppermute(x, axis, [(i, i ^ k) for i in range(n)])


def swap_pair(x, k, j):
    experts_n = lax.axis_size("expert")
    tensor_n = lax.axis_size("tensor")
    if j == 0:
        return swap(x, "expert", k)
    if k == 0:
        return swap(x, "tensor", j)
    table = [
        (e * tensor_n + t, (e ^ k) * tensor_n + (t ^ j))
        for e in range(experts_n)
        for t in range(tensor_n)
    ]
    return lax.ppermute(x, ("expert", "tensor"), table)


def gather_pack(block):
    near = swap(block, "tensor", 1)
    far = swap(block, "tensor", 2)
    return [block, near, far, swap(far, "tensor", 1)]


def sum_pack(keep, far, send):
    arrived = swap(send, "tensor", 1)
    (total,) = run_kernel(
        add_far_kernel, [shape_of(far.shape, low)], [far, arrived], "add_far", 8
    )
    return keep, arrived, swap(total, "tensor", 2)


def send_rows(bufs):
    experts_n = len(bufs)
    held = []
    for j in (0, 2):
        for k in range(experts_n):
            held.append(bufs[k] if (j, k) == (0, 0) else swap_pair(bufs[k], k, j))
    return held + [swap(x, "tensor", 1) for x in held]


def return_rows(keep, send, capacity):
    experts_n = lax.axis_size("expert")
    arrived = swap(send, "tensor", 1)
    sums = run_kernel(
        add_back_kernel,
        [shape_of((capacity, keep.shape[1]), low)] * (2 * experts_n),
        [keep, arrived],
        "add_back",
        8,
    )
    out = []
    for j in (0, 2):
        for k in range(experts_n):
            part = sums[(j // 2) * experts_n + k]
            out.append(part if (j, k) == (0, 0) else swap_pair(part, k, j))
    return out


def sum_all(rows):
    for axis in ("tensor", "expert", "dp"):
        bit = 1
        while bit < lax.axis_size(axis):
            rows = rows + swap(rows, axis, bit)
            bit *= 2
    return rows


def sum_owner(grad, axis):
    n = lax.axis_size(axis)
    here = lax.axis_index(axis)

    def piece(k):
        return lax.dynamic_index_in_dim(grad, here ^ k, 0, keepdims=False)

    pieces = [piece(0)] + [swap(piece(k), axis, k) for k in range(1, n)]
    return functools.reduce(lambda a, b: a + b, [p.astype(full) for p in pieces])


def pack_tables(row_order, lengths, width):
    tensor_n = lax.axis_size("tensor")
    mine = lax.axis_index("tensor")
    micro_n, seq = row_order.shape
    cut = row_order.reshape(micro_n, tensor_n, seq // tensor_n)
    order = jnp.concatenate(
        [
            lax.dynamic_index_in_dim(cut, mine ^ j, 1, keepdims=False)
            for j in range(tensor_n)
        ],
        axis=1,
    )
    starts = jnp.cumsum(lengths, axis=1, dtype=jnp.int32) - lengths
    reached = order[:, :, None] >= starts[:, None, :]
    begin = jnp.max(jnp.where(reached, starts[:, None, :], 0), axis=2)
    half = HDIM // 2
    lane = jnp.arange(width, dtype=jnp.int32)
    frequency = jnp.exp(
        -math.log(10000.0) * (lane % half).astype(full) / half
    )
    angles = (order - begin).astype(full)[:, :, None] * frequency[None, None, :]
    sign = jnp.where(lane % HDIM < half, -1.0, 1.0)
    allowed = (begin[:, :, None] <= order[:, None, :]) & (order[:, None, :] <= order[:, :, None])
    bias = jnp.where(allowed, 0.0, masked_value).astype(low)
    return jnp.cos(angles), jnp.sin(angles) * sign, bias


def local(
    tokens,
    cotangent,
    row_order,
    lengths,
    routes,
    norm_gains,
    w_qkv,
    w_out,
    w_gate_up,
    w_down,
    w_router,
    const_proj,
    const_vec,
):
    layers = w_qkv.shape[0]
    micro_n, rows_n, model = tokens.shape
    routes_n = w_router.shape[2]
    experts_n = lax.axis_size("expert")
    tensor_n = lax.axis_size("tensor")
    dp_n = lax.axis_size("dp")
    capacity = 9 * rows_n // (4 * (experts_n + 4))
    heads_width = w_qkv.shape[3]
    hidden_n = w_down.shape[2]
    seq = tensor_n * rows_n
    expert_rows = 2 * experts_n * capacity
    assert tensor_n == 4 and heads_width == 3 * HDIM and rows_n == 128

    cos, sin, bias = pack_tables(row_order[:, 0], lengths[:, 0], 128)
    pair = 2 * HDIM
    w_cat = jnp.concatenate(
        [
            w_qkv[:, 0, :, :pair],
            w_qkv[:, 1, :, :pair],
            w_qkv[:, 2, :, :pair],
            w_qkv[:, 0, :, pair:],
            w_qkv[:, 1, :, pair:],
            w_qkv[:, 2, :, pair:],
            jnp.zeros((layers, model, HDIM), low),
        ],
        axis=-1,
    )
    w_mix = jnp.pad(w_out, ((0, 0), (0, HDIM), (0, 0)))
    router = jnp.concatenate([w_router, const_proj], axis=-1)
    router = jnp.pad(router, ((0, 0), (0, 0), (0, 128 - router.shape[-1])))
    top = lax.reduce_precision(router, 8, 7)
    middle = lax.reduce_precision(router - top, 8, 7)
    router_low = jnp.concatenate([top, middle, router - top - middle], axis=-1).astype(low)
    router_back = jnp.swapaxes(router, 1, 2)
    relative = jnp.where(routes < experts_n, routes ^ lax.axis_index("expert"), routes)
    routes_row = jnp.swapaxes(relative, 2, 3)
    gains = norm_gains.reshape(layers, 2, 1, model)

    def fwd_layer(m, l, stream, h, previous):
        hs = gather_pack(h)
        keep, far, send, saved, mixed, logsum = run_kernel(
            functools.partial(attn_fwd_kernel, tensor_n),
            [
                shape_of((rows_n, model), low),
                shape_of((rows_n, model), low),
                shape_of((2 * rows_n, model), low),
                shape_of((seq, 768), low),
                shape_of((seq, 256), low),
                shape_of((seq, 128), full),
            ],
            [*hs, w_cat[l], w_mix[l], cos[m], sin[m], bias[m]],
            "attn_fwd",
            24,
            flops=2 * seq * model * 1024 + 12 * seq * seq * 128,
        )
        mid, h_moe, logits, aux, pick, *bufs = run_kernel(
            functools.partial(mid_kernel, experts_n, routes_n),
            [
                shape_of((rows_n, model), full),
                shape_of((rows_n, model), low),
                shape_of((rows_n, 128), full),
                shape_of((rows_n, 128), full),
                shape_of((experts_n * capacity, 2 * rows_n), low),
            ]
            + [shape_of((capacity, model), low)] * experts_n,
            [
                *sum_pack(keep, far, send),
                stream,
                gains[l, 1],
                router_low[l],
                routes[l, m],
                routes_row[l, m],
                previous,
            ],
            "mid",
            16,
            flops=4 * rows_n * model * 384,
        )
        held = send_rows(bufs)
        keep, send = run_kernel(
            functools.partial(expert_fwd_kernel, len(held)),
            [shape_of((expert_rows, model), low)] * 2,
            [*held, w_gate_up[l, 0], w_down[l, 0]],
            "expert_fwd",
            24,
            flops=2 * 2 * expert_rows * model * 3 * hidden_n,
        )
        arrivals = return_rows(keep, send, capacity)
        last = l == layers - 1
        common = [
            *arrivals, pick, aux, routes[l, m], h_moe, mid, const_vec[l],
        ]
        if last:
            (out,) = run_kernel(
                functools.partial(combine_kernel, experts_n, len(arrivals), True),
                [shape_of((rows_n, model), low)],
                common,
                "combine_last",
                16,
                flops=4 * rows_n * model * 256,
            )
            h_next = None
        else:
            out, h_next = run_kernel(
                functools.partial(combine_kernel, experts_n, len(arrivals), False),
                [shape_of((rows_n, model), full), shape_of((rows_n, model), low)],
                [*common, gains[l + 1, 0]],
                "combine",
                16,
                flops=4 * rows_n * model * 256,
            )
        kept = dict(
            hs=hs, saved=saved, mixed=mixed, logsum=logsum, mid=mid, h_moe=h_moe, aux=aux,
            pick=pick, held=held, arrivals=arrivals, stream=stream,
        )
        return out, h_next, logits, kept

    def route_outs():
        return [
            shape_of((rows_n, 128), full),
            shape_of((rows_n, model), full),
            shape_of((32, model), full),
        ] + [shape_of((capacity, model), low)] * experts_n

    def bwd_moe(m, l, kept, dstream, dlocal, bufs):
        grads = send_rows(bufs)
        keep, send, hidden, dgu = run_kernel(
            functools.partial(expert_bwd_kernel, len(grads)),
            [shape_of((expert_rows, model), low)] * 2
            + [
                shape_of((2 * expert_rows, hidden_n), low),
                shape_of((2 * expert_rows, 2 * hidden_n), low),
            ],
            [*kept["held"], *grads, w_gate_up[l, 0], w_down[l, 0]],
            "expert_bwd",
            32,
            flops=2 * 2 * expert_rows * model * 5 * hidden_n,
        )
        arrivals = return_rows(keep, send, capacity)
        dmid, dattn, dgain = run_kernel(
            functools.partial(expert_norm_back_kernel, len(arrivals)),
            [
                shape_of((rows_n, model), full),
                shape_of((rows_n, model), low),
                shape_of((8, model), full),
            ],
            [*arrivals, kept["pick"], dlocal, kept["mid"], gains[l, 1], dstream],
            "expert_norm_back",
            16,
            flops=4 * rows_n * model * 128,
        )
        return dmid, dattn, dgain, [*kept["held"], *grads, hidden, dgu]

    def bwd_attn(m, l, kept, dattn):
        ds = gather_pack(dattn)
        keep, far, send, dqkv = run_kernel(
            functools.partial(attn_bwd_kernel, tensor_n),
            [
                shape_of((rows_n, model), low),
                shape_of((rows_n, model), low),
                shape_of((2 * rows_n, model), low),
                shape_of((seq, 640), low),
            ],
            [
                *ds, w_cat[l], w_mix[l], cos[m], sin[m], bias[m], kept["saved"], kept["logsum"],
            ],
            "attn_bwd",
            32,
            flops=2 * seq * model * 1024 + 30 * seq * seq * 128,
            scratch=[
                pltpu.VMEM((seq, seq), low),
                pltpu.VMEM((seq, seq), low),
                pltpu.VMEM((seq, 256), full),
            ],
        )
        parts = sum_pack(keep, far, send)
        return parts, [*kept["hs"], *ds, dqkv, kept["mixed"]]

    micro = range(micro_n)
    streams = [tokens[m] for m in micro]
    hs = [
        run_kernel(
            norm_kernel, [shape_of((rows_n, model), low)], [tokens[m], gains[0, 0]], "norm", 8
        )[0]
        for m in micro
    ]
    zero_logits = jnp.zeros((rows_n, 128), full)
    logits = [zero_logits for _ in micro]
    kept = [[None] * layers for _ in micro]
    for l in range(layers):
        for m in micro:
            streams[m], hs[m], logits[m], kept[m][l] = fwd_layer(
                m, l, streams[m], hs[m], logits[m]
            )
    outputs = jnp.stack(streams)

    dstream = [cotangent[m] for m in micro]
    dlogits = [None] * micro_n
    smalls = []
    attn_grads = [None] * layers
    expert_grads = [None] * layers
    parts = [None] * micro_n
    dmids = [None] * micro_n
    attn_gain = [None] * layers
    for l in reversed(range(layers)):
        weights_in = []
        small_here = []
        for m in micro:
            k = kept[m][l]
            tail = [k["pick"], k["aux"], routes[l, m], k["h_moe"], const_vec[l], router_back[l]]
            if l == layers - 1:
                dlogits[m], dlocal, small, *bufs = run_kernel(
                    functools.partial(
                        last_back_kernel, experts_n, routes_n, len(k["arrivals"])
                    ),
                    route_outs(),
                    [*k["arrivals"], cotangent[m], *tail],
                    "last_back",
                    24,
                    flops=8 * rows_n * model * 256,
                )
            else:
                dgain, dstream[m], dlogits[m], dlocal, small, *bufs = run_kernel(
                    functools.partial(
                        next_back_kernel, experts_n, routes_n, len(k["arrivals"])
                    ),
                    [shape_of((8, model), full), shape_of((rows_n, model), full)]
                    + route_outs(),
                    [
                        *k["arrivals"],
                        *parts[m],
                        kept[m][l + 1]["stream"],
                        gains[l + 1, 0],
                        dmids[m],
                        *tail,
                        dlogits[m],
                    ],
                    "next_back",
                    24,
                    flops=8 * rows_n * model * 256,
                )
                attn_gain[l + 1] = dgain if m == 0 else attn_gain[l + 1] + dgain
            dmids[m], dattn, dgain, for_weights = bwd_moe(m, l, k, dstream[m], dlocal, bufs)
            weights_in.append((for_weights, dattn))
            small_here.append((small, dgain))
        (expert_grads[l],) = run_kernel(
            functools.partial(expert_weights_kernel, len(kept[0][l]["held"]), micro_n),
            [shape_of((model, 3 * hidden_n), low)],
            [x for for_weights, _ in weights_in for x in for_weights],
            "expert_weights",
            32,
            flops=2 * 2 * expert_rows * micro_n * model * 3 * hidden_n,
        )
        smalls.append(
            (
                sum(s for s, _ in small_here),
                sum(g for _, g in small_here),
            )
        )
        attn_in = []
        for m in micro:
            parts[m], more = bwd_attn(m, l, kept[m][l], weights_in[m][1])
            attn_in += more
        (attn_grads[l],) = run_kernel(
            functools.partial(attn_weights_kernel, tensor_n, micro_n),
            [shape_of((model, 768), low)],
            attn_in,
            "attn_weights",
            32,
            flops=2 * seq * micro_n * model * 768,
        )
    smalls = smalls[::-1]
    grad_inputs = []
    for m in micro:
        dgain, out = run_kernel(
            input_back_kernel,
            [shape_of((8, model), full), shape_of((rows_n, model), full)],
            [*parts[m], tokens[m], gains[0, 0], dmids[m]],
            "input_back",
            16,
        )
        attn_gain[0] = dgain if m == 0 else attn_gain[0] + dgain
        grad_inputs.append(out)

    small = [
        sum_all(jnp.concatenate([s[: routes_n + 4], s[24:26], g[0:1]], axis=0))
        for s, g in smalls
    ]
    gain_sums = [sum_all(g[0:1]) for g in attn_gain]
    grad_qkv = []
    grad_out = []
    grad_gate_up = []
    grad_down = []
    for l in range(layers):
        g = expert_grads[l].reshape(dp_n, model // dp_n, 3 * hidden_n)
        total = sum_owner(g, "dp")
        grad_gate_up.append(
            jnp.stack([total[:, :hidden_n], total[:, hidden_n : 2 * hidden_n]])[None]
        )
        grad_down.append(total[:, 2 * hidden_n :].T[None])
        g = attn_grads[l].reshape(dp_n, experts_n, model // (dp_n * experts_n), 768)
        g = sum_owner(jnp.swapaxes(g, 0, 1), "expert").astype(low)
        total = sum_owner(g, "dp")
        grad_qkv.append(
            jnp.stack(
                [
                    jnp.concatenate([total[:, 0:128], total[:, 384:448]], axis=1),
                    jnp.concatenate([total[:, 128:256], total[:, 448:512]], axis=1),
                    jnp.concatenate([total[:, 256:384], total[:, 512:576]], axis=1),
                ]
            )
        )
        grad_out.append(jnp.concatenate([total[:, 640:768], total[:, 576:640]], axis=1).T)
    small = jnp.stack(small)
    return (
        outputs,
        jnp.stack(grad_inputs),
        jnp.concatenate(gain_sums, axis=0),
        small[:, routes_n + 6],
        jnp.stack(grad_qkv),
        jnp.stack(grad_out),
        jnp.stack(grad_gate_up),
        jnp.stack(grad_down),
        jnp.swapaxes(small[:, :routes_n], 1, 2),
        jnp.swapaxes(small[:, routes_n : routes_n + 4], 1, 2),
        small[:, routes_n + 4 : routes_n + 6],
    )


def solution(mesh):
    return jax.shard_map(
        local,
        mesh=mesh,
        in_specs=(
            P(None, ("dp", "expert", "tensor"), None),
            P(None, ("dp", "expert", "tensor"), None),
            P(None, ("dp", "expert"), None),
            P(None, ("dp", "expert"), None),
            P(None, None, ("dp", "expert", "tensor"), None),
            P(),
            P(None, None, None, "tensor"),
            P(None, "tensor", None),
            P(None, "expert", None, None, "tensor"),
            P(None, "expert", "tensor", None),
            P(),
            P(),
            P(),
        ),
        out_specs=(
            P(None, ("dp", "expert", "tensor"), None),
            P(None, ("dp", "expert", "tensor"), None),
            P(),
            P(),
            P(None, None, ("dp", "expert"), "tensor"),
            P(None, "tensor", ("dp", "expert")),
            P(None, "expert", None, "dp", "tensor"),
            P(None, "expert", "tensor", "dp"),
            P(),
            P(),
            P(),
        ),
        check_vma=False,
    )
```

```python
import functools
import math

import jax
import jax.numpy as jnp
from jax import lax
from jax.experimental import pallas as pl
from jax.experimental.pallas import tpu as pltpu
from jax.sharding import PartitionSpec as P

HDIM = 64
epsilon = 1e-06
masked_value = -1e30
highest = lax.Precision.HIGHEST
low = jnp.bfloat16
full = jnp.float32
MIB = 1 << 20


def shape_of(shape, dtype):
    return jax.ShapeDtypeStruct(shape, dtype)


def run_kernel(body, outs, ins, name, limit, flops=0, scratch=(), scalars=0, after=()):
    ins = list(ins)
    taken = len(ins)
    in_bytes = sum(a.size * a.dtype.itemsize for a in ins)
    out_bytes = sum(math.prod(o.shape) * jnp.dtype(o.dtype).itemsize for o in outs)
    vmem = pl.BlockSpec(memory_space=pltpu.VMEM)
    smem = pl.BlockSpec(memory_space=pltpu.SMEM)
    skip = len(after)

    def kernel(*refs):
        body(*refs[:taken], *refs[taken + skip :])

    return pl.pallas_call(
        kernel,
        out_shape=tuple(outs),
        in_specs=[smem] * scalars
        + [vmem] * (taken - scalars)
        + [pl.BlockSpec(memory_space=pl.ANY)] * skip,
        out_specs=tuple([vmem] * len(outs)),
        scratch_shapes=list(scratch),
        compiler_params=pltpu.CompilerParams(vmem_limit_bytes=limit * MIB),
        cost_estimate=pl.CostEstimate(
            flops=0, bytes_accessed=0, transcendentals=0
        ),
        name=name,
    )(*ins, *after)


def dot(a, b):
    return jnp.dot(a, b, preferred_element_type=full)


def dot_nt(a, b):
    return lax.dot_general(a, b, (((1,), (1,)), ((), ())), preferred_element_type=full)


def dot_tn(a, b):
    return lax.dot_general(a, b, (((0,), (0,)), ((), ())), preferred_element_type=full)


def lanes(rows, width=128):
    return lax.broadcasted_iota(jnp.int32, (rows, width), 1)


def sublanes(rows, width=128):
    return lax.broadcasted_iota(jnp.int32, (rows, width), 0)


def join(parts):
    if parts[0].shape[0] % 16:
        return jnp.concatenate([p.astype(full) for p in parts], axis=0).astype(low)
    return jnp.concatenate(parts, axis=0)


def stack_rows(refs, start=0, count=None):
    if count is None or count == refs[0].shape[0]:
        return join([r[...] for r in refs])
    if count % 16 or start % 16:
        return join([r[...].astype(full)[start : start + count].astype(low) for r in refs])
    return join([r[start : start + count, :] for r in refs])


def rms_scale(rows):
    return lax.rsqrt(jnp.mean(rows * rows, axis=-1, keepdims=True) + epsilon)


def split2(rows):
    top = rows.astype(low)
    return top, (rows - top.astype(full)).astype(low)


def as_column(row):
    n = row.shape[1]
    return jnp.sum(jnp.where(sublanes(n, n) == lanes(n, n), row, 0.0), axis=1, keepdims=True)


def norm_kernel(m, tokens, gains, out):
    rows = tokens[m].astype(full)
    out[...] = (rows * rms_scale(rows) * gains[0, 0:1, :]).astype(low)


def tables_kernel(tensor_n, place, lengths, order, w_router, const_proj, tokens, gains, cos, sin, bias, router_low,
                  router_back, normed):
    norm_kernel(1, tokens, gains, normed)
    micro_n, _, seq = order.shape
    rows_n = seq // tensor_n
    segments = lengths.shape[2]
    mine = place[0]
    half = HDIM // 2
    lane = lanes(rows_n)
    frequency = jnp.exp((lane % half).astype(full) * (-math.log(10000.0) / half))
    sign = jnp.where(lane % HDIM < half, -1.0, 1.0)
    for m in range(micro_n):
        row = order[m].astype(full)
        cuts = [row[:, j * rows_n : (j + 1) * rows_n] for j in range(tensor_n)]
        blocks = []
        for j in range(tensor_n):
            block = jnp.zeros((1, rows_n), full)
            for i in range(tensor_n):
                block = jnp.where((mine ^ j) == i, cuts[i], block)
            blocks.append(block)
        across = jnp.concatenate(blocks, axis=1)
        starts = []
        total = lengths[m, 0, 0]
        for s in range(1, segments):
            starts.append(total.astype(full))
            total = total + lengths[m, 0, s]
        for j in range(tensor_n):
            part = slice(j * rows_n, (j + 1) * rows_n)
            down = as_column(blocks[j])
            begin = jnp.zeros_like(down)
            for start in starts:
                begin = jnp.where(down >= start, start, begin)
            angle = (down - begin) * frequency
            cos[m, part, :] = jnp.cos(angle)
            sin[m, part, :] = jnp.sin(angle) * sign
            bias[m, part, :] = jnp.where(
                (begin <= across) & (across <= down), 0.0, masked_value
            ).astype(low)
    routes_n, layers, model = w_router.shape
    proj_n = const_proj.shape[1]
    for l in range(layers):
        both = jnp.concatenate(
            [w_router[r, l : l + 1, :] for r in range(routes_n)]
            + [const_proj[l], jnp.zeros((128 - routes_n - proj_n, model), full)],
            axis=0,
        )
        top = both.astype(low)
        rest = both - top.astype(full)
        middle = rest.astype(low)
        router_low[l, 0:128, :] = top
        router_low[l, 128:256, :] = middle
        router_low[l, 256:384, :] = (rest - middle.astype(full)).astype(low)
        router_back[l] = both


def swap_halves(rows):
    lane = lanes(rows.shape[0])
    half = HDIM // 2
    return jnp.where(
        lane % HDIM < half, pltpu.roll(rows, 128 - half, 1), pltpu.roll(rows, half, 1)
    )


def half_masks():
    lane = lanes(1)
    return (lane < HDIM).astype(full).astype(low), (lane >= HDIM).astype(full).astype(low)


def attn_fwd_kernel(l, m, blocks, *refs):
    heads = refs[:blocks]
    w, wo, cos, sin, bias, keep, far, send, saved, mixed, logsum = refs[blocks:]
    rows_n = keep.shape[0]
    pair = 2 * HDIM
    h = stack_rows(heads)
    c = cos[m]
    s = sin[m]
    lane = lanes(h.shape[0])

    def turn(chunk):
        return chunk * c + swap_halves(chunk) * s

    q = dot_nt(h, w[l, 0])
    k = dot_nt(h, w[l, 1])
    v = dot_nt(h, w[l, 2])
    saved[:, 0:128] = (turn(q[:, 0:pair]) * 0.125).astype(low)
    saved[:, 128:256] = turn(k[:, 0:pair]).astype(low)
    saved[:, 256:384] = v[:, 0:pair].astype(low)
    third = turn(jnp.concatenate([q[:, pair:], k[:, pair:]], axis=1))
    saved[:, 384:512] = jnp.where(lane < HDIM, third * 0.125, 0.0).astype(low)
    saved[:, 512:640] = jnp.where(lane < HDIM, pltpu.roll(third, HDIM, 1), 0.0).astype(low)
    saved[:, 640:768] = jnp.concatenate(
        [v[:, pair:], jnp.zeros((h.shape[0], HDIM), full)], axis=1
    ).astype(low)
    first, second = half_masks()
    lane = lanes(rows_n)
    for i in range(blocks):
        part = slice(i * rows_n, (i + 1) * rows_n)
        shift = bias[m, part, :].astype(full)
        q01 = saved[part, 0:128]
        q2 = saved[part, 384:512]
        results = []
        sums = []
        for query, keys, values in (
            (q01 * first, slice(128, 256), slice(256, 384)),
            (q01 * second, slice(128, 256), slice(256, 384)),
            (q2, slice(512, 640), slice(640, 768)),
        ):
            scores = dot_nt(query, saved[:, keys]) + shift
            peak = jnp.max(scores, axis=-1, keepdims=True)
            exponent = jnp.exp(scores - peak)
            total = jnp.sum(exponent, axis=-1, keepdims=True)
            probs = (exponent * (1.0 / total)).astype(low)
            results.append(dot(probs, saved[:, values]))
            sums.append(peak + jnp.log(total))
        logsum[part, :] = jnp.where(lane == 0, sums[0], jnp.where(lane == 1, sums[1], sums[2]))
        mixed[part, 0:pair] = jnp.where(lane < HDIM, results[0], results[1]).astype(low)
        mixed[part, pair : pair + HDIM] = results[2][:, 0:HDIM].astype(low)
        value = dot(mixed[part, :], wo[l]).astype(low)
        if i == 0:
            keep[...] = value
        elif i == 2:
            far[...] = value
        else:
            at = (i // 2) * rows_n
            send[at : at + rows_n, :] = value


def attn_bwd_kernel(l, m, blocks, *refs):
    grads = refs[:blocks]
    (w, wo, cos, sin, bias, saved, logsum, keep, far, send, dqkv, probs_s, dscore_s, dq_s) = refs[
        blocks:
    ]
    rows_n = keep.shape[0]
    pair = 2 * HDIM
    c = cos[m]
    s = sin[m]
    dattn = stack_rows(grads)
    dmix = dot_nt(dattn, wo[l]).astype(low)
    seq = dmix.shape[0]
    d01 = dmix[:, 0:pair]
    d2 = jnp.concatenate([dmix[:, pair:], jnp.zeros((seq, HDIM), low)], axis=1)
    first, second = half_masks()
    q01 = saved[:, 0:128]
    k01 = saved[:, 128:256]
    v01 = saved[:, 256:384]
    q2 = saved[:, 384:512]
    k2 = saved[:, 512:640]
    v2 = saved[:, 640:768]
    heads = (
        (q01 * first, k01 * first, v01, d01 * first),
        (q01 * second, k01 * second, v01, d01 * second),
        (q2, k2, v2, d2),
    )
    dks = []
    dvs = []
    for n, (query, keys, values, dout) in enumerate(heads):
        for i in range(blocks):
            part = slice(i * rows_n, (i + 1) * rows_n)
            scores = dot_nt(query[part], keys) + bias[m, part, :].astype(full)
            probs = jnp.exp(scores - logsum[part, n : n + 1])
            dprobs = dot_nt(dout[part], values)
            inner = jnp.sum(probs * dprobs, axis=-1, keepdims=True)
            dscores = (probs * (dprobs - inner)).astype(low)
            probs_s[part, :] = probs.astype(low)
            dscore_s[part, :] = dscores
            dq = dot(dscores, keys)
            if n == 1:
                dq_s[part, 0:128] += dq
            else:
                at = 128 * (n // 2)
                dq_s[part, at : at + 128] = dq
        dks.append(dot_tn(dscore_s[...], query))
        dvs.append(dot_tn(probs_s[...], dout))

    def turn_back(chunk):
        return chunk * c - swap_halves(chunk) * s

    third = turn_back(dq_s[:, 128:256] * 0.125 + pltpu.roll(dks[2], HDIM, 1)).astype(low)
    dq = jnp.concatenate([turn_back(dq_s[:, 0:128] * 0.125).astype(low), third[:, :HDIM]], axis=1)
    dk = jnp.concatenate([turn_back(dks[0] + dks[1]).astype(low), third[:, HDIM:]], axis=1)
    dv = jnp.concatenate([dvs[0] + dvs[1], dvs[2][:, :HDIM]], axis=1).astype(low)
    dqkv[0] = dq
    dqkv[1] = dk
    dqkv[2] = dv
    dh = (dot(dq, w[l, 0]) + dot(dk, w[l, 1]) + dot(dv, w[l, 2])).astype(low)
    keep[...] = dh[0:rows_n]
    far[...] = dh[2 * rows_n : 3 * rows_n]
    send[0:rows_n, :] = dh[rows_n : 2 * rows_n]
    send[rows_n : 2 * rows_n, :] = dh[3 * rows_n : 4 * rows_n]


def attn_weights_kernel(blocks, micro, dp_n, experts_n, *refs):
    place = refs[0]
    total = (2 * blocks + 2) * micro
    outs = refs[1 + total : -1]
    out = refs[-1]
    refs = refs[1 : 1 + total]
    per = 2 * blocks + 2
    pair = 2 * HDIM
    groups = [refs[m * per : (m + 1) * per] for m in range(micro)]
    h = jnp.concatenate([stack_rows(g[:blocks]) for g in groups], axis=0)
    d = jnp.concatenate([stack_rows(g[blocks : 2 * blocks]) for g in groups], axis=0)
    third = []
    for i in range(3):
        part = dot_tn(h, jnp.concatenate([g[2 * blocks][i] for g in groups], axis=0))
        out[:, i * pair : (i + 1) * pair] = part[:, :pair].astype(low)
        third.append(part[:, pair:])
    part = dot_tn(d, jnp.concatenate([g[2 * blocks + 1][...] for g in groups], axis=0))
    out[:, 3 * pair : 4 * pair] = part[:, :pair].astype(low)
    third.append(part[:, pair:])
    out[:, 4 * pair : 5 * pair] = jnp.concatenate(third[0:2], axis=1).astype(low)
    out[:, 5 * pair : 6 * pair] = jnp.concatenate(third[2:4], axis=1).astype(low)
    share = out.shape[0] // (dp_n * experts_n)
    for ref, units in zip(outs, owner_units()):
        rows_n = ref.shape[0] // len(units)
        for i, (zr, er, part) in enumerate(units):
            owner = (place[2] ^ zr) * experts_n + (place[1] ^ er)
            at = pl.multiple_of(owner * share + part * rows_n, rows_n)
            ref[i * rows_n : (i + 1) * rows_n, :] = out[pl.ds(at, rows_n), :]


def owner_units():
    return (
        [(z, 0, 0) for z in (0, 2, 1, 3)],
        [(z, 1, 0) for z in (0, 2, 1, 3)],
        [(z, e, 1) for e in (0, 1) for z in (0, 2)],
        [(z, e, 1) for e in (0, 1) for z in (1, 3)],
    )


def halves_kernel(pairs, *refs):
    for n in range(pairs):
        one, two = refs[2 * n : 2 * n + 2]
        first, second = refs[2 * pairs + 2 * n : 2 * pairs + 2 * n + 2]
        rows_n = first.shape[0]
        first[...] = (one[0:rows_n, :].astype(full) + two[0:rows_n, :].astype(full)).astype(low)
        second[...] = (one[rows_n:, :].astype(full) + two[rows_n:, :].astype(full)).astype(low)


def weave_kernel(one, one_in, two, two_in, keep, send):
    rows_n = one.shape[0] // 2
    for n, (a, b) in enumerate(((one, one_in), (two, two_in))):
        at = slice(n * rows_n, (n + 1) * rows_n)
        keep[at, :] = (a[0:rows_n, :].astype(full) + b[0:rows_n, :].astype(full)).astype(low)
        send[at, :] = (a[rows_n:, :].astype(full) + b[rows_n:, :].astype(full)).astype(low)


def add_far_kernel(far, arrived, out):
    rows_n = far.shape[0]
    out[...] = (far[...].astype(full) + arrived[rows_n : 2 * rows_n, :].astype(full)).astype(low)


def add_back_kernel(keep, arrived, *outs):
    rows_n = outs[0].shape[0]
    for i, out in enumerate(outs):
        part = slice(i * rows_n, (i + 1) * rows_n)
        out[...] = (keep[part, :].astype(full) + arrived[part, :].astype(full)).astype(low)


def fill_bufs(bufs, earlier, parts, capacity):
    for k, buf in enumerate(bufs):
        pieces = []
        for f, part in enumerate(parts):
            if earlier:
                before = earlier[k][...].astype(full)
                pieces.append(before[f * capacity : (f + 1) * capacity])
            pieces.append(part[k * capacity : (k + 1) * capacity])
        buf[...] = jnp.concatenate(pieces, axis=0).astype(low)


def mid_kernel(l, m, experts_n, routes_n, capacity, last, earlier_n, *refs):
    place, keep, arrived, across, stream, gains, router, routes = refs[:8]
    at = 8
    if l:
        previous = refs[at]
        at += 1
    if last:
        cotangent = refs[at]
        at += 1
    earlier = refs[at : at + earlier_n]
    at += earlier_n
    mid, h_moe, logits_out, aux, pick, *bufs = refs[at:]
    rows_n = keep.shape[0]
    rows = stream[m] if l == 0 else stream[...]
    rows = (
        rows.astype(full)
        + keep[...].astype(full)
        + arrived[0:rows_n, :].astype(full)
        + across[...].astype(full)
    )
    mid[...] = rows
    h = (rows * rms_scale(rows) * gains[l, 1:2, :]).astype(low)
    h_moe[...] = h
    parts = dot_nt(h, router[l])
    raw = parts[:, 0:128] + parts[:, 128:256] + parts[:, 256:384]
    lane = lanes(rows_n)
    logits = raw + previous[...] if l else raw
    logits_out[...] = jnp.where(lane < routes_n, logits, 0.0)
    columns = [as_column(routes[l, m, k : k + 1, :].astype(full)) for k in range(2)]
    picked = [
        jnp.sum(jnp.where(lane.astype(full) == column, logits, 0.0), axis=-1, keepdims=True)
        for column in columns
    ]
    peak = jnp.maximum(picked[0], picked[1])
    gate = [jnp.exp(p - peak) for p in picked]
    both = gate[0] + gate[1]
    gates = [gate[0] / both, gate[1] / both]
    numbers = list(gates)
    for j in range(2):
        two = [raw[:, routes_n + 2 * j + i : routes_n + 2 * j + i + 1] for i in range(2)]
        peak = jnp.maximum(two[0], two[1])
        power = [jnp.exp(p - peak) for p in two]
        both = power[0] + power[1]
        numbers += [power[0] / both, power[1] / both]
    numbers += columns
    value = jnp.zeros((rows_n, 128), full)
    for i, number in enumerate(numbers):
        value = jnp.where(lane == i, number, value)
    aux[...] = value
    here = place[1]
    along = []
    for k in range(2):
        route = routes[l, m, k : k + 1, :]
        along.append(jnp.where(route < experts_n, route ^ here, route).astype(full))
    index_rows = max(16, experts_n)
    expert = sublanes(index_rows, rows_n).astype(full)
    member = ((along[0] == expert) | (along[1] == expert)).astype(full).astype(low)
    before = (sublanes(rows_n, rows_n) < lanes(rows_n, rows_n)).astype(full).astype(low)
    rank = dot(member, before)
    slot = sublanes(capacity, rows_n).astype(full)
    picks = [
        jnp.concatenate(
            [
                ((slot == rank[k : k + 1, :]) & (route == k)).astype(full)
                for k in range(experts_n)
            ],
            axis=0,
        )
        for route in along
    ]
    pick[:, 0:rows_n] = picks[0].astype(low)
    pick[:, rows_n : 2 * rows_n] = picks[1].astype(low)
    sent = [dot((picks[0] + picks[1]).astype(low), h)]
    if last:
        dstream = cotangent[m].astype(full)
        sent.append(
            dot(picks[0].astype(low), (gates[0] * dstream).astype(low))
            + dot(picks[1].astype(low), (gates[1] * dstream).astype(low))
        )
    fill_bufs(bufs, earlier, sent, capacity)


def route_columns(aux):
    return [aux[:, 6 + k : 7 + k] for k in range(2)]


def route_values(experts_n, pick, values_low, aux, columns, h, vec):
    rows_n = h.shape[0]
    twice = jnp.concatenate([pick[...], pick[...]], axis=0)
    both = dot_tn(twice, values_low)
    values = []
    for k in range(2):
        route = columns[k]
        scale = (route == experts_n + 1).astype(full)
        value = both[k * rows_n : (k + 1) * rows_n]
        for j in range(2):
            here = (route == experts_n + 2 + j).astype(full)
            scale = scale + here * aux[:, 2 + 2 * j : 3 + 2 * j]
            value = value + (here * aux[:, 3 + 2 * j : 4 + 2 * j]) * vec[j : j + 1, :]
        values.append(value + scale * h)
    return values


def combine_kernel(l, m, experts_n, capacity, arrivals_n, *refs):
    arrivals = refs[:arrivals_n]
    pick, aux, h_moe, mid, vec, gains, stream, h_next = refs[arrivals_n:]
    columns = route_columns(aux)
    values = route_values(
        experts_n, pick, stack_rows(arrivals, m * capacity, capacity), aux, columns,
        h_moe[...].astype(full), vec[l],
    )
    rows = mid[...] + aux[:, 0:1] * values[0] + aux[:, 1:2] * values[1]
    stream[...] = rows
    h_next[...] = (rows * rms_scale(rows) * gains[l + 1, 0:1, :]).astype(low)


def route_back(
    l, experts_n, routes_n, dstream, values, pick, aux, columns, h_low, vec, router_back, dnext,
    small,
):
    lane = lanes(dstream.shape[0])
    h = h_low.astype(full)
    gates = [aux[:, k : k + 1] for k in range(2)]
    dgate = [jnp.sum(dstream * v, axis=-1, keepdims=True) for v in values]
    mean = gates[0] * dgate[0] + gates[1] * dgate[1]
    dlogits = dnext
    for k in range(2):
        dlogits = dlogits + jnp.where(lane.astype(full) == columns[k], gates[k] * (dgate[k] - mean), 0.0)

    def gate_of(route):
        return sum((columns[k] == route).astype(full) * gates[k] for k in range(2))

    along_h = jnp.sum(dstream * h, axis=-1, keepdims=True)
    scale = gate_of(experts_n + 1)
    both = dlogits
    for j in range(2):
        share = gate_of(experts_n + 2 + j)
        mix = [aux[:, 2 + 2 * j + i : 3 + 2 * j + i] for i in range(2)]
        along_v = jnp.sum(dstream * vec[l, j : j + 1, :], axis=-1, keepdims=True)
        dm = [share * along_h, share * along_v]
        inner = mix[0] * dm[0] + mix[1] * dm[1]
        for i in range(2):
            both = jnp.where(lane == routes_n + 2 * j + i, mix[i] * (dm[i] - inner), both)
        scale = scale + mix[0] * share
        small[24 + j : 25 + j, :] = jnp.sum((mix[1] * share) * dstream, axis=0, keepdims=True)
    dlocal = scale * dstream + jnp.dot(
        both, router_back[l], precision=highest, preferred_element_type=full
    )
    top, rest = split2(both)
    small[0:24, :] = (dot_tn(top, h_low) + dot_tn(rest, h_low))[0:24]
    return dlogits, dlocal


def norm_back(dh, rows, gain):
    scale = rms_scale(rows)
    unit = rows * scale
    dn = dh * gain
    drows = scale * (dn - unit * jnp.mean(dn * unit, axis=-1, keepdims=True))
    return drows, jnp.sum(dh * unit, axis=0, keepdims=True)


def turn_kernel(l, m, experts_n, routes_n, capacity, arrivals_n, earlier_n, *refs):
    arrivals = refs[:arrivals_n]
    pick, aux, h_moe, mid, vec, gains, router_back, cotangent = refs[
        arrivals_n : arrivals_n + 8
    ]
    at = arrivals_n + 8
    earlier = refs[at : at + earlier_n]
    out, dmid, dattn, dlogits_out, small = refs[at + earlier_n :]
    micro = len(earlier) + 1
    columns = route_columns(aux)
    h_low = h_moe[...]
    values = route_values(
        experts_n, pick, stack_rows(arrivals, m * capacity, capacity), aux, columns,
        h_low.astype(full), vec[l],
    )
    rows = mid[...]
    for i, ref in enumerate(earlier):
        out[i] = ref[i]
    out[m] = (rows + aux[:, 0:1] * values[0] + aux[:, 1:2] * values[1]).astype(low)
    for i in range(m + 1, out.shape[0]):
        out[i] = jnp.zeros(out.shape[1:], low)
    small[24:32, :] = jnp.zeros((8, small.shape[1]), full)
    dstream = cotangent[m].astype(full)
    dlogits, dlocal = route_back(
        l, experts_n, routes_n, dstream, values, pick, aux, columns, h_low, vec, router_back,
        jnp.zeros((dstream.shape[0], 128), full), small,
    )
    dlogits_out[...] = dlogits
    rows_n = rows.shape[0]
    both = pick[:, 0:rows_n] + pick[:, rows_n : 2 * rows_n]
    twice = jnp.concatenate([both, both], axis=0)
    at = (cotangent.shape[0] + m) * capacity
    dh = dlocal + dot_tn(twice, stack_rows(arrivals, at, capacity))
    drows, dgain = norm_back(dh, rows, gains[l, 1:2, :])
    small[26:27, :] = dgain
    value = dstream + drows
    dmid[...] = value
    dattn[...] = value.astype(low)


def next_back_kernel(l, m, experts_n, routes_n, capacity, arrivals_n, earlier_n, *refs):
    arrivals = refs[:arrivals_n]
    (keep, arrived, across, stream, gains, dmid, pick, aux, h_moe, vec, router_back,
     dnext) = refs[arrivals_n : arrivals_n + 12]
    at = arrivals_n + 12
    earlier = refs[at : at + earlier_n]
    dstream_out, dlogits_out, dlocal_out, small, *bufs = refs[at + earlier_n :]
    rows_n = keep.shape[0]
    dh = keep[...].astype(full) + arrived[0:rows_n, :].astype(full) + across[...].astype(full)
    drows, dgain = norm_back(dh, stream[...], gains[l + 1, 0:1, :])
    dstream = dmid[...] + drows
    dstream_out[...] = dstream
    small[24:32, :] = jnp.zeros((8, small.shape[1]), full)
    small[27:28, :] = dgain
    columns = route_columns(aux)
    h_low = h_moe[...]
    values = route_values(
        experts_n, pick, stack_rows(arrivals, m * capacity, capacity), aux, columns,
        h_low.astype(full), vec[l],
    )
    gates = [aux[:, k : k + 1] for k in range(2)]
    sent = dot(pick[:, 0:rows_n], (gates[0] * dstream).astype(low)) + dot(
        pick[:, rows_n : 2 * rows_n], (gates[1] * dstream).astype(low)
    )
    fill_bufs(bufs, earlier, [sent], capacity)
    dlogits, dlocal = route_back(
        l, experts_n, routes_n, dstream, values, pick, aux, columns, h_low, vec, router_back,
        dnext[...], small,
    )
    dlogits_out[...] = dlogits
    dlocal_out[...] = dlocal


def expert_norm_back_kernel(l, m, capacity, arrivals_n, *refs):
    arrivals = refs[:arrivals_n]
    pick, dlocal, mid, gains, dstream, dmid, dattn, dgain_out = refs[arrivals_n:]
    rows_n = mid.shape[0]
    both = pick[:, 0:rows_n] + pick[:, rows_n : 2 * rows_n]
    twice = jnp.concatenate([both, both], axis=0)
    dh = dlocal[...] + dot_tn(twice, stack_rows(arrivals, m * capacity, capacity))
    drows, dgain = norm_back(dh, mid[...], gains[l, 1:2, :])
    dgain_out[...] = jnp.broadcast_to(dgain, dgain_out.shape)
    value = dstream[...] + drows
    dmid[...] = value
    dattn[...] = value.astype(low)


def input_back_kernel(micro, *refs):
    tokens, gains = refs[4 * micro : 4 * micro + 2]
    out, dgain_out = refs[4 * micro + 2 :]
    total = None
    for m in range(micro):
        keep, arrived, across, dmid = refs[4 * m : 4 * m + 4]
        rows_n = keep.shape[0]
        dh = keep[...].astype(full) + arrived[0:rows_n, :].astype(full) + across[...].astype(full)
        drows, dgain = norm_back(dh, tokens[m].astype(full), gains[0, 0:1, :])
        out[m] = dmid[...] + drows
        total = dgain if m == 0 else total + dgain
    dgain_out[...] = jnp.broadcast_to(total, dgain_out.shape)


def expert_fwd_kernel(l, blocks_n, *refs):
    gate_up, down, keep, send = refs[blocks_n:]
    rows = stack_rows(refs[:blocks_n])
    g = dot(rows, gate_up[l, 0, 0])
    u = dot(rows, gate_up[l, 0, 1])
    hidden = (g * jax.nn.sigmoid(g) * u).astype(low)
    value = dot(hidden, down[l, 0]).astype(low)
    half = keep.shape[0]
    keep[...] = value[0:half]
    send[...] = value[half:]


def expert_back(l, rows, grads, gate_up, down):
    g = dot(rows, gate_up[l, 0, 0])
    u = dot(rows, gate_up[l, 0, 1])
    dhidden = dot_nt(grads, down[l, 0])
    s = jax.nn.sigmoid(g)
    silu = g * s
    hidden = (silu * u).astype(low)
    dg = (dhidden * u * s * (1.0 + g * (1.0 - s))).astype(low)
    du = (dhidden * silu).astype(low)
    drows = (dot_nt(dg, gate_up[l, 0, 0]) + dot_nt(du, gate_up[l, 0, 1])).astype(low)
    return hidden, dg, du, drows


def expert_both_kernel(l, blocks_n, *refs):
    blocks = refs[:blocks_n]
    gate_up, down, keep, send, hidden_out, dgu_out = refs[blocks_n:]
    each = blocks[0].shape[0] // 2
    rows = stack_rows(blocks, 0, each)
    grads = stack_rows(blocks, each, each)
    hidden, dg, du, drows = expert_back(l, rows, grads, gate_up, down)
    hidden_out[...] = hidden
    width = dg.shape[1]
    dgu_out[:, 0:width] = dg
    dgu_out[:, width : 2 * width] = du
    value = dot(hidden, down[l, 0]).astype(low)
    for i in range(blocks_n):
        out = keep if i < blocks_n // 2 else send
        at = 2 * each * (i % (blocks_n // 2))
        out[at : at + each, :] = value[i * each : (i + 1) * each]
        out[at + each : at + 2 * each, :] = drows[i * each : (i + 1) * each]


def expert_bwd_kernel(l, blocks_n, *refs):
    gate_up, down, keep, send, hidden_out, dgu_out = refs[2 * blocks_n :]
    rows = stack_rows(refs[:blocks_n])
    grads = stack_rows(refs[blocks_n : 2 * blocks_n])
    hidden, dg, du, drows = expert_back(l, rows, grads, gate_up, down)
    hidden_out[...] = hidden
    width = dg.shape[1]
    dgu_out[:, 0:width] = dg
    dgu_out[:, width : 2 * width] = du
    half = keep.shape[0]
    keep[...] = drows[0:half]
    send[...] = drows[half:]


def turned(n):
    order = [0]
    bit = n // 2
    while bit:
        order = order + [k + bit for k in order]
        bit //= 2
    bits = n.bit_length() - 1
    return [int(format(i, "b").zfill(bits)[::-1], 2) for i in range(n)]


def expert_weights_kernel(blocks_n, apart, pieces, *refs):
    place = refs[0]
    refs = refs[1:]
    if apart:
        rows = stack_rows(refs[:blocks_n])
        grads = stack_rows(refs[blocks_n : 2 * blocks_n])
    else:
        each = refs[0].shape[0] // 2
        rows = stack_rows(refs[:blocks_n], 0, each)
        grads = stack_rows(refs[:blocks_n], each, each)
    hidden, dgu, *outs, total = refs[-5:]
    width = dgu.shape[1]
    total[:, 0:width] = dot_tn(rows, dgu[...]).astype(low)
    total[:, width : width + hidden.shape[1]] = dot_tn(grads, hidden[...]).astype(low)
    share = total.shape[0] // pieces
    order = turned(pieces)
    for i, k in enumerate(order):
        at = pl.multiple_of((place[2] ^ k) * share, share)
        out = outs[2 * i // pieces]
        i = i % (pieces // 2)
        out[i * share : (i + 1) * share, :] = total[pl.ds(at, share), :]


def expert_total_kernel(layers, parts, *refs):
    gate_up, down = refs[layers * parts :]
    width = gate_up.shape[4]
    for l in range(layers):
        mine = refs[l * parts : (l + 1) * parts]
        for i in range(3):
            part = slice(i * width, (i + 1) * width)
            total = mine[0][:, part].astype(full)
            for ref in mine[1:]:
                total = total + ref[:, part].astype(full)
            if i < 2:
                gate_up[l, 0, i] = total
            else:
                down[l, 0] = total


def attn_total_kernel(layers, parts, *refs):
    qkv, out = refs[layers * parts :]
    pair = 2 * HDIM
    for l in range(layers):
        mine = refs[l * parts : (l + 1) * parts]
        total = mine[0][...].astype(full)
        for ref in mine[1:]:
            total = total + ref[...].astype(full)
        third = total[:, 4 * pair :]
        for i in range(3):
            qkv[l, i, :, 0:pair] = total[:, i * pair : (i + 1) * pair]
            qkv[l, i, :, pair : pair + HDIM] = third[:, i * HDIM : (i + 1) * HDIM]
        out[l, 0:pair, :] = total[:, 3 * pair : 4 * pair].T
        out[l, pair : pair + HDIM, :] = third[:, 3 * HDIM :].T


def swap(x, axis, k):
    n = lax.axis_size(axis)
    return lax.ppermute(x, axis, [(i, i ^ k) for i in range(n)])


def swap_pair(x, k, j):
    experts_n = lax.axis_size("expert")
    tensor_n = lax.axis_size("tensor")
    if j == 0:
        return swap(x, "expert", k)
    if k == 0:
        return swap(x, "tensor", j)
    table = [
        (e * tensor_n + t, (e ^ k) * tensor_n + (t ^ j))
        for e in range(experts_n)
        for t in range(tensor_n)
    ]
    return lax.ppermute(x, ("expert", "tensor"), table)


def gather_pack(block):
    near = swap(block, "tensor", 1)
    far = swap(block, "tensor", 2)
    return [block, near, far, swap(far, "tensor", 1)]


def sum_pack(keep, far, send):
    arrived = swap(send, "tensor", 1)
    (total,) = run_kernel(
        add_far_kernel, [shape_of(far.shape, low)], [far, arrived], "add_far", 8
    )
    return keep, arrived, swap(total, "tensor", 2)


def send_rows(bufs):
    experts_n = len(bufs)
    held = []
    for j in (0, 2):
        for k in range(experts_n):
            held.append(bufs[k] if (j, k) == (0, 0) else swap_pair(bufs[k], k, j))
    return held + [swap(x, "tensor", 1) for x in held]


def return_rows(keep, send, each):
    experts_n = lax.axis_size("expert")
    arrived = swap(send, "tensor", 1)
    sums = run_kernel(
        add_back_kernel,
        [shape_of((each, keep.shape[1]), low)] * (2 * experts_n),
        [keep, arrived],
        "add_back",
        8,
    )
    out = []
    for j in (0, 2):
        for k in range(experts_n):
            part = sums[(j // 2) * experts_n + k]
            out.append(part if (j, k) == (0, 0) else swap_pair(part, k, j))
    return out


def small_pack_kernel(layers, micro, routes_n, *refs):
    smalls = [refs[l * micro : (l + 1) * micro] for l in range(layers)]
    at = layers * micro
    gains = [refs[at + l * micro : at + (l + 1) * micro] for l in range(layers - 1)]
    first_gain, out = refs[-2:]
    pieces = []
    last_gain = first_gain[0:1, :]
    for l in range(layers):
        total = smalls[l][0][...]
        for ref in smalls[l][1:]:
            total = total + ref[...]
        if l < layers - 1:
            moe = gains[l][0][0:1, :]
            for ref in gains[l][1:]:
                moe = moe + ref[0:1, :]
        else:
            moe = total[26:27]
        pieces += [total[0 : routes_n + 4], total[24:26], moe, last_gain]
        last_gain = total[27:28]
    rows = sum(p.shape[0] for p in pieces)
    if out.shape[0] > rows:
        pieces.append(jnp.zeros((out.shape[0] - rows, out.shape[1]), full))
    out[...] = jnp.concatenate(pieces, axis=0)


def sum_kernel(*refs):
    total = refs[0][...]
    for ref in refs[1:-1]:
        total = total + ref[...]
    refs[-1][...] = total


def small_out_kernel(layers, routes_n, parts, *refs):
    attn_gains, moe_gains, router, proj, vec = refs[parts:]
    total = refs[0][...]
    for ref in refs[1:parts]:
        total = total + ref[...]
    each = routes_n + 8
    for l in range(layers):
        mine = total[l * each : (l + 1) * each]
        for r in range(routes_n):
            router[r, l : l + 1, :] = mine[r : r + 1]
        proj[l] = mine[routes_n : routes_n + 4]
        vec[l] = mine[routes_n + 4 : routes_n + 6]
        moe_gains[l : l + 1, :] = mine[routes_n + 6 : routes_n + 7]
        attn_gains[l : l + 1, :] = mine[routes_n + 7 : routes_n + 8]


def sum_rows(parts):
    (out,) = run_kernel(sum_kernel, [shape_of(parts[0].shape, parts[0].dtype)], parts, "sum", 8)
    return out


def sum_all(rows):
    rows = sum_rows([rows, swap(rows, "tensor", 1)])
    parts = [rows]
    for j in (0, 2):
        for k in range(lax.axis_size("expert")):
            if (j, k) != (0, 0):
                parts.append(swap_pair(rows, k, j))
    rows = sum_rows(parts)
    return [rows] + [swap(rows, "dp", k) for k in range(1, lax.axis_size("dp"))]


def pieces_of(grad, axis):
    n = lax.axis_size(axis)
    here = lax.axis_index(axis)

    def piece(k):
        return lax.dynamic_index_in_dim(grad, here ^ k, 0, keepdims=False)

    return [piece(0)] + [swap(piece(k), axis, k) for k in range(1, n)]


def local(
    tokens,
    cotangent,
    row_order,
    lengths,
    routes,
    norm_gains,
    w_qkv,
    w_out,
    w_gate_up,
    w_down,
    w_router,
    const_proj,
    const_vec,
):
    layers = w_qkv.shape[0]
    micro_n, rows_n, model = tokens.shape
    routes_n = w_router.shape[2]
    experts_n = lax.axis_size("expert")
    tensor_n = lax.axis_size("tensor")
    dp_n = lax.axis_size("dp")
    capacity = 9 * rows_n // (4 * (experts_n + 4))
    heads_width = w_qkv.shape[3]
    hidden_n = w_down.shape[2]
    seq = tensor_n * rows_n
    each = micro_n * capacity
    half_rows = 2 * experts_n * each
    blocks_n = 4 * experts_n
    arrivals_n = 2 * experts_n
    micro = range(micro_n)
    expert_limit = 12 if half_rows <= 384 else 40
    assert tensor_n == 4 and heads_width == 3 * HDIM and rows_n == 128 and micro_n == 2

    w_qkv = jnp.swapaxes(w_qkv, 2, 3)
    routes = jnp.swapaxes(routes, 2, 3)
    hs = [None] * micro_n
    (hs[0],) = run_kernel(
        functools.partial(norm_kernel, 0),
        [shape_of((rows_n, model), low)],
        [tokens, norm_gains],
        "norm",
        8,
    )
    place = jnp.stack([lax.axis_index(a) for a in ("tensor", "expert", "dp")]).astype(jnp.int32)
    cos, sin, bias, router_low, router_back, hs[1] = run_kernel(
        functools.partial(tables_kernel, tensor_n),
        [
            shape_of((micro_n, seq, 128), full),
            shape_of((micro_n, seq, 128), full),
            shape_of((micro_n, seq, seq), low),
            shape_of((layers, 384, model), low),
            shape_of((layers, 128, model), full),
            shape_of((rows_n, model), low),
        ],
        [
            place, lengths, row_order, jnp.transpose(w_router, (2, 0, 1)),
            jnp.swapaxes(const_proj, 1, 2), tokens, norm_gains,
        ],
        "tables",
        12,
        scalars=2,
    )

    def attn_fwd(m, l, h):
        heads = gather_pack(h)
        keep, far, send, saved, mixed, logsum = run_kernel(
            functools.partial(attn_fwd_kernel, l, m, tensor_n),
            [
                shape_of((rows_n, model), low),
                shape_of((rows_n, model), low),
                shape_of((2 * rows_n, model), low),
                shape_of((seq, 768), low),
                shape_of((seq, heads_width), low),
                shape_of((seq, 128), full),
            ],
            [*heads, w_qkv, w_out, cos, sin, bias],
            "attn_fwd",
            12,
            flops=2 * seq * model * 1024 + 12 * seq * seq * 128,
        )
        return sum_pack(keep, far, send), dict(
            heads=heads, saved=saved, mixed=mixed, logsum=logsum
        )

    def attn_bwd(m, l, kept, dattn, after):
        grads = gather_pack(dattn)
        keep, far, send, dqkv = run_kernel(
            functools.partial(attn_bwd_kernel, l, m, tensor_n),
            [
                shape_of((rows_n, model), low),
                shape_of((rows_n, model), low),
                shape_of((2 * rows_n, model), low),
                shape_of((3, seq, heads_width), low),
            ],
            [*grads, w_qkv, w_out, cos, sin, bias, kept["saved"], kept["logsum"]],
            "attn_bwd",
            12,
            flops=2 * seq * model * 1024 + 30 * seq * seq * 128,
            scratch=[
                pltpu.VMEM((seq, seq), low),
                pltpu.VMEM((seq, seq), low),
                pltpu.VMEM((seq, 256), full),
            ],
            after=after,
        )
        return sum_pack(keep, far, send), [*kept["heads"], *grads, dqkv, kept["mixed"]]

    share = model // (dp_n * experts_n)

    woven = dp_n == 4 and experts_n == 2 and share % 32 == 0

    def attn_weights(ins, after):
        outs = [shape_of((model, model), low)]
        if woven:
            outs = [shape_of((4 * share // 2, model), low)] * 4
        return run_kernel(
            functools.partial(attn_weights_kernel, tensor_n, micro_n, dp_n, experts_n),
            outs,
            [place, *ins],
            "attn_weights",
            12,
            flops=2 * seq * micro_n * model * model,
            scratch=[pltpu.VMEM((model, model), low)] if woven else [],
            scalars=1,
            after=after,
        )

    def attn_sums(parts):
        if not woven:
            grad = parts[0].reshape(dp_n, experts_n, share, model)
            mine = pieces_of(jnp.swapaxes(grad, 0, 1), "expert")
            total = sum(x.astype(full) for x in mine).astype(low)
            return pieces_of(total, "dp"), []
        one, one_out, two, two_out = parts
        one_in = swap(one_out, "expert", 1)
        two_in = swap(two_out, "dp", 1)
        one, one_out, two, two_out = halves([(one, one_in), (two, two_in)])
        first = two
        one_in = swap(one_out, "dp", 1)
        two_in = swap(two_out, "expert", 1)
        keep, send = run_kernel(
            weave_kernel,
            [shape_of((share, model), low)] * 2,
            [one, one_in, two, two_in],
            "weave",
            8,
        )
        return [keep, swap(send, "dp", 2)], [first, keep]

    def expert_weights(blocks, hidden, dgu, apart):
        return run_kernel(
            functools.partial(expert_weights_kernel, blocks_n, apart, dp_n),
            [shape_of((model // 2, 3 * hidden_n), low)] * 2,
            [place, *blocks, hidden, dgu],
            "expert_weights",
            expert_limit,
            flops=2 * 2 * half_rows * model * 3 * hidden_n,
            scratch=[pltpu.VMEM((model, 3 * hidden_n), low)],
            scalars=1,
        )

    def halves(pairs):
        rows_n = pairs[0][0].shape[0] // 2
        return run_kernel(
            functools.partial(halves_kernel, len(pairs)),
            [shape_of((rows_n, x.shape[1]), low) for x, _ in pairs for _ in range(2)],
            [x for pair in pairs for x in pair],
            "halves",
            12,
        )

    def expert_sums(parts):
        keep, send = parts
        stages = []
        bit = 1
        while True:
            came = swap(send, "dp", bit)
            bit *= 2
            if bit == dp_n:
                return [keep, came], stages
            keep, send = halves([(keep, came)])
            stages.append(send)

    expert_outs = [
        shape_of((2 * half_rows, hidden_n), low),
        shape_of((2 * half_rows, 2 * hidden_n), low),
    ]

    stream = [tokens] * micro_n
    logits = [None] * micro_n
    kept = [[None] * layers for _ in micro]
    for l in range(layers):
        last = l == layers - 1
        kinds = 2 if last else 1
        bufs = []
        for m in micro:
            parts, k = attn_fwd(m, l, hs[m])
            mid, h_moe, logits[m], aux, pick, *bufs = run_kernel(
                functools.partial(
                    mid_kernel, l, m, experts_n, routes_n, capacity, last, len(bufs)
                ),
                [
                    shape_of((rows_n, model), full),
                    shape_of((rows_n, model), low),
                    shape_of((rows_n, 128), full),
                    shape_of((rows_n, 128), full),
                    shape_of((experts_n * capacity, 2 * rows_n), low),
                ]
                + [shape_of(((m + 1) * kinds * capacity, model), low)] * experts_n,
                [place, *parts, stream[m], norm_gains, router_low, routes]
                + ([logits[m]] if l else [])
                + ([cotangent] if last else [])
                + bufs,
                "mid",
                12,
                flops=4 * rows_n * model * 384,
                scalars=1,
            )
            kept[m][l] = dict(
                k, mid=mid, h_moe=h_moe, aux=aux, pick=pick, stream=stream[m],
            )
        held = send_rows(bufs)
        if last:
            keep, send, hidden, dgu = run_kernel(
                functools.partial(expert_both_kernel, l, blocks_n),
                [shape_of((kinds * half_rows, model), low)] * 2 + expert_outs,
                [*held, w_gate_up, w_down],
                "expert_both",
                expert_limit,
                flops=2 * 2 * half_rows * model * 6 * hidden_n,
            )
        else:
            keep, send = run_kernel(
                functools.partial(expert_fwd_kernel, l, blocks_n),
                [shape_of((half_rows, model), low)] * 2,
                [*held, w_gate_up, w_down],
                "expert_fwd",
                expert_limit,
                flops=2 * 2 * half_rows * model * 3 * hidden_n,
            )
        arrivals = return_rows(keep, send, kinds * each)
        for m in micro:
            kept[m][l]["held"] = held
            kept[m][l]["arrivals"] = arrivals
        if last:
            break
        for m in micro:
            k = kept[m][l]
            stream[m], hs[m] = run_kernel(
                functools.partial(combine_kernel, l, m, experts_n, capacity, arrivals_n),
                [shape_of((rows_n, model), full), shape_of((rows_n, model), low)],
                [
                    *arrivals, k["pick"], k["aux"], k["h_moe"], k["mid"], const_vec, norm_gains,
                ],
                "combine",
                12,
                flops=4 * rows_n * model * 256,
            )

    l = layers - 1
    expert_grads = [None] * layers
    expert_pieces = [None] * layers
    attn_pieces = [None] * layers
    smalls = [[None] * micro_n for _ in range(layers)]
    gains = [None] * (layers - 1)
    expert_grads[l] = expert_weights(held, hidden, dgu, False)
    expert_pieces[l], stages = expert_sums(expert_grads[l])
    outputs = []
    dmid = [None] * micro_n
    dattn = [None] * micro_n
    dlogits = [None] * micro_n
    for m in micro:
        k = kept[m][l]
        out, dmid[m], dattn[m], dlogits[m], smalls[l][m] = run_kernel(
            functools.partial(
                turn_kernel, l, m, experts_n, routes_n, capacity, arrivals_n, len(outputs)
            ),
            [
                shape_of((micro_n, rows_n, model), low),
                shape_of((rows_n, model), full),
                shape_of((rows_n, model), low),
                shape_of((rows_n, 128), full),
                shape_of((32, model), full),
            ],
            [
                *arrivals, k["pick"], k["aux"], k["h_moe"], k["mid"], const_vec, norm_gains,
                router_back, cotangent, *outputs,
            ],
            "turn",
            12,
            flops=12 * rows_n * model * 256,
            after=[expert_grads[l][0]],
        )
        outputs = [out]
    (outputs,) = outputs
    before_bwd = [[], stages]
    before_weights = []
    attn_in = None
    while True:
        parts = [None] * micro_n
        grads_in = []
        for m in micro:
            parts[m], more = attn_bwd(m, l, kept[m][l], dattn[m], before_bwd[m])
            grads_in += more
        attn_in = grads_in
        if l == 0:
            break
        l -= 1
        bufs = []
        dstream = [None] * micro_n
        dlocal = [None] * micro_n
        for m in micro:
            k = kept[m][l]
            dstream[m], dlogits[m], dlocal[m], smalls[l][m], *bufs = run_kernel(
                functools.partial(
                    next_back_kernel, l, m, experts_n, routes_n, capacity, arrivals_n, len(bufs)
                ),
                [
                    shape_of((rows_n, model), full),
                    shape_of((rows_n, 128), full),
                    shape_of((rows_n, model), full),
                    shape_of((32, model), full),
                ]
                + [shape_of(((m + 1) * capacity, model), low)] * experts_n,
                [
                    *k["arrivals"], *parts[m], kept[m][l + 1]["stream"], norm_gains, dmid[m],
                    k["pick"], k["aux"], k["h_moe"], const_vec, router_back, dlogits[m],
                    *bufs,
                ],
                "next_back",
                12,
                flops=12 * rows_n * model * 256,
            )
        held = kept[0][l]["held"]
        grads = send_rows(bufs)
        keep, send, hidden, dgu = run_kernel(
            functools.partial(expert_bwd_kernel, l, blocks_n),
            [shape_of((half_rows, model), low)] * 2 + expert_outs,
            [*held, *grads, w_gate_up, w_down],
            "expert_bwd",
            expert_limit,
            flops=2 * 2 * half_rows * model * 5 * hidden_n,
            after=expert_pieces[l + 1][1:],
        )
        arrivals = return_rows(keep, send, each)
        expert_grads[l] = expert_weights([*held, *grads], hidden, dgu, True)
        expert_pieces[l], stages = expert_sums(expert_grads[l])
        gains[l] = [None] * micro_n
        for m in micro:
            k = kept[m][l]
            dmid[m], dattn[m], dgain = run_kernel(
                functools.partial(expert_norm_back_kernel, l, m, capacity, arrivals_n),
                [
                    shape_of((rows_n, model), full),
                    shape_of((rows_n, model), low),
                    shape_of((8, model), full),
                ],
                [*arrivals, k["pick"], dlocal[m], k["mid"], norm_gains, dstream[m]],
                "expert_norm_back",
                12,
                flops=4 * rows_n * model * 128,
                after=[expert_grads[l][0]],
            )
            gains[l][m] = dgain
        grad = attn_weights(attn_in, [dattn[0]])
        attn_pieces[l + 1], more = attn_sums(grad)
        before_bwd = [[grad[0]], [*stages, *more[:1]]]
        before_weights = more[1:]

    grad = attn_weights(attn_in, before_weights)
    attn_pieces[0], _ = attn_sums(grad)
    grad_tokens, first_gain = run_kernel(
        functools.partial(input_back_kernel, micro_n),
        [shape_of((micro_n, rows_n, model), full), shape_of((8, model), full)],
        [x for m in micro for x in (*parts[m], dmid[m])] + [tokens, norm_gains],
        "input_back",
        12,
    )

    each_small = routes_n + 8
    (small,) = run_kernel(
        functools.partial(small_pack_kernel, layers, micro_n, routes_n),
        [shape_of((-(-layers * each_small // 8) * 8, model), full)],
        [x for xs in smalls + gains for x in xs] + [first_gain],
        "small_pack",
        8,
    )
    small = sum_all(small)
    attn_gains, moe_gains, grad_router, grad_proj, grad_vec = run_kernel(
        functools.partial(small_out_kernel, layers, routes_n, len(small)),
        [
            shape_of((layers, model), full),
            shape_of((layers, model), full),
            shape_of((routes_n, layers, model), full),
            shape_of((layers, 4, model), full),
            shape_of((layers, 2, model), full),
        ],
        small,
        "small_out",
        8,
    )
    grad_gate_up, grad_down = run_kernel(
        functools.partial(expert_total_kernel, layers, 2),
        [
            shape_of((layers, 1, 2, model // dp_n, hidden_n), full),
            shape_of((layers, 1, model // dp_n, hidden_n), full),
        ],
        [x for pieces in expert_pieces for x in pieces],
        "expert_total",
        12,
        after=[grad[0]],
    )
    grad_qkv, grad_out = run_kernel(
        functools.partial(attn_total_kernel, layers, len(attn_pieces[0])),
        [
            shape_of((layers, 3, share, heads_width), full),
            shape_of((layers, heads_width, share), full),
        ],
        [x for pieces in attn_pieces for x in pieces],
        "attn_total",
        12,
    )
    return (
        outputs,
        grad_tokens,
        attn_gains,
        moe_gains,
        grad_qkv,
        grad_out,
        grad_gate_up,
        jnp.swapaxes(grad_down, 2, 3),
        jnp.transpose(grad_router, (1, 2, 0)),
        jnp.swapaxes(grad_proj, 1, 2),
        grad_vec,
    )


def solution(mesh):
    return jax.shard_map(
        local,
        mesh=mesh,
        in_specs=(
            P(None, ("dp", "expert", "tensor"), None),
            P(None, ("dp", "expert", "tensor"), None),
            P(None, ("dp", "expert"), None),
            P(None, ("dp", "expert"), None),
            P(None, None, ("dp", "expert", "tensor"), None),
            P(),
            P(None, None, None, "tensor"),
            P(None, "tensor", None),
            P(None, "expert", None, None, "tensor"),
            P(None, "expert", "tensor", None),
            P(),
            P(),
            P(),
        ),
        out_specs=(
            P(None, ("dp", "expert", "tensor"), None),
            P(None, ("dp", "expert", "tensor"), None),
            P(),
            P(),
            P(None, None, ("dp", "expert"), "tensor"),
            P(None, "tensor", ("dp", "expert")),
            P(None, "expert", None, "dp", "tensor"),
            P(None, "expert", "tensor", "dp"),
            P(),
            P(),
            P(),
        ),
        check_vma=False,
    )
```

```python
import functools
import math

import jax
import jax.numpy as jnp
from jax import lax
from jax.experimental import pallas as pl
from jax.experimental.pallas import tpu as pltpu
from jax.sharding import PartitionSpec as P

HDIM = 64
epsilon = 1e-06
masked_value = -1e30
highest = lax.Precision.HIGHEST
low = jnp.bfloat16
full = jnp.float32
MIB = 1 << 20


FLOPS_PER_US = 1.1e9
MICROS = {"tables": 3.0}


def shape_of(shape, dtype):
    return jax.ShapeDtypeStruct(shape, dtype)


def run_kernel(body, outs, ins, name, limit, scratch=(), scalars=0, after=()):
    ins = list(ins)
    taken = len(ins)
    vmem = pl.BlockSpec(memory_space=pltpu.VMEM)
    smem = pl.BlockSpec(memory_space=pltpu.SMEM)
    skip = len(after)

    def kernel(*refs):
        body(*refs[:taken], *refs[taken + skip :])

    return pl.pallas_call(
        kernel,
        out_shape=tuple(outs),
        in_specs=[smem] * scalars
        + [vmem] * (taken - scalars)
        + [pl.BlockSpec(memory_space=pl.ANY)] * skip,
        out_specs=tuple([vmem] * len(outs)),
        scratch_shapes=list(scratch),
        compiler_params=pltpu.CompilerParams(vmem_limit_bytes=limit * MIB),
        cost_estimate=pl.CostEstimate(
            flops=int(MICROS.get(name, 0.0) * FLOPS_PER_US), bytes_accessed=0, transcendentals=0
        ),
        name=name,
    )(*ins, *after)


def dot(a, b):
    return jnp.dot(a, b, preferred_element_type=full)


def dot_nt(a, b):
    return lax.dot_general(a, b, (((1,), (1,)), ((), ())), preferred_element_type=full)


def dot_tn(a, b):
    return lax.dot_general(a, b, (((0,), (0,)), ((), ())), preferred_element_type=full)


def lanes(rows, width=128):
    return lax.broadcasted_iota(jnp.int32, (rows, width), 1)


def sublanes(rows, width=128):
    return lax.broadcasted_iota(jnp.int32, (rows, width), 0)


def join(parts):
    if parts[0].shape[0] % 16:
        return jnp.concatenate([p.astype(full) for p in parts], axis=0).astype(low)
    return jnp.concatenate(parts, axis=0)


def stack_rows(refs, start=0, count=None):
    if count is None or count == refs[0].shape[0]:
        return join([r[...] for r in refs])
    if count % 16 or start % 16:
        return join([r[...].astype(full)[start : start + count].astype(low) for r in refs])
    return join([r[start : start + count, :] for r in refs])


def rms_scale(rows):
    return lax.rsqrt(jnp.mean(rows * rows, axis=-1, keepdims=True) + epsilon)


def split2(rows):
    top = rows.astype(low)
    return top, (rows - top.astype(full)).astype(low)


def as_column(row):
    n = row.shape[1]
    return jnp.sum(jnp.where(sublanes(n, n) == lanes(n, n), row, 0.0), axis=1, keepdims=True)


def norm_kernel(m, tokens, gains, out):
    rows = tokens[m].astype(full)
    out[...] = (rows * rms_scale(rows) * gains[0, 0:1, :]).astype(low)


def tables_kernel(tensor_n, place, lengths, order, w_router, const_proj, tokens, gains, cos, sin, bias, router_low,
                  normed):
    norm_kernel(1, tokens, gains, normed)
    micro_n, _, seq = order.shape
    rows_n = seq // tensor_n
    segments = lengths.shape[2]
    mine = place[0]
    half = HDIM // 2
    lane = lanes(rows_n)
    frequency = jnp.exp((lane % half).astype(full) * (-math.log(10000.0) / half))
    sign = jnp.where(lane % HDIM < half, -1.0, 1.0)
    for m in range(micro_n):
        row = order[m].astype(full)
        cuts = [row[:, j * rows_n : (j + 1) * rows_n] for j in range(tensor_n)]
        blocks = []
        for j in range(tensor_n):
            block = jnp.zeros((1, rows_n), full)
            for i in range(tensor_n):
                block = jnp.where((mine ^ j) == i, cuts[i], block)
            blocks.append(block)
        across = jnp.concatenate(blocks, axis=1)
        starts = []
        total = lengths[m, 0, 0]
        for s in range(1, segments):
            starts.append(total.astype(full))
            total = total + lengths[m, 0, s]
        for j in range(tensor_n):
            part = slice(j * rows_n, (j + 1) * rows_n)
            down = as_column(blocks[j])
            begin = jnp.zeros_like(down)
            for start in starts:
                begin = jnp.where(down >= start, start, begin)
            angle = (down - begin) * frequency
            cos[m, part, :] = jnp.cos(angle)
            sin[m, part, :] = jnp.sin(angle) * sign
            bias[m, part, :] = jnp.where(
                (begin <= across) & (across <= down), 0.0, masked_value
            ).astype(low)
    routes_n, layers, model = w_router.shape
    proj_n = const_proj.shape[1]
    for l in range(layers):
        both = jnp.concatenate(
            [w_router[r, l : l + 1, :] for r in range(routes_n)]
            + [const_proj[l], jnp.zeros((128 - routes_n - proj_n, model), full)],
            axis=0,
        )
        top = both.astype(low)
        rest = both - top.astype(full)
        middle = rest.astype(low)
        router_low[l, 0:128, :] = top
        router_low[l, 128:256, :] = middle
        router_low[l, 256:384, :] = (rest - middle.astype(full)).astype(low)


def swap_halves(rows):
    lane = lanes(rows.shape[0])
    half = HDIM // 2
    return jnp.where(
        lane % HDIM < half, pltpu.roll(rows, 128 - half, 1), pltpu.roll(rows, half, 1)
    )


def half_masks():
    lane = lanes(1)
    return (lane < HDIM).astype(full).astype(low), (lane >= HDIM).astype(full).astype(low)


def attn_fwd_kernel(l, m, blocks, *refs):
    heads = refs[:blocks]
    w, wo, cos, sin, bias, keep, far, send, saved, mixed, logsum = refs[blocks:]
    pair = 2 * HDIM
    h = stack_rows(heads)
    c = cos[m]
    s = sin[m]
    lane = lanes(h.shape[0])

    def turn(chunk):
        return chunk * c + swap_halves(chunk) * s

    q = dot_nt(h, w[l, 0])
    k = dot_nt(h, w[l, 1])
    v = dot_nt(h, w[l, 2])
    saved[:, 0:128] = (turn(q[:, 0:pair]) * 0.125).astype(low)
    saved[:, 128:256] = turn(k[:, 0:pair]).astype(low)
    saved[:, 256:384] = v[:, 0:pair].astype(low)
    third = turn(jnp.concatenate([q[:, pair:], k[:, pair:]], axis=1))
    saved[:, 384:512] = jnp.where(lane < HDIM, third * 0.125, 0.0).astype(low)
    saved[:, 512:640] = jnp.where(lane < HDIM, pltpu.roll(third, HDIM, 1), 0.0).astype(low)
    saved[:, 640:768] = jnp.concatenate(
        [v[:, pair:], jnp.zeros((h.shape[0], HDIM), full)], axis=1
    ).astype(low)
    first, second = half_masks()
    shift = bias[m].astype(full)
    q01 = saved[:, 0:128]
    heads = (
        (q01 * first, slice(128, 256), slice(256, 384)),
        (q01 * second, slice(128, 256), slice(256, 384)),
        (saved[:, 384:512], slice(512, 640), slice(640, 768)),
    )
    scores = [dot_nt(query, saved[:, keys]) + shift for query, keys, _ in heads]
    peaks = [jnp.max(x, axis=-1, keepdims=True) for x in scores]
    powers = [jnp.exp(x - peak) for x, peak in zip(scores, peaks)]
    totals = [jnp.sum(x, axis=-1, keepdims=True) for x in powers]
    results = [
        dot((x * (1.0 / total)).astype(low), saved[:, values])
        for x, total, (_, _, values) in zip(powers, totals, heads)
    ]
    sums = [peak + jnp.log(total) for peak, total in zip(peaks, totals)]
    logsum[...] = jnp.where(lane == 0, sums[0], jnp.where(lane == 1, sums[1], sums[2]))
    mixed[:, 0:pair] = jnp.where(lane < HDIM, results[0], results[1]).astype(low)
    mixed[:, pair : pair + HDIM] = results[2][:, 0:HDIM].astype(low)
    spread(dot(mixed[...], wo[l]).astype(low), keep, far, send)


def spread(value, keep, far, send):
    rows_n = keep.shape[0]
    keep[...] = value[0:rows_n]
    far[...] = value[2 * rows_n : 3 * rows_n]
    send[0:rows_n, :] = value[rows_n : 2 * rows_n]
    send[rows_n : 2 * rows_n, :] = value[3 * rows_n : 4 * rows_n]


def attn_bwd_kernel(l, m, blocks, *refs):
    grads = refs[:blocks]
    w, wo, cos, sin, bias, saved, logsum, *more = refs[blocks:]
    if not l:
        *rows, gains, dgain = more[: blocks + 1] + more[-1:]
        more = more[blocks + 1 : -1]
    keep, far, send, dqkv = more
    pair = 2 * HDIM
    c = cos[m]
    s = sin[m]
    dattn = stack_rows(grads)
    dmix = dot_nt(dattn, wo[l]).astype(low)
    seq = dmix.shape[0]
    d01 = dmix[:, 0:pair]
    d2 = jnp.concatenate([dmix[:, pair:], jnp.zeros((seq, HDIM), low)], axis=1)
    first, second = half_masks()
    q01 = saved[:, 0:128]
    k01 = saved[:, 128:256]
    v01 = saved[:, 256:384]
    q2 = saved[:, 384:512]
    k2 = saved[:, 512:640]
    v2 = saved[:, 640:768]
    heads = (
        (q01 * first, k01 * first, v01, d01 * first),
        (q01 * second, k01 * second, v01, d01 * second),
        (q2, k2, v2, d2),
    )
    shift = bias[m].astype(full)
    dqs, dks, dvs = [], [], []
    for n, (query, keys, values, dout) in enumerate(heads):
        probs = jnp.exp(dot_nt(query, keys) + shift - logsum[:, n : n + 1])
        dprobs = dot_nt(dout, values)
        inner = jnp.sum(probs * dprobs, axis=-1, keepdims=True)
        dscores = (probs * (dprobs - inner)).astype(low)
        dqs.append(dot(dscores, keys))
        dks.append(dot_tn(dscores, query))
        dvs.append(dot_tn(probs.astype(low), dout))

    def turn_back(chunk):
        return chunk * c - swap_halves(chunk) * s

    third = turn_back(dqs[2] * 0.125 + pltpu.roll(dks[2], HDIM, 1)).astype(low)
    dq = jnp.concatenate([turn_back((dqs[0] + dqs[1]) * 0.125).astype(low), third[:, :HDIM]], axis=1)
    dk = jnp.concatenate([turn_back(dks[0] + dks[1]).astype(low), third[:, HDIM:]], axis=1)
    dv = jnp.concatenate([dvs[0] + dvs[1], dvs[2][:, :HDIM]], axis=1).astype(low)
    dqkv[0] = dq
    dqkv[1] = dk
    dqkv[2] = dv
    dh = dot(dq, w[l, 0]) + dot(dk, w[l, 1]) + dot(dv, w[l, 2])
    spread(dh.astype(low), keep, far, send)
    if not l:
        along = jnp.sum(dh * stack_rows(rows).astype(full), axis=0, keepdims=True)
        dgain[...] = jnp.broadcast_to(along / gains[l, 0:1, :], dgain.shape)


def attn_weights_kernel(blocks, micro, dp_n, experts_n, units, *refs):
    place = refs[0]
    total = (2 * blocks + 2) * micro
    outs = refs[1 + total : -1]
    out = refs[-1]
    refs = refs[1 : 1 + total]
    per = 2 * blocks + 2
    pair = 2 * HDIM
    groups = [refs[m * per : (m + 1) * per] for m in range(micro)]
    h = jnp.concatenate([stack_rows(g[:blocks]) for g in groups], axis=0)
    d = jnp.concatenate([stack_rows(g[blocks : 2 * blocks]) for g in groups], axis=0)
    third = []
    for i in range(3):
        part = dot_tn(h, jnp.concatenate([g[2 * blocks][i] for g in groups], axis=0))
        out[:, i * pair : (i + 1) * pair] = part[:, :pair].astype(low)
        third.append(part[:, pair:])
    part = dot_tn(d, jnp.concatenate([g[2 * blocks + 1][...] for g in groups], axis=0))
    out[:, 3 * pair : 4 * pair] = part[:, :pair].astype(low)
    third.append(part[:, pair:])
    out[:, 4 * pair : 5 * pair] = jnp.concatenate(third[0:2], axis=1).astype(low)
    out[:, 5 * pair : 6 * pair] = jnp.concatenate(third[2:4], axis=1).astype(low)
    share = out.shape[0] // (dp_n * experts_n)
    for ref, mine in zip(outs, units):
        rows_n = ref.shape[0] // len(mine)
        for i, (zr, er, part) in enumerate(mine):
            owner = (place[2] ^ zr) * experts_n + (place[1] ^ er)
            at = pl.multiple_of(owner * share + part * rows_n, rows_n)
            ref[i * rows_n : (i + 1) * rows_n, :] = out[pl.ds(at, rows_n), :]


WOVEN = (
    [(z, 0, 0) for z in (0, 2, 1, 3)],
    [(z, 1, 0) for z in (0, 2, 1, 3)],
    [(z, e, 1) for e in (0, 1) for z in (0, 2)],
    [(z, e, 1) for e in (0, 1) for z in (1, 3)],
)


def halves_kernel(pairs, *refs):
    outs = list(refs[2 * pairs :])
    for n in range(pairs):
        one, two = refs[2 * n : 2 * n + 2]
        at = 0
        while at < one.shape[0]:
            out = outs.pop(0)
            rows_n = out.shape[0]
            part = slice(at, at + rows_n)
            out[...] = (one[part, :].astype(full) + two[part, :].astype(full)).astype(low)
            at += rows_n


def weave_kernel(one, one_in, two, two_in, keep, send):
    rows_n = one.shape[0] // 2
    for n, (a, b) in enumerate(((one, one_in), (two, two_in))):
        at = slice(n * rows_n, (n + 1) * rows_n)
        keep[at, :] = (a[0:rows_n, :].astype(full) + b[0:rows_n, :].astype(full)).astype(low)
        send[at, :] = (a[rows_n:, :].astype(full) + b[rows_n:, :].astype(full)).astype(low)


def add_far_kernel(far, arrived, out):
    rows_n = far.shape[0]
    out[...] = (far[...].astype(full) + arrived[rows_n : 2 * rows_n, :].astype(full)).astype(low)


def add_back_kernel(keep, arrived, *outs):
    rows_n = outs[0].shape[0]
    for i, out in enumerate(outs):
        part = slice(i * rows_n, (i + 1) * rows_n)
        out[...] = (keep[part, :].astype(full) + arrived[part, :].astype(full)).astype(low)


def fill_bufs(bufs, earlier, parts, capacity):
    for k, buf in enumerate(bufs):
        pieces = []
        for f, part in enumerate(parts):
            if earlier:
                before = earlier[k][...].astype(full)
                pieces.append(before[f * capacity : (f + 1) * capacity])
            pieces.append(part[k * capacity : (k + 1) * capacity])
        buf[...] = jnp.concatenate(pieces, axis=0).astype(low)


def mid_kernel(l, m, experts_n, routes_n, capacity, last, earlier_n, *refs):
    place, keep, arrived, across, stream, gains, router, routes = refs[:8]
    at = 8
    if l:
        previous = refs[at]
        at += 1
    if last:
        cotangent = refs[at]
        at += 1
    earlier = refs[at : at + earlier_n]
    at += earlier_n
    mid, h_moe, logits_out, aux, pick, *bufs = refs[at:]
    rows_n = keep.shape[0]
    rows = stream[m] if l == 0 else stream[...]
    rows = (
        rows.astype(full)
        + keep[...].astype(full)
        + arrived[0:rows_n, :].astype(full)
        + across[...].astype(full)
    )
    mid[...] = rows
    h = (rows * rms_scale(rows) * gains[l, 1:2, :]).astype(low)
    h_moe[...] = h
    parts = dot_nt(h, router[l])
    raw = parts[:, 0:128] + parts[:, 128:256] + parts[:, 256:384]
    lane = lanes(rows_n)
    logits = raw + previous[...] if l else raw
    logits_out[...] = jnp.where(lane < routes_n, logits, 0.0)
    columns = [as_column(routes[l, m, k : k + 1, :].astype(full)) for k in range(2)]
    picked = [
        jnp.sum(jnp.where(lane.astype(full) == column, logits, 0.0), axis=-1, keepdims=True)
        for column in columns
    ]
    peak = jnp.maximum(picked[0], picked[1])
    gate = [jnp.exp(p - peak) for p in picked]
    both = gate[0] + gate[1]
    gates = [gate[0] / both, gate[1] / both]
    numbers = list(gates)
    for j in range(2):
        two = [raw[:, routes_n + 2 * j + i : routes_n + 2 * j + i + 1] for i in range(2)]
        peak = jnp.maximum(two[0], two[1])
        power = [jnp.exp(p - peak) for p in two]
        both = power[0] + power[1]
        numbers += [power[0] / both, power[1] / both]
    numbers += columns
    value = jnp.zeros((rows_n, 128), full)
    for i, number in enumerate(numbers):
        value = jnp.where(lane == i, number, value)
    aux[...] = value
    here = place[1]
    along = []
    for k in range(2):
        route = routes[l, m, k : k + 1, :]
        along.append(jnp.where(route < experts_n, route ^ here, route).astype(full))
    index_rows = max(16, experts_n)
    expert = sublanes(index_rows, rows_n).astype(full)
    member = ((along[0] == expert) | (along[1] == expert)).astype(full).astype(low)
    before = (sublanes(rows_n, rows_n) < lanes(rows_n, rows_n)).astype(full).astype(low)
    rank = dot(member, before)
    slot = sublanes(capacity, rows_n).astype(full)
    picks = [
        jnp.concatenate(
            [
                ((slot == rank[k : k + 1, :]) & (route == k)).astype(full)
                for k in range(experts_n)
            ],
            axis=0,
        )
        for route in along
    ]
    pick[:, 0:rows_n] = picks[0].astype(low)
    pick[:, rows_n : 2 * rows_n] = picks[1].astype(low)
    sent = [dot((picks[0] + picks[1]).astype(low), h)]
    if last:
        dstream = cotangent[m].astype(full)
        sent.append(
            dot(picks[0].astype(low), (gates[0] * dstream).astype(low))
            + dot(picks[1].astype(low), (gates[1] * dstream).astype(low))
        )
    fill_bufs(bufs, earlier, sent, capacity)


def route_columns(aux):
    return [aux[:, 6 + k : 7 + k] for k in range(2)]


def route_values(experts_n, pick, values_low, aux, columns, h, vec):
    rows_n = h.shape[0]
    twice = jnp.concatenate([pick[...], pick[...]], axis=0)
    both = dot_tn(twice, values_low)
    values = []
    for k in range(2):
        route = columns[k]
        scale = (route == experts_n + 1).astype(full)
        value = both[k * rows_n : (k + 1) * rows_n]
        for j in range(2):
            here = (route == experts_n + 2 + j).astype(full)
            scale = scale + here * aux[:, 2 + 2 * j : 3 + 2 * j]
            value = value + (here * aux[:, 3 + 2 * j : 4 + 2 * j]) * vec[j : j + 1, :]
        values.append(value + scale * h)
    return values


def combine_kernel(l, m, experts_n, capacity, arrivals_n, *refs):
    arrivals = refs[:arrivals_n]
    pick, aux, h_moe, mid, vec, gains, stream, h_next = refs[arrivals_n:]
    columns = route_columns(aux)
    values = route_values(
        experts_n, pick, stack_rows(arrivals, m * capacity, capacity), aux, columns,
        h_moe[...].astype(full), vec[l],
    )
    rows = mid[...] + aux[:, 0:1] * values[0] + aux[:, 1:2] * values[1]
    stream[...] = rows
    h_next[...] = (rows * rms_scale(rows) * gains[l + 1, 0:1, :]).astype(low)


def route_back(
    l, experts_n, routes_n, dstream, values, pick, aux, columns, h_low, vec, router, dnext,
    small,
):
    lane = lanes(dstream.shape[0])
    h = h_low.astype(full)
    gates = [aux[:, k : k + 1] for k in range(2)]
    dgate = [jnp.sum(dstream * v, axis=-1, keepdims=True) for v in values]
    mean = gates[0] * dgate[0] + gates[1] * dgate[1]
    dlogits = dnext
    for k in range(2):
        dlogits = dlogits + jnp.where(lane.astype(full) == columns[k], gates[k] * (dgate[k] - mean), 0.0)

    def gate_of(route):
        return sum((columns[k] == route).astype(full) * gates[k] for k in range(2))

    along_h = jnp.sum(dstream * h, axis=-1, keepdims=True)
    scale = gate_of(experts_n + 1)
    both = dlogits
    for j in range(2):
        share = gate_of(experts_n + 2 + j)
        mix = [aux[:, 2 + 2 * j + i : 3 + 2 * j + i] for i in range(2)]
        along_v = jnp.sum(dstream * vec[l, j : j + 1, :], axis=-1, keepdims=True)
        dm = [share * along_h, share * along_v]
        inner = mix[0] * dm[0] + mix[1] * dm[1]
        for i in range(2):
            both = jnp.where(lane == routes_n + 2 * j + i, mix[i] * (dm[i] - inner), both)
        scale = scale + mix[0] * share
        small[24 + j : 25 + j, :] = jnp.sum((mix[1] * share) * dstream, axis=0, keepdims=True)
    top, rest = split2(both)
    dlocal = scale * dstream + (
        dot(top, router[l, 0:128, :])
        + dot(top, router[l, 128:256, :])
        + dot(rest, router[l, 0:128, :])
    )
    small[0:24, :] = (dot_tn(top, h_low) + dot_tn(rest, h_low))[0:24]
    return dlogits, dlocal


def norm_back(dh, rows, gain):
    scale = rms_scale(rows)
    unit = rows * scale
    dn = dh * gain
    drows = scale * (dn - unit * jnp.mean(dn * unit, axis=-1, keepdims=True))
    return drows, jnp.sum(dh * unit, axis=0, keepdims=True)


def turn_kernel(l, m, experts_n, routes_n, capacity, arrivals_n, earlier_n, *refs):
    arrivals = refs[:arrivals_n]
    pick, aux, h_moe, mid, vec, gains, router, cotangent = refs[
        arrivals_n : arrivals_n + 8
    ]
    at = arrivals_n + 8
    earlier = refs[at : at + earlier_n]
    out, dmid, dattn, dlogits_out, small = refs[at + earlier_n :]
    micro = len(earlier) + 1
    columns = route_columns(aux)
    h_low = h_moe[...]
    values = route_values(
        experts_n, pick, stack_rows(arrivals, m * capacity, capacity), aux, columns,
        h_low.astype(full), vec[l],
    )
    rows = mid[...]
    for i, ref in enumerate(earlier):
        out[i] = ref[i]
    out[m] = (rows + aux[:, 0:1] * values[0] + aux[:, 1:2] * values[1]).astype(low)
    for i in range(m + 1, out.shape[0]):
        out[i] = jnp.zeros(out.shape[1:], low)
    small[24:32, :] = jnp.zeros((8, small.shape[1]), full)
    dstream = cotangent[m].astype(full)
    dlogits, dlocal = route_back(
        l, experts_n, routes_n, dstream, values, pick, aux, columns, h_low, vec, router,
        jnp.zeros((dstream.shape[0], 128), full), small,
    )
    dlogits_out[...] = dlogits
    rows_n = rows.shape[0]
    both = pick[:, 0:rows_n] + pick[:, rows_n : 2 * rows_n]
    twice = jnp.concatenate([both, both], axis=0)
    at = (cotangent.shape[0] + m) * capacity
    dh = dlocal + dot_tn(twice, stack_rows(arrivals, at, capacity))
    drows, dgain = norm_back(dh, rows, gains[l, 1:2, :])
    small[26:27, :] = dgain
    value = dstream + drows
    dmid[...] = value
    dattn[...] = value.astype(low)


def next_back_kernel(l, m, experts_n, routes_n, capacity, arrivals_n, earlier_n, *refs):
    arrivals = refs[:arrivals_n]
    (keep, arrived, across, stream, gains, dmid, pick, aux, h_moe, vec, router,
     dnext) = refs[arrivals_n : arrivals_n + 12]
    at = arrivals_n + 12
    earlier = refs[at : at + earlier_n]
    dstream_out, dlogits_out, dlocal_out, small, *bufs = refs[at + earlier_n :]
    rows_n = keep.shape[0]
    dh = keep[...].astype(full) + arrived[0:rows_n, :].astype(full) + across[...].astype(full)
    drows, dgain = norm_back(dh, stream[...], gains[l + 1, 0:1, :])
    dstream = dmid[...] + drows
    dstream_out[...] = dstream
    small[24:32, :] = jnp.zeros((8, small.shape[1]), full)
    small[27:28, :] = dgain
    columns = route_columns(aux)
    h_low = h_moe[...]
    values = route_values(
        experts_n, pick, stack_rows(arrivals, m * capacity, capacity), aux, columns,
        h_low.astype(full), vec[l],
    )
    gates = [aux[:, k : k + 1] for k in range(2)]
    sent = dot(pick[:, 0:rows_n], (gates[0] * dstream).astype(low)) + dot(
        pick[:, rows_n : 2 * rows_n], (gates[1] * dstream).astype(low)
    )
    fill_bufs(bufs, earlier, [sent], capacity)
    dlogits, dlocal = route_back(
        l, experts_n, routes_n, dstream, values, pick, aux, columns, h_low, vec, router,
        dnext[...], small,
    )
    dlogits_out[...] = dlogits
    dlocal_out[...] = dlocal


def expert_norm_back_kernel(l, m, capacity, arrivals_n, *refs):
    arrivals = refs[:arrivals_n]
    pick, dlocal, mid, gains, dstream, dmid, dattn, dgain_out = refs[arrivals_n:]
    rows_n = mid.shape[0]
    both = pick[:, 0:rows_n] + pick[:, rows_n : 2 * rows_n]
    twice = jnp.concatenate([both, both], axis=0)
    dh = dlocal[...] + dot_tn(twice, stack_rows(arrivals, m * capacity, capacity))
    drows, dgain = norm_back(dh, mid[...], gains[l, 1:2, :])
    dgain_out[...] = jnp.broadcast_to(dgain, dgain_out.shape)
    value = dstream[...] + drows
    dmid[...] = value
    dattn[...] = value.astype(low)


def input_back_kernel(micro, *refs):
    tokens, gains, out = refs[4 * micro :]
    for m in range(micro):
        keep, arrived, across, dmid = refs[4 * m : 4 * m + 4]
        rows_n = keep.shape[0]
        dh = keep[...].astype(full) + arrived[0:rows_n, :].astype(full) + across[...].astype(full)
        drows, _ = norm_back(dh, tokens[m].astype(full), gains[0, 0:1, :])
        out[m] = dmid[...] + drows


def expert_fwd_kernel(l, blocks_n, *refs):
    gate_up, down, keep, send = refs[blocks_n:]
    rows = stack_rows(refs[:blocks_n])
    g = dot(rows, gate_up[l, 0, 0])
    u = dot(rows, gate_up[l, 0, 1])
    hidden = (g * jax.nn.sigmoid(g) * u).astype(low)
    value = dot(hidden, down[l, 0]).astype(low)
    half = keep.shape[0]
    keep[...] = value[0:half]
    send[...] = value[half:]


def expert_back(l, rows, grads, gate_up, down):
    g = dot(rows, gate_up[l, 0, 0])
    u = dot(rows, gate_up[l, 0, 1])
    dhidden = dot_nt(grads, down[l, 0])
    s = jax.nn.sigmoid(g)
    silu = g * s
    hidden = (silu * u).astype(low)
    dg = (dhidden * u * s * (1.0 + g * (1.0 - s))).astype(low)
    du = (dhidden * silu).astype(low)
    drows = (dot_nt(dg, gate_up[l, 0, 0]) + dot_nt(du, gate_up[l, 0, 1])).astype(low)
    return hidden, dg, du, drows


def expert_both_kernel(l, blocks_n, *refs):
    blocks = refs[:blocks_n]
    gate_up, down, keep, send, hidden_out, dgu_out = refs[blocks_n:]
    each = blocks[0].shape[0] // 2
    rows = stack_rows(blocks, 0, each)
    grads = stack_rows(blocks, each, each)
    hidden, dg, du, drows = expert_back(l, rows, grads, gate_up, down)
    hidden_out[...] = hidden
    width = dg.shape[1]
    dgu_out[:, 0:width] = dg
    dgu_out[:, width : 2 * width] = du
    value = dot(hidden, down[l, 0]).astype(low)
    for i in range(blocks_n):
        out = keep if i < blocks_n // 2 else send
        at = 2 * each * (i % (blocks_n // 2))
        out[at : at + each, :] = value[i * each : (i + 1) * each]
        out[at + each : at + 2 * each, :] = drows[i * each : (i + 1) * each]


def expert_bwd_kernel(l, blocks_n, *refs):
    gate_up, down, keep, send, hidden_out, dgu_out = refs[2 * blocks_n :]
    rows = stack_rows(refs[:blocks_n])
    grads = stack_rows(refs[blocks_n : 2 * blocks_n])
    hidden, dg, du, drows = expert_back(l, rows, grads, gate_up, down)
    hidden_out[...] = hidden
    width = dg.shape[1]
    dgu_out[:, 0:width] = dg
    dgu_out[:, width : 2 * width] = du
    half = keep.shape[0]
    keep[...] = drows[0:half]
    send[...] = drows[half:]


def turned(n):
    order = [0]
    bit = n // 2
    while bit:
        order = order + [k + bit for k in order]
        bit //= 2
    bits = n.bit_length() - 1
    return [int(format(i, "b").zfill(bits)[::-1], 2) for i in range(n)]


def expert_weights_kernel(blocks_n, apart, pieces, packed, *refs):
    place = refs[0]
    refs = refs[1:]
    if packed:
        extra = (refs[-5][...].astype(full) + refs[-4][...].astype(full)).astype(low)
        refs = refs[:-5] + refs[-3:]
    if apart:
        rows = stack_rows(refs[:blocks_n])
        grads = stack_rows(refs[blocks_n : 2 * blocks_n])
    else:
        each = refs[0].shape[0] // 2
        rows = stack_rows(refs[:blocks_n], 0, each)
        grads = stack_rows(refs[:blocks_n], each, each)
    hidden, dgu, *outs, total = refs[-5:]
    width = dgu.shape[1]
    total[:, 0:width] = dot_tn(rows, dgu[...]).astype(low)
    total[:, width : width + hidden.shape[1]] = dot_tn(grads, hidden[...]).astype(low)
    share = total.shape[0] // pieces
    order = turned(pieces)
    for i, k in enumerate(order):
        at = pl.multiple_of((place[2] ^ k) * share, share)
        out = outs[2 * i // pieces]
        unit = out.shape[0] // (pieces // 2)
        to = (i % (pieces // 2)) * unit
        out[to : to + share, :] = total[pl.ds(at, share), :]
        if packed:
            more = unit - share
            width = extra.shape[1]
            for n in range(2):
                out[to + share : to + unit, n * width : (n + 1) * width] = extra[
                    (2 * i + n) * more : (2 * i + n + 1) * more
                ]


def expert_total_kernel(layers, *refs):
    gate_up, down, *packed = refs[2 * layers :]
    width, share = gate_up.shape[4], gate_up.shape[3]
    for l in range(layers):
        total = refs[2 * l][...].astype(full) + refs[2 * l + 1][...].astype(full)
        for i in range(2):
            gate_up[l, 0, i] = total[0:share, i * width : (i + 1) * width]
        down[l, 0] = total[0:share, 2 * width : 3 * width]
        if packed and l < layers - 1:
            half = packed[l].shape[1]
            packed[l][...] = jnp.concatenate(
                [total[share:, 0:half], total[share:, half : 2 * half]], axis=0
            )


def attn_total_kernel(layers, counts, *refs):
    qkv, out = refs[sum(counts) :]
    pair = 2 * HDIM
    for l in range(layers):
        mine = refs[sum(counts[:l]) : sum(counts[: l + 1])]
        total = mine[0][...].astype(full)
        for ref in mine[1:]:
            total = total + ref[...].astype(full)
        third = total[:, 4 * pair :]
        for i in range(3):
            qkv[l, i, :, 0:pair] = total[:, i * pair : (i + 1) * pair]
            qkv[l, i, :, pair : pair + HDIM] = third[:, i * HDIM : (i + 1) * HDIM]
        out[l, 0:pair, :] = total[:, 3 * pair : 4 * pair].T
        out[l, pair : pair + HDIM, :] = third[:, 3 * HDIM :].T


def swap(x, axis, k):
    n = lax.axis_size(axis)
    return lax.ppermute(x, axis, [(i, i ^ k) for i in range(n)])


def swap_pair(x, k, j):
    experts_n = lax.axis_size("expert")
    tensor_n = lax.axis_size("tensor")
    if j == 0:
        return swap(x, "expert", k)
    if k == 0:
        return swap(x, "tensor", j)
    table = [
        (e * tensor_n + t, (e ^ k) * tensor_n + (t ^ j))
        for e in range(experts_n)
        for t in range(tensor_n)
    ]
    return lax.ppermute(x, ("expert", "tensor"), table)


def attend(blocks, call):
    results = []
    for m, block in enumerate(blocks):
        near = swap(block, "tensor", 1)
        far = swap(block, "tensor", 2)
        pack = [block, near, far, swap(far, "tensor", 1)]
        (keep, away, send, *rest), extra = call(m, pack, [])
        arrived = swap(send, "tensor", 1)
        (total,) = run_kernel(
            add_far_kernel, [shape_of(away.shape, low)], [away, arrived], "add_far", 8
        )
        results.append(([keep, arrived, swap(total, "tensor", 2)], extra))
    return results


def send_rows(bufs):
    experts_n = len(bufs)
    far = [swap_pair(buf, k, 2) for k, buf in enumerate(bufs)]
    near = [bufs[0]] + [swap_pair(bufs[k], k, 0) for k in range(1, experts_n)]
    held = near + far
    return held + [swap(x, "tensor", 1) for x in held]


def return_rows(keep, send, each):
    experts_n = lax.axis_size("expert")
    arrived = swap(send, "tensor", 1)
    sums = run_kernel(
        add_back_kernel,
        [shape_of((each, keep.shape[1]), low)] * (2 * experts_n),
        [keep, arrived],
        "add_back",
        8,
    )
    far = [swap_pair(sums[experts_n + k], k, 2) for k in range(experts_n)]
    near = [sums[0]] + [swap_pair(sums[k], k, 0) for k in range(1, experts_n)]
    return near + far, sums[0]


def small_pack_kernel(layers, micro, routes_n, *refs):
    smalls = [refs[l * micro : (l + 1) * micro] for l in range(layers)]
    at = layers * micro
    gains = [refs[at + l * micro : at + (l + 1) * micro] for l in range(layers - 1)]
    *first_gains, out = refs[at + (layers - 1) * micro :]
    pieces = []
    last_gain = sum(ref[0:1, :] for ref in first_gains)
    for l in range(layers):
        total = smalls[l][0][...]
        for ref in smalls[l][1:]:
            total = total + ref[...]
        if l < layers - 1:
            moe = gains[l][0][0:1, :]
            for ref in gains[l][1:]:
                moe = moe + ref[0:1, :]
        else:
            moe = total[26:27]
        pieces += [total[0 : routes_n + 4], total[24:26], moe, last_gain]
        last_gain = total[27:28]
    rows = sum(p.shape[0] for p in pieces)
    if out.shape[0] > rows:
        pieces.append(jnp.zeros((out.shape[0] - rows, out.shape[1]), full))
    out[...] = jnp.concatenate(pieces, axis=0)


def sum_kernel(*refs):
    total = refs[0][...]
    for ref in refs[1:-1]:
        total = total + ref[...]
    refs[-1][...] = total


def small_out_kernel(layers, routes_n, parts, *refs):
    attn_gains, moe_gains, router, proj, vec = refs[parts:]
    total = refs[0][...]
    for ref in refs[1:parts]:
        total = total + ref[...]
    each = routes_n + 8
    for l in range(layers):
        mine = total[l * each : (l + 1) * each]
        for r in range(routes_n):
            router[r, l : l + 1, :] = mine[r : r + 1]
        proj[l] = mine[routes_n : routes_n + 4]
        vec[l] = mine[routes_n + 4 : routes_n + 6]
        moe_gains[l : l + 1, :] = mine[routes_n + 6 : routes_n + 7]
        attn_gains[l : l + 1, :] = mine[routes_n + 7 : routes_n + 8]


def sum_rows(parts):
    (out,) = run_kernel(sum_kernel, [shape_of(parts[0].shape, parts[0].dtype)], parts, "sum", 8)
    return out


def sum_all(rows):
    rows = sum_rows([rows, swap(rows, "tensor", 1)])
    parts = [rows]
    for j in (0, 2):
        for k in range(lax.axis_size("expert")):
            if (j, k) != (0, 0):
                parts.append(swap_pair(rows, k, j))
    rows = sum_rows(parts)
    return [rows] + [swap(rows, "dp", k) for k in range(1, lax.axis_size("dp"))]


def pieces_of(grad, axis):
    n = lax.axis_size(axis)
    here = lax.axis_index(axis)

    def piece(k):
        return lax.dynamic_index_in_dim(grad, here ^ k, 0, keepdims=False)

    return [piece(0)] + [swap(piece(k), axis, k) for k in range(1, n)]


def local(
    tokens,
    cotangent,
    row_order,
    lengths,
    routes,
    norm_gains,
    w_qkv,
    w_out,
    w_gate_up,
    w_down,
    w_router,
    const_proj,
    const_vec,
):
    layers = w_qkv.shape[0]
    micro_n, rows_n, model = tokens.shape
    routes_n = w_router.shape[2]
    experts_n = lax.axis_size("expert")
    tensor_n = lax.axis_size("tensor")
    dp_n = lax.axis_size("dp")
    capacity = 9 * rows_n // (4 * (experts_n + 4))
    heads_width = w_qkv.shape[3]
    hidden_n = w_down.shape[2]
    seq = tensor_n * rows_n
    each = micro_n * capacity
    half_rows = 2 * experts_n * each
    blocks_n = 4 * experts_n
    arrivals_n = 2 * experts_n
    micro = range(micro_n)
    expert_limit = 12 if half_rows <= 384 else 40
    assert tensor_n == 4 and heads_width == 3 * HDIM and rows_n == 128 and micro_n == 2

    w_qkv = jnp.swapaxes(w_qkv, 2, 3)
    routes = jnp.swapaxes(routes, 2, 3)
    hs = [None] * micro_n
    (hs[0],) = run_kernel(
        functools.partial(norm_kernel, 0),
        [shape_of((rows_n, model), low)],
        [tokens, norm_gains],
        "norm",
        8,
    )
    place = jnp.stack([lax.axis_index(a) for a in ("tensor", "expert", "dp")]).astype(jnp.int32)
    cos, sin, bias, router_low, hs[1] = run_kernel(
        functools.partial(tables_kernel, tensor_n),
        [
            shape_of((micro_n, seq, 128), full),
            shape_of((micro_n, seq, 128), full),
            shape_of((micro_n, seq, seq), low),
            shape_of((layers, 384, model), low),
            shape_of((rows_n, model), low),
        ],
        [
            place, lengths, row_order, jnp.transpose(w_router, (2, 0, 1)),
            jnp.swapaxes(const_proj, 1, 2), tokens, norm_gains,
        ],
        "tables",
        12,
        scalars=2,
    )

    def attn_fwd(l, blocks):
        def call(m, heads, after):
            results = run_kernel(
                functools.partial(attn_fwd_kernel, l, m, tensor_n),
                [
                    shape_of((rows_n, model), low),
                    shape_of((rows_n, model), low),
                    shape_of((2 * rows_n, model), low),
                    shape_of((seq, 768), low),
                    shape_of((seq, heads_width), low),
                    shape_of((seq, 128), full),
                ],
                [*heads, w_qkv, w_out, cos, sin, bias],
                "attn_fwd",
                12,
                after=after,
            )
            saved, mixed, logsum = results[3:]
            return results, dict(heads=heads, saved=saved, mixed=mixed, logsum=logsum)

        return attend(blocks, call)

    first_gains = []

    def attn_bwd(l, blocks, kept, after):
        def call(m, grads, after_here):
            results = run_kernel(
                functools.partial(attn_bwd_kernel, l, m, tensor_n),
                [
                    shape_of((rows_n, model), low),
                    shape_of((rows_n, model), low),
                    shape_of((2 * rows_n, model), low),
                    shape_of((3, seq, heads_width), low),
                ]
                + [shape_of((8, model), full)] * (l == 0),
                [
                    *grads, w_qkv, w_out, cos, sin, bias, kept[m][l]["saved"],
                    kept[m][l]["logsum"], *([] if l else [*kept[m][l]["heads"], norm_gains]),
                ],
                "attn_bwd",
                12,
                after=[*after_here, *after[m]],
            )
            if not l:
                first_gains.append(results[4])
            return results, [*kept[m][l]["heads"], *grads, results[3], kept[m][l]["mixed"]]

        return attend(blocks, call)

    share = model // (dp_n * experts_n)

    woven = experts_n == 2 and dp_n == 4 and share % 32 == 0

    def attn_weights(ins, after, last):
        if last and woven:
            units = WOVEN
            outs = [shape_of((4 * share // 2, model), low)] * 4
        elif woven:
            units = [[(z, e, 0) for z in turned(dp_n)] for e in (0, 1)]
            outs = [shape_of((dp_n * share, model), low)] * 2
        else:
            units = []
            outs = [shape_of((model, model), low)]
        return run_kernel(
            functools.partial(attn_weights_kernel, tensor_n, micro_n, dp_n, experts_n, units),
            outs,
            [place, *ins],
            "attn_weights",
            12,
            scratch=[pltpu.VMEM((model, model), low)] if units else [],
            scalars=1,
            after=after,
        )

    def attn_sums(parts, after):
        if len(parts) == 1:
            grad = parts[0].reshape(dp_n, experts_n, share, model)
            mine = pieces_of(jnp.swapaxes(grad, 0, 1), "expert")
            total = sum(x.astype(full) for x in mine).astype(low)
            return pieces_of(total, "dp")
        one, one_out, two, two_out = parts
        two_in = swap(two_out, "dp", 1)
        one_in = swap(one_out, "expert", 1)
        one, one_out, two, two_out = halves([(one, one_in), (two, two_in)])
        one_in = swap(one_out, "dp", 1)
        two_in = swap(two_out, "expert", 1)
        keep, send = run_kernel(
            weave_kernel,
            [shape_of((share, model), low)] * 2,
            [one, one_in, two, two_in],
            "weave",
            8,
            after=after,
        )
        return [keep, swap(send, "dp", 2)]

    def expert_weights(blocks, hidden, dgu, apart, after, packed=()):
        rows = model // 2 + sum(x.shape[0] // 4 for x in packed[:1])
        return run_kernel(
            functools.partial(expert_weights_kernel, blocks_n, apart, dp_n, bool(packed)),
            [shape_of((rows, 3 * hidden_n), low)] * 2,
            [place, *blocks, hidden, dgu, *packed],
            "expert_weights",
            expert_limit,
            scratch=[pltpu.VMEM((model, 3 * hidden_n), low)],
            scalars=1,
            after=after,
        )

    def halves(pairs, after=()):
        return run_kernel(
            functools.partial(halves_kernel, len(pairs)),
            [
                shape_of((x.shape[0] // 2, x.shape[1]), low)
                for x, _ in pairs
                for _ in range(2)
            ],
            [x for pair in pairs for x in pair],
            "halves",
            12,
            after=after,
        )

    def halve_on(keep, came, after=()):
        bit = 1
        first = None
        while 2 * bit < dp_n:
            keep, send = halves([(keep, came)], after)
            after = ()
            bit *= 2
            first = send if first is None else first
            came = swap(send, "dp", bit)
        return [keep, came], first

    expert_outs = [
        shape_of((2 * half_rows, hidden_n), low),
        shape_of((2 * half_rows, 2 * hidden_n), low),
    ]

    stream = [tokens] * micro_n
    logits = [None] * micro_n
    kept = [[None] * layers for _ in micro]
    for l in range(layers):
        last = l == layers - 1
        kinds = 2 if last else 1
        bufs = []
        for m, (parts, k) in enumerate(attn_fwd(l, hs)):
            mid, h_moe, logits[m], aux, pick, *bufs = run_kernel(
                functools.partial(
                    mid_kernel, l, m, experts_n, routes_n, capacity, last, len(bufs)
                ),
                [
                    shape_of((rows_n, model), full),
                    shape_of((rows_n, model), low),
                    shape_of((rows_n, 128), full),
                    shape_of((rows_n, 128), full),
                    shape_of((experts_n * capacity, 2 * rows_n), low),
                ]
                + [shape_of(((m + 1) * kinds * capacity, model), low)] * experts_n,
                [place, *parts, stream[m], norm_gains, router_low, routes]
                + ([logits[m]] if l else [])
                + ([cotangent] if last else [])
                + bufs,
                "mid",
                12,
                scalars=1,
            )
            kept[m][l] = dict(
                k, mid=mid, h_moe=h_moe, aux=aux, pick=pick, stream=stream[m],
            )
        held = send_rows(bufs)
        if last:
            keep, send, hidden, dgu = run_kernel(
                functools.partial(expert_both_kernel, l, blocks_n),
                [shape_of((kinds * half_rows, model), low)] * 2 + expert_outs,
                [*held, w_gate_up, w_down],
                "expert_both",
                expert_limit,
            )
        else:
            keep, send = run_kernel(
                functools.partial(expert_fwd_kernel, l, blocks_n),
                [shape_of((half_rows, model), low)] * 2,
                [*held, w_gate_up, w_down],
                "expert_fwd",
                expert_limit,
            )
        arrivals, summed = return_rows(keep, send, kinds * each)
        for m in micro:
            kept[m][l]["held"] = held
            kept[m][l]["arrivals"] = arrivals
        if last:
            break
        for m in micro:
            k = kept[m][l]
            stream[m], hs[m] = run_kernel(
                functools.partial(combine_kernel, l, m, experts_n, capacity, arrivals_n),
                [shape_of((rows_n, model), full), shape_of((rows_n, model), low)],
                [
                    *arrivals, k["pick"], k["aux"], k["h_moe"], k["mid"], const_vec, norm_gains,
                ],
                "combine",
                12,
            )

    l = layers - 1
    expert_grads = [None] * layers
    expert_pieces = [None] * layers
    attn_pieces = [None] * layers
    smalls = [[None] * micro_n for _ in range(layers)]
    gains = [None] * (layers - 1)
    expert_grads[l] = expert_weights(held, hidden, dgu, False, [summed])
    expert_pieces[l], first = halve_on(
        expert_grads[l][0], swap(expert_grads[l][1], "dp", 1)
    )
    outputs = []
    dmid = [None] * micro_n
    dattn = [None] * micro_n
    dlogits = [None] * micro_n
    for m in micro:
        k = kept[m][l]
        out, dmid[m], dattn[m], dlogits[m], smalls[l][m] = run_kernel(
            functools.partial(
                turn_kernel, l, m, experts_n, routes_n, capacity, arrivals_n, len(outputs)
            ),
            [
                shape_of((micro_n, rows_n, model), low),
                shape_of((rows_n, model), full),
                shape_of((rows_n, model), low),
                shape_of((rows_n, 128), full),
                shape_of((32, model), full),
            ],
            [
                *arrivals, k["pick"], k["aux"], k["h_moe"], k["mid"], const_vec, norm_gains,
                router_low, cotangent, *outputs,
            ],
            "turn",
            12,
            after=[expert_grads[l][0]],
        )
        outputs = [out]
    (outputs,) = outputs
    before_bwd = [[], [first]]
    attn_in = None
    while True:
        parts = [None] * micro_n
        grads_in = []
        for m, (parts[m], more) in enumerate(attn_bwd(l, dattn, kept, before_bwd)):
            grads_in += more
        attn_in = grads_in
        if l == 0:
            break
        l -= 1
        grad = attn_weights(attn_in, [], False)
        packed = []
        if woven:
            packed = [grad[0], swap(grad[1], "expert", 1)]
        else:
            attn_pieces[l + 1] = attn_sums(grad, [])
        bufs = []
        dstream = [None] * micro_n
        dlocal = [None] * micro_n
        for m in micro:
            k = kept[m][l]
            dstream[m], dlogits[m], dlocal[m], smalls[l][m], *bufs = run_kernel(
                functools.partial(
                    next_back_kernel, l, m, experts_n, routes_n, capacity, arrivals_n, len(bufs)
                ),
                [
                    shape_of((rows_n, model), full),
                    shape_of((rows_n, 128), full),
                    shape_of((rows_n, model), full),
                    shape_of((32, model), full),
                ]
                + [shape_of(((m + 1) * capacity, model), low)] * experts_n,
                [
                    *k["arrivals"], *parts[m], kept[m][l + 1]["stream"], norm_gains, dmid[m],
                    k["pick"], k["aux"], k["h_moe"], const_vec, router_low, dlogits[m],
                    *bufs,
                ],
                "next_back",
                12,
                after=[] if m else [grad[0]],
            )
        held = kept[0][l]["held"]
        grads = send_rows(bufs)
        keep, send, hidden, dgu = run_kernel(
            functools.partial(expert_bwd_kernel, l, blocks_n),
            [shape_of((half_rows, model), low)] * 2 + expert_outs,
            [*held, *grads, w_gate_up, w_down],
            "expert_bwd",
            expert_limit,
            after=[expert_pieces[l + 1][1], *packed[1:]],
        )
        arrivals, summed = return_rows(keep, send, each)
        expert_grads[l] = expert_weights(
            [*held, *grads], hidden, dgu, True, [summed], packed
        )
        expert_came = swap(expert_grads[l][1], "dp", 1)
        gains[l] = [None] * micro_n
        for m in micro:
            k = kept[m][l]
            dmid[m], dattn[m], dgain = run_kernel(
                functools.partial(expert_norm_back_kernel, l, m, capacity, arrivals_n),
                [
                    shape_of((rows_n, model), full),
                    shape_of((rows_n, model), low),
                    shape_of((8, model), full),
                ],
                [*arrivals, k["pick"], dlocal[m], k["mid"], norm_gains, dstream[m]],
                "expert_norm_back",
                12,
                after=[expert_grads[l][0]],
            )
            gains[l][m] = dgain
        before_bwd = [[], []]
        if l:
            expert_pieces[l], first = halve_on(expert_grads[l][0], expert_came)
            before_bwd = [[], [first]]

    grad = attn_weights(attn_in, [], True)
    if layers > 1:
        expert_pieces[0], _ = halve_on(expert_grads[0][0], expert_came, [grad[0]])
    attn_pieces[0] = attn_sums(grad, [])
    (grad_tokens,) = run_kernel(
        functools.partial(input_back_kernel, micro_n),
        [shape_of((micro_n, rows_n, model), full)],
        [x for m in micro for x in (*parts[m], dmid[m])] + [tokens, norm_gains],
        "input_back",
        12,
    )

    each_small = routes_n + 8
    (small,) = run_kernel(
        functools.partial(small_pack_kernel, layers, micro_n, routes_n),
        [shape_of((-(-layers * each_small // 8) * 8, model), full)],
        [x for xs in [*smalls, *gains, first_gains] for x in xs],
        "small_pack",
        8,
    )
    small = sum_all(small)
    attn_gains, moe_gains, grad_router, grad_proj, grad_vec = run_kernel(
        functools.partial(small_out_kernel, layers, routes_n, len(small)),
        [
            shape_of((layers, model), full),
            shape_of((layers, model), full),
            shape_of((routes_n, layers, model), full),
            shape_of((layers, 4, model), full),
            shape_of((layers, 2, model), full),
        ],
        small,
        "small_out",
        8,
    )
    grad_gate_up, grad_down, *packed = run_kernel(
        functools.partial(expert_total_kernel, layers),
        [
            shape_of((layers, 1, 2, model // dp_n, hidden_n), full),
            shape_of((layers, 1, model // dp_n, hidden_n), full),
        ]
        + [shape_of((share, model), full)] * (layers - 1 if woven else 0),
        [x for pieces in expert_pieces for x in pieces],
        "expert_total",
        12,
        after=[grad[0]],
    )
    if woven:
        attn_pieces[1:] = [[x] for x in packed]
    grad_qkv, grad_out = run_kernel(
        functools.partial(attn_total_kernel, layers, [len(x) for x in attn_pieces]),
        [
            shape_of((layers, 3, share, heads_width), full),
            shape_of((layers, heads_width, share), full),
        ],
        [x for pieces in attn_pieces for x in pieces],
        "attn_total",
        12,
    )
    return (
        outputs,
        grad_tokens,
        attn_gains,
        moe_gains,
        grad_qkv,
        grad_out,
        grad_gate_up,
        jnp.swapaxes(grad_down, 2, 3),
        jnp.transpose(grad_router, (1, 2, 0)),
        jnp.swapaxes(grad_proj, 1, 2),
        grad_vec,
    )


def solution(mesh):
    return jax.shard_map(
        local,
        mesh=mesh,
        in_specs=(
            P(None, ("dp", "expert", "tensor"), None),
            P(None, ("dp", "expert", "tensor"), None),
            P(None, ("dp", "expert"), None),
            P(None, ("dp", "expert"), None),
            P(None, None, ("dp", "expert", "tensor"), None),
            P(),
            P(None, None, None, "tensor"),
            P(None, "tensor", None),
            P(None, "expert", None, None, "tensor"),
            P(None, "expert", "tensor", None),
            P(),
            P(),
            P(),
        ),
        out_specs=(
            P(None, ("dp", "expert", "tensor"), None),
            P(None, ("dp", "expert", "tensor"), None),
            P(),
            P(),
            P(None, None, ("dp", "expert"), "tensor"),
            P(None, "tensor", ("dp", "expert")),
            P(None, "expert", None, "dp", "tensor"),
            P(None, "expert", "tensor", "dp"),
            P(),
            P(),
            P(),
        ),
        check_vma=False,
    )
```

```python
import functools
import math

import jax
import jax.numpy as jnp
from jax import lax
from jax.experimental import pallas as pl
from jax.experimental.pallas import tpu as pltpu
from jax.sharding import PartitionSpec as P

HDIM = 64
epsilon = 1e-06
masked_value = -1e30
highest = lax.Precision.HIGHEST
low = jnp.bfloat16
full = jnp.float32
MIB = 1 << 20


FLOPS_PER_US = 1.1e9
MICROS = {"tables": 3.0}


def shape_of(shape, dtype):
    return jax.ShapeDtypeStruct(shape, dtype)


def run_kernel(body, outs, ins, name, limit, scratch=(), scalars=0, after=(), fetched=0):
    ins = list(ins)
    taken = len(ins)
    for i in range(taken - fetched, taken):
        ins[i] = pltpu.with_memory_space_constraint(ins[i], pltpu.HBM)
    vmem = pl.BlockSpec(memory_space=pltpu.VMEM)
    smem = pl.BlockSpec(memory_space=pltpu.SMEM)
    skip = len(after)

    scratch = list(scratch)
    buffers = [pltpu.VMEM(a.shape, a.dtype) for a in ins[taken - fetched :]] if fetched else []

    def kernel(*refs):
        given = refs[:taken]
        rest = refs[taken + skip :]
        if fetched:
            done = rest[-1]
            inside = rest[-1 - fetched : -1]
            rest = rest[: -1 - fetched]
            copies = [
                pltpu.make_async_copy(a, b, done.at[i])
                for i, (a, b) in enumerate(zip(given[taken - fetched :], inside))
            ]
            for copy in copies:
                copy.start()
            for copy in copies:
                copy.wait()
            given = (*given[: taken - fetched], *inside)
        body(*given, *rest)

    if fetched:
        scratch += [*buffers, pltpu.SemaphoreType.DMA((fetched,))]
    return pl.pallas_call(
        kernel,
        out_shape=tuple(outs),
        in_specs=[smem] * scalars
        + [vmem] * (taken - scalars - fetched)
        + [pl.BlockSpec(memory_space=pltpu.HBM)] * fetched
        + [pl.BlockSpec(memory_space=pl.ANY)] * skip,
        out_specs=tuple([vmem] * len(outs)),
        scratch_shapes=scratch,
        compiler_params=pltpu.CompilerParams(vmem_limit_bytes=limit * MIB),
        cost_estimate=pl.CostEstimate(
            flops=int(MICROS.get(name, 0.0) * FLOPS_PER_US), bytes_accessed=0, transcendentals=0
        ),
        name=name,
    )(*ins, *after)


def dot(a, b):
    return jnp.dot(a, b, preferred_element_type=full)


def dot_nt(a, b):
    return lax.dot_general(a, b, (((1,), (1,)), ((), ())), preferred_element_type=full)


def dot_tn(a, b):
    return lax.dot_general(a, b, (((0,), (0,)), ((), ())), preferred_element_type=full)


def lanes(rows, width=128):
    return lax.broadcasted_iota(jnp.int32, (rows, width), 1)


def sublanes(rows, width=128):
    return lax.broadcasted_iota(jnp.int32, (rows, width), 0)


def join(parts):
    if parts[0].shape[0] % 16:
        return jnp.concatenate([p.astype(full) for p in parts], axis=0).astype(low)
    return jnp.concatenate(parts, axis=0)


def stack_rows(refs, start=0, count=None):
    if count is None or count == refs[0].shape[0]:
        return join([r[...] for r in refs])
    if count % 16 or start % 16:
        return join([r[...].astype(full)[start : start + count].astype(low) for r in refs])
    return join([r[start : start + count, :] for r in refs])


def rms_scale(rows):
    return lax.rsqrt(jnp.mean(rows * rows, axis=-1, keepdims=True) + epsilon)


def split2(rows):
    top = rows.astype(low)
    return top, (rows - top.astype(full)).astype(low)


def as_column(row):
    n = row.shape[1]
    return jnp.sum(jnp.where(sublanes(n, n) == lanes(n, n), row, 0.0), axis=1, keepdims=True)


def norm_kernel(m, tokens, gains, out):
    rows = tokens[m].astype(full)
    out[...] = (rows * rms_scale(rows) * gains[0, 0:1, :]).astype(low)


def tables_kernel(tensor_n, place, lengths, order, w_router, const_proj, tokens, gains, cos, sin, bias, router_low,
                  normed):
    norm_kernel(1, tokens, gains, normed)
    micro_n, _, seq = order.shape
    rows_n = seq // tensor_n
    segments = lengths.shape[2]
    mine = place[0]
    half = HDIM // 2
    lane = lanes(rows_n)
    frequency = jnp.exp((lane % half).astype(full) * (-math.log(10000.0) / half))
    sign = jnp.where(lane % HDIM < half, -1.0, 1.0)
    for m in range(micro_n):
        row = order[m].astype(full)
        cuts = [row[:, j * rows_n : (j + 1) * rows_n] for j in range(tensor_n)]
        blocks = []
        for j in range(tensor_n):
            block = jnp.zeros((1, rows_n), full)
            for i in range(tensor_n):
                block = jnp.where((mine ^ j) == i, cuts[i], block)
            blocks.append(block)
        across = jnp.concatenate(blocks, axis=1)
        starts = []
        total = lengths[m, 0, 0]
        for s in range(1, segments):
            starts.append(total.astype(full))
            total = total + lengths[m, 0, s]
        for j in range(tensor_n):
            part = slice(j * rows_n, (j + 1) * rows_n)
            down = as_column(blocks[j])
            begin = jnp.zeros_like(down)
            for start in starts:
                begin = jnp.where(down >= start, start, begin)
            angle = (down - begin) * frequency
            cos[m, part, :] = jnp.cos(angle)
            sin[m, part, :] = jnp.sin(angle) * sign
            bias[m, part, :] = jnp.where(
                (begin <= across) & (across <= down), 0.0, masked_value
            ).astype(low)
    routes_n, layers, model = w_router.shape
    proj_n = const_proj.shape[1]
    for l in range(layers):
        both = jnp.concatenate(
            [w_router[r, l : l + 1, :] for r in range(routes_n)]
            + [const_proj[l], jnp.zeros((128 - routes_n - proj_n, model), full)],
            axis=0,
        )
        top = both.astype(low)
        rest = both - top.astype(full)
        middle = rest.astype(low)
        router_low[l, 0:128, :] = top
        router_low[l, 128:256, :] = middle
        router_low[l, 256:384, :] = (rest - middle.astype(full)).astype(low)


def swap_halves(rows):
    lane = lanes(rows.shape[0])
    half = HDIM // 2
    return jnp.where(
        lane % HDIM < half, pltpu.roll(rows, 128 - half, 1), pltpu.roll(rows, half, 1)
    )


def half_masks():
    lane = lanes(1)
    return (lane < HDIM).astype(full).astype(low), (lane >= HDIM).astype(full).astype(low)


def attn_fwd_kernel(l, m, blocks, *refs):
    heads = refs[:blocks]
    w, wo, cos, sin, bias, keep, far, send, saved, mixed, logsum = refs[blocks:]
    pair = 2 * HDIM
    h = stack_rows(heads)
    c = cos[m]
    s = sin[m]
    lane = lanes(h.shape[0])

    def turn(chunk):
        return chunk * c + swap_halves(chunk) * s

    q = dot_nt(h, w[l, 0])
    k = dot_nt(h, w[l, 1])
    v = dot_nt(h, w[l, 2])
    saved[:, 0:128] = (turn(q[:, 0:pair]) * 0.125).astype(low)
    saved[:, 128:256] = turn(k[:, 0:pair]).astype(low)
    saved[:, 256:384] = v[:, 0:pair].astype(low)
    third = turn(jnp.concatenate([q[:, pair:], k[:, pair:]], axis=1))
    saved[:, 384:512] = jnp.where(lane < HDIM, third * 0.125, 0.0).astype(low)
    saved[:, 512:640] = jnp.where(lane < HDIM, pltpu.roll(third, HDIM, 1), 0.0).astype(low)
    saved[:, 640:768] = jnp.concatenate(
        [v[:, pair:], jnp.zeros((h.shape[0], HDIM), full)], axis=1
    ).astype(low)
    first, second = half_masks()
    shift = bias[m].astype(full)
    q01 = saved[:, 0:128]
    heads = (
        (q01 * first, slice(128, 256), slice(256, 384)),
        (q01 * second, slice(128, 256), slice(256, 384)),
        (saved[:, 384:512], slice(512, 640), slice(640, 768)),
    )
    scores = [dot_nt(query, saved[:, keys]) + shift for query, keys, _ in heads]
    peaks = [jnp.max(x, axis=-1, keepdims=True) for x in scores]
    powers = [jnp.exp(x - peak) for x, peak in zip(scores, peaks)]
    totals = [jnp.sum(x, axis=-1, keepdims=True) for x in powers]
    results = [
        dot((x * (1.0 / total)).astype(low), saved[:, values])
        for x, total, (_, _, values) in zip(powers, totals, heads)
    ]
    sums = [peak + jnp.log(total) for peak, total in zip(peaks, totals)]
    logsum[...] = jnp.where(lane == 0, sums[0], jnp.where(lane == 1, sums[1], sums[2]))
    mixed[:, 0:pair] = jnp.where(lane < HDIM, results[0], results[1]).astype(low)
    mixed[:, pair : pair + HDIM] = results[2][:, 0:HDIM].astype(low)
    spread(dot(mixed[...], wo[l]).astype(low), keep, far, send)


def spread(value, keep, far, send):
    rows_n = keep.shape[0]
    keep[...] = value[0:rows_n]
    far[...] = value[2 * rows_n : 3 * rows_n]
    send[0:rows_n, :] = value[rows_n : 2 * rows_n]
    send[rows_n : 2 * rows_n, :] = value[3 * rows_n : 4 * rows_n]


def attn_bwd_kernel(l, m, blocks, *refs):
    grads = refs[:blocks]
    w, wo, cos, sin, bias, saved, logsum, *more = refs[blocks:]
    if not l:
        *rows, gains, dgain = more[: blocks + 1] + more[-1:]
        more = more[blocks + 1 : -1]
    keep, far, send, dqkv = more
    pair = 2 * HDIM
    c = cos[m]
    s = sin[m]
    dattn = stack_rows(grads)
    dmix = dot_nt(dattn, wo[l]).astype(low)
    seq = dmix.shape[0]
    d01 = dmix[:, 0:pair]
    d2 = jnp.concatenate([dmix[:, pair:], jnp.zeros((seq, HDIM), low)], axis=1)
    first, second = half_masks()
    q01 = saved[:, 0:128]
    k01 = saved[:, 128:256]
    v01 = saved[:, 256:384]
    q2 = saved[:, 384:512]
    k2 = saved[:, 512:640]
    v2 = saved[:, 640:768]
    heads = (
        (q01 * first, k01 * first, v01, d01 * first),
        (q01 * second, k01 * second, v01, d01 * second),
        (q2, k2, v2, d2),
    )
    shift = bias[m].astype(full)
    dqs, dks, dvs = [], [], []
    for n, (query, keys, values, dout) in enumerate(heads):
        probs = jnp.exp(dot_nt(query, keys) + shift - logsum[:, n : n + 1])
        dprobs = dot_nt(dout, values)
        inner = jnp.sum(probs * dprobs, axis=-1, keepdims=True)
        dscores = (probs * (dprobs - inner)).astype(low)
        dqs.append(dot(dscores, keys))
        dks.append(dot_tn(dscores, query))
        dvs.append(dot_tn(probs.astype(low), dout))

    def turn_back(chunk):
        return chunk * c - swap_halves(chunk) * s

    third = turn_back(dqs[2] * 0.125 + pltpu.roll(dks[2], HDIM, 1)).astype(low)
    dq = jnp.concatenate([turn_back((dqs[0] + dqs[1]) * 0.125).astype(low), third[:, :HDIM]], axis=1)
    dk = jnp.concatenate([turn_back(dks[0] + dks[1]).astype(low), third[:, HDIM:]], axis=1)
    dv = jnp.concatenate([dvs[0] + dvs[1], dvs[2][:, :HDIM]], axis=1).astype(low)
    dqkv[0] = dq
    dqkv[1] = dk
    dqkv[2] = dv
    dh = dot(dq, w[l, 0]) + dot(dk, w[l, 1]) + dot(dv, w[l, 2])
    spread(dh.astype(low), keep, far, send)
    if not l:
        along = jnp.sum(dh * stack_rows(rows).astype(full), axis=0, keepdims=True)
        dgain[...] = jnp.broadcast_to(along / gains[l, 0:1, :], dgain.shape)


def attn_weights_kernel(blocks, micro, dp_n, experts_n, units, *refs):
    place = refs[0]
    total = (2 * blocks + 2) * micro
    outs = refs[1 + total : -1]
    out = refs[-1]
    refs = refs[1 : 1 + total]
    per = 2 * blocks + 2
    pair = 2 * HDIM
    groups = [refs[m * per : (m + 1) * per] for m in range(micro)]
    h = jnp.concatenate([stack_rows(g[:blocks]) for g in groups], axis=0)
    d = jnp.concatenate([stack_rows(g[blocks : 2 * blocks]) for g in groups], axis=0)
    third = []
    for i in range(3):
        part = dot_tn(h, jnp.concatenate([g[2 * blocks][i] for g in groups], axis=0))
        out[:, i * pair : (i + 1) * pair] = part[:, :pair].astype(low)
        third.append(part[:, pair:])
    part = dot_tn(d, jnp.concatenate([g[2 * blocks + 1][...] for g in groups], axis=0))
    out[:, 3 * pair : 4 * pair] = part[:, :pair].astype(low)
    third.append(part[:, pair:])
    out[:, 4 * pair : 5 * pair] = jnp.concatenate(third[0:2], axis=1).astype(low)
    out[:, 5 * pair : 6 * pair] = jnp.concatenate(third[2:4], axis=1).astype(low)
    share = out.shape[0] // (dp_n * experts_n)
    for ref, mine in zip(outs, units):
        rows_n = ref.shape[0] // len(mine)
        for i, (zr, er, part) in enumerate(mine):
            owner = (place[2] ^ zr) * experts_n + (place[1] ^ er)
            at = pl.multiple_of(owner * share + part * rows_n, rows_n)
            ref[i * rows_n : (i + 1) * rows_n, :] = out[pl.ds(at, rows_n), :]


WOVEN = (
    [(z, 0, 0) for z in (0, 2, 1, 3)],
    [(z, 1, 0) for z in (0, 2, 1, 3)],
    [(z, e, 1) for e in (0, 1) for z in (0, 2)],
    [(z, e, 1) for e in (0, 1) for z in (1, 3)],
)


def halves_kernel(pairs, *refs):
    outs = list(refs[2 * pairs :])
    for n in range(pairs):
        one, two = refs[2 * n : 2 * n + 2]
        at = 0
        while at < one.shape[0]:
            out = outs.pop(0)
            rows_n = out.shape[0]
            part = slice(at, at + rows_n)
            out[...] = (one[part, :].astype(full) + two[part, :].astype(full)).astype(low)
            at += rows_n


def weave_kernel(one, one_in, two, two_in, keep, send):
    rows_n = one.shape[0] // 2
    for n, (a, b) in enumerate(((one, one_in), (two, two_in))):
        at = slice(n * rows_n, (n + 1) * rows_n)
        keep[at, :] = (a[0:rows_n, :].astype(full) + b[0:rows_n, :].astype(full)).astype(low)
        send[at, :] = (a[rows_n:, :].astype(full) + b[rows_n:, :].astype(full)).astype(low)


def add_far_kernel(far, arrived, out):
    rows_n = far.shape[0]
    out[...] = (far[...].astype(full) + arrived[rows_n : 2 * rows_n, :].astype(full)).astype(low)


def add_back_kernel(keep, arrived, *outs):
    rows_n = outs[0].shape[0]
    for i, out in enumerate(outs):
        part = slice(i * rows_n, (i + 1) * rows_n)
        out[...] = (keep[part, :].astype(full) + arrived[part, :].astype(full)).astype(low)


def fill_bufs(bufs, earlier, parts, capacity):
    for k, buf in enumerate(bufs):
        pieces = []
        for f, part in enumerate(parts):
            if earlier:
                before = earlier[k][...].astype(full)
                pieces.append(before[f * capacity : (f + 1) * capacity])
            pieces.append(part[k * capacity : (k + 1) * capacity])
        buf[...] = jnp.concatenate(pieces, axis=0).astype(low)


def mid_kernel(l, m, experts_n, routes_n, capacity, last, earlier_n, *refs):
    place, keep, arrived, across, stream, gains, router, routes = refs[:8]
    at = 8
    if l:
        previous = refs[at]
        at += 1
    if last:
        cotangent = refs[at]
        at += 1
    earlier = refs[at : at + earlier_n]
    at += earlier_n
    mid, h_moe, logits_out, aux, pick, *bufs = refs[at:]
    rows_n = keep.shape[0]
    rows = stream[m] if l == 0 else stream[...]
    rows = (
        rows.astype(full)
        + keep[...].astype(full)
        + arrived[0:rows_n, :].astype(full)
        + across[...].astype(full)
    )
    mid[...] = rows
    h = (rows * rms_scale(rows) * gains[l, 1:2, :]).astype(low)
    h_moe[...] = h
    parts = dot_nt(h, router[l])
    raw = parts[:, 0:128] + parts[:, 128:256] + parts[:, 256:384]
    lane = lanes(rows_n)
    logits = raw + previous[...] if l else raw
    logits_out[...] = jnp.where(lane < routes_n, logits, 0.0)
    columns = [as_column(routes[l, m, k : k + 1, :].astype(full)) for k in range(2)]
    picked = [
        jnp.sum(jnp.where(lane.astype(full) == column, logits, 0.0), axis=-1, keepdims=True)
        for column in columns
    ]
    peak = jnp.maximum(picked[0], picked[1])
    gate = [jnp.exp(p - peak) for p in picked]
    both = gate[0] + gate[1]
    gates = [gate[0] / both, gate[1] / both]
    numbers = list(gates)
    for j in range(2):
        two = [raw[:, routes_n + 2 * j + i : routes_n + 2 * j + i + 1] for i in range(2)]
        peak = jnp.maximum(two[0], two[1])
        power = [jnp.exp(p - peak) for p in two]
        both = power[0] + power[1]
        numbers += [power[0] / both, power[1] / both]
    numbers += columns
    value = jnp.zeros((rows_n, 128), full)
    for i, number in enumerate(numbers):
        value = jnp.where(lane == i, number, value)
    aux[...] = value
    here = place[1]
    along = []
    for k in range(2):
        route = routes[l, m, k : k + 1, :]
        along.append(jnp.where(route < experts_n, route ^ here, route).astype(full))
    index_rows = max(16, experts_n)
    expert = sublanes(index_rows, rows_n).astype(full)
    member = ((along[0] == expert) | (along[1] == expert)).astype(full).astype(low)
    before = (sublanes(rows_n, rows_n) < lanes(rows_n, rows_n)).astype(full).astype(low)
    rank = dot(member, before)
    slot = sublanes(capacity, rows_n).astype(full)
    picks = [
        jnp.concatenate(
            [
                ((slot == rank[k : k + 1, :]) & (route == k)).astype(full)
                for k in range(experts_n)
            ],
            axis=0,
        )
        for route in along
    ]
    pick[:, 0:rows_n] = picks[0].astype(low)
    pick[:, rows_n : 2 * rows_n] = picks[1].astype(low)
    sent = [dot((picks[0] + picks[1]).astype(low), h)]
    if last:
        dstream = cotangent[m].astype(full)
        sent.append(
            dot(picks[0].astype(low), (gates[0] * dstream).astype(low))
            + dot(picks[1].astype(low), (gates[1] * dstream).astype(low))
        )
    fill_bufs(bufs, earlier, sent, capacity)


def route_columns(aux):
    return [aux[:, 6 + k : 7 + k] for k in range(2)]


def route_values(experts_n, pick, values_low, aux, columns, h, vec):
    rows_n = h.shape[0]
    twice = jnp.concatenate([pick[...], pick[...]], axis=0)
    both = dot_tn(twice, values_low)
    values = []
    for k in range(2):
        route = columns[k]
        scale = (route == experts_n + 1).astype(full)
        value = both[k * rows_n : (k + 1) * rows_n]
        for j in range(2):
            here = (route == experts_n + 2 + j).astype(full)
            scale = scale + here * aux[:, 2 + 2 * j : 3 + 2 * j]
            value = value + (here * aux[:, 3 + 2 * j : 4 + 2 * j]) * vec[j : j + 1, :]
        values.append(value + scale * h)
    return values


def combine_kernel(l, m, experts_n, capacity, arrivals_n, *refs):
    arrivals = refs[:arrivals_n]
    pick, aux, h_moe, mid, vec, gains, stream, h_next = refs[arrivals_n:]
    columns = route_columns(aux)
    values = route_values(
        experts_n, pick, stack_rows(arrivals, m * capacity, capacity), aux, columns,
        h_moe[...].astype(full), vec[l],
    )
    rows = mid[...] + aux[:, 0:1] * values[0] + aux[:, 1:2] * values[1]
    stream[...] = rows
    h_next[...] = (rows * rms_scale(rows) * gains[l + 1, 0:1, :]).astype(low)


def route_back(
    l, experts_n, routes_n, dstream, values, pick, aux, columns, h_low, vec, router, dnext,
    small,
):
    lane = lanes(dstream.shape[0])
    h = h_low.astype(full)
    gates = [aux[:, k : k + 1] for k in range(2)]
    dgate = [jnp.sum(dstream * v, axis=-1, keepdims=True) for v in values]
    mean = gates[0] * dgate[0] + gates[1] * dgate[1]
    dlogits = dnext
    for k in range(2):
        dlogits = dlogits + jnp.where(lane.astype(full) == columns[k], gates[k] * (dgate[k] - mean), 0.0)

    def gate_of(route):
        return sum((columns[k] == route).astype(full) * gates[k] for k in range(2))

    along_h = jnp.sum(dstream * h, axis=-1, keepdims=True)
    scale = gate_of(experts_n + 1)
    both = dlogits
    for j in range(2):
        share = gate_of(experts_n + 2 + j)
        mix = [aux[:, 2 + 2 * j + i : 3 + 2 * j + i] for i in range(2)]
        along_v = jnp.sum(dstream * vec[l, j : j + 1, :], axis=-1, keepdims=True)
        dm = [share * along_h, share * along_v]
        inner = mix[0] * dm[0] + mix[1] * dm[1]
        for i in range(2):
            both = jnp.where(lane == routes_n + 2 * j + i, mix[i] * (dm[i] - inner), both)
        scale = scale + mix[0] * share
        small[24 + j : 25 + j, :] = jnp.sum((mix[1] * share) * dstream, axis=0, keepdims=True)
    top, rest = split2(both)
    dlocal = scale * dstream + (
        dot(top, router[l, 0:128, :])
        + dot(top, router[l, 128:256, :])
        + dot(rest, router[l, 0:128, :])
    )
    small[0:24, :] = (dot_tn(top, h_low) + dot_tn(rest, h_low))[0:24]
    return dlogits, dlocal


def norm_back(dh, rows, gain):
    scale = rms_scale(rows)
    unit = rows * scale
    dn = dh * gain
    drows = scale * (dn - unit * jnp.mean(dn * unit, axis=-1, keepdims=True))
    return drows, jnp.sum(dh * unit, axis=0, keepdims=True)


def turn_kernel(l, m, experts_n, routes_n, capacity, arrivals_n, earlier_n, *refs):
    arrivals = refs[:arrivals_n]
    pick, aux, h_moe, mid, vec, gains, router, cotangent = refs[
        arrivals_n : arrivals_n + 8
    ]
    at = arrivals_n + 8
    earlier = refs[at : at + earlier_n]
    out, dmid, dattn, dlogits_out, small = refs[at + earlier_n :]
    micro = len(earlier) + 1
    columns = route_columns(aux)
    h_low = h_moe[...]
    values = route_values(
        experts_n, pick, stack_rows(arrivals, m * capacity, capacity), aux, columns,
        h_low.astype(full), vec[l],
    )
    rows = mid[...]
    for i, ref in enumerate(earlier):
        out[i] = ref[i]
    out[m] = (rows + aux[:, 0:1] * values[0] + aux[:, 1:2] * values[1]).astype(low)
    for i in range(m + 1, out.shape[0]):
        out[i] = jnp.zeros(out.shape[1:], low)
    small[24:32, :] = jnp.zeros((8, small.shape[1]), full)
    dstream = cotangent[m].astype(full)
    dlogits, dlocal = route_back(
        l, experts_n, routes_n, dstream, values, pick, aux, columns, h_low, vec, router,
        jnp.zeros((dstream.shape[0], 128), full), small,
    )
    dlogits_out[...] = dlogits
    rows_n = rows.shape[0]
    both = pick[:, 0:rows_n] + pick[:, rows_n : 2 * rows_n]
    twice = jnp.concatenate([both, both], axis=0)
    at = (cotangent.shape[0] + m) * capacity
    dh = dlocal + dot_tn(twice, stack_rows(arrivals, at, capacity))
    drows, dgain = norm_back(dh, rows, gains[l, 1:2, :])
    small[26:27, :] = dgain
    value = dstream + drows
    dmid[...] = value
    dattn[...] = value.astype(low)


def next_back_kernel(l, m, experts_n, routes_n, capacity, arrivals_n, earlier_n, *refs):
    arrivals = refs[:arrivals_n]
    (keep, arrived, across, stream, gains, dmid, pick, aux, h_moe, vec, router,
     dnext) = refs[arrivals_n : arrivals_n + 12]
    at = arrivals_n + 12
    earlier = refs[at : at + earlier_n]
    dstream_out, dlogits_out, dlocal_out, small, *bufs = refs[at + earlier_n :]
    rows_n = keep.shape[0]
    dh = keep[...].astype(full) + arrived[0:rows_n, :].astype(full) + across[...].astype(full)
    drows, dgain = norm_back(dh, stream[...], gains[l + 1, 0:1, :])
    dstream = dmid[...] + drows
    dstream_out[...] = dstream
    small[24:32, :] = jnp.zeros((8, small.shape[1]), full)
    small[27:28, :] = dgain
    columns = route_columns(aux)
    h_low = h_moe[...]
    values = route_values(
        experts_n, pick, stack_rows(arrivals, m * capacity, capacity), aux, columns,
        h_low.astype(full), vec[l],
    )
    gates = [aux[:, k : k + 1] for k in range(2)]
    sent = dot(pick[:, 0:rows_n], (gates[0] * dstream).astype(low)) + dot(
        pick[:, rows_n : 2 * rows_n], (gates[1] * dstream).astype(low)
    )
    fill_bufs(bufs, earlier, [sent], capacity)
    dlogits, dlocal = route_back(
        l, experts_n, routes_n, dstream, values, pick, aux, columns, h_low, vec, router,
        dnext[...], small,
    )
    dlogits_out[...] = dlogits
    dlocal_out[...] = dlocal


def expert_norm_back_kernel(l, m, capacity, arrivals_n, *refs):
    arrivals = refs[:arrivals_n]
    pick, dlocal, mid, gains, dstream, dmid, dattn, dgain_out = refs[arrivals_n:]
    rows_n = mid.shape[0]
    both = pick[:, 0:rows_n] + pick[:, rows_n : 2 * rows_n]
    twice = jnp.concatenate([both, both], axis=0)
    dh = dlocal[...] + dot_tn(twice, stack_rows(arrivals, m * capacity, capacity))
    drows, dgain = norm_back(dh, mid[...], gains[l, 1:2, :])
    dgain_out[...] = jnp.broadcast_to(dgain, dgain_out.shape)
    value = dstream[...] + drows
    dmid[...] = value
    dattn[...] = value.astype(low)


def input_back_kernel(micro, *refs):
    tokens, gains, out = refs[4 * micro :]
    for m in range(micro):
        keep, arrived, across, dmid = refs[4 * m : 4 * m + 4]
        rows_n = keep.shape[0]
        dh = keep[...].astype(full) + arrived[0:rows_n, :].astype(full) + across[...].astype(full)
        drows, _ = norm_back(dh, tokens[m].astype(full), gains[0, 0:1, :])
        out[m] = dmid[...] + drows


def expert_fwd_kernel(l, blocks_n, *refs):
    gate_up, down, keep, send = refs[blocks_n:]
    rows = stack_rows(refs[:blocks_n])
    g = dot(rows, gate_up[l, 0, 0])
    u = dot(rows, gate_up[l, 0, 1])
    hidden = (g * jax.nn.sigmoid(g) * u).astype(low)
    value = dot(hidden, down[l, 0]).astype(low)
    half = keep.shape[0]
    keep[...] = value[0:half]
    send[...] = value[half:]


def expert_back(l, rows, grads, gate_up, down):
    g = dot(rows, gate_up[l, 0, 0])
    u = dot(rows, gate_up[l, 0, 1])
    dhidden = dot_nt(grads, down[l, 0])
    s = jax.nn.sigmoid(g)
    silu = g * s
    hidden = (silu * u).astype(low)
    dg = (dhidden * u * s * (1.0 + g * (1.0 - s))).astype(low)
    du = (dhidden * silu).astype(low)
    drows = (dot_nt(dg, gate_up[l, 0, 0]) + dot_nt(du, gate_up[l, 0, 1])).astype(low)
    return hidden, dg, du, drows


def expert_both_kernel(l, blocks_n, *refs):
    blocks = refs[:blocks_n]
    gate_up, down, keep, send, hidden_out, dgu_out = refs[blocks_n:]
    each = blocks[0].shape[0] // 2
    rows = stack_rows(blocks, 0, each)
    grads = stack_rows(blocks, each, each)
    hidden, dg, du, drows = expert_back(l, rows, grads, gate_up, down)
    hidden_out[...] = hidden
    width = dg.shape[1]
    dgu_out[:, 0:width] = dg
    dgu_out[:, width : 2 * width] = du
    value = dot(hidden, down[l, 0]).astype(low)
    for i in range(blocks_n):
        out = keep if i < blocks_n // 2 else send
        at = 2 * each * (i % (blocks_n // 2))
        out[at : at + each, :] = value[i * each : (i + 1) * each]
        out[at + each : at + 2 * each, :] = drows[i * each : (i + 1) * each]


def expert_bwd_kernel(l, blocks_n, *refs):
    gate_up, down, keep, send, hidden_out, dgu_out = refs[2 * blocks_n :]
    rows = stack_rows(refs[:blocks_n])
    grads = stack_rows(refs[blocks_n : 2 * blocks_n])
    hidden, dg, du, drows = expert_back(l, rows, grads, gate_up, down)
    hidden_out[...] = hidden
    width = dg.shape[1]
    dgu_out[:, 0:width] = dg
    dgu_out[:, width : 2 * width] = du
    half = keep.shape[0]
    keep[...] = drows[0:half]
    send[...] = drows[half:]


def turned(n):
    order = [0]
    bit = n // 2
    while bit:
        order = order + [k + bit for k in order]
        bit //= 2
    bits = n.bit_length() - 1
    return [int(format(i, "b").zfill(bits)[::-1], 2) for i in range(n)]


def expert_weights_kernel(blocks_n, apart, pieces, packed, parts, *refs):
    place = refs[0]
    refs = refs[1:]
    if packed:
        ends = refs[-1 - 2 * parts :]
        one, two = refs[-3 - 2 * parts : -1 - 2 * parts]
        extra = (one[...].astype(full) + two[...].astype(full)).astype(low)
        refs = (*refs[: -3 - 2 * parts], *ends)
    if apart:
        rows = stack_rows(refs[:blocks_n])
        grads = stack_rows(refs[blocks_n : 2 * blocks_n])
    else:
        each = refs[0].shape[0] // 2
        rows = stack_rows(refs[:blocks_n], 0, each)
        grads = stack_rows(refs[:blocks_n], each, each)
    hidden, dgu, *outs, total = refs[-3 - 2 * parts :]
    width = dgu.shape[1]
    total[:, 0:width] = dot_tn(rows, dgu[...]).astype(low)
    total[:, width : width + hidden.shape[1]] = dot_tn(grads, hidden[...]).astype(low)
    share = total.shape[0] // pieces
    for i, k in enumerate(turned(pieces)):
        at = pl.multiple_of((place[2] ^ k) * share, share)
        mine = [total[pl.ds(at, share), :]]
        if packed:
            more = extra.shape[0] // pieces // 2
            mine.append(
                jnp.concatenate(
                    [extra[(2 * i + n) * more : (2 * i + n + 1) * more] for n in range(2)], axis=1
                )
            )
        unit = jnp.concatenate(mine, axis=0)
        begin = 0
        for part in range(parts):
            out = outs[2 * part + 2 * i // pieces]
            rows_n = out.shape[0] // (pieces // 2)
            to = i % (pieces // 2) * rows_n
            out[to : to + rows_n, :] = unit[begin : begin + rows_n]
            begin += rows_n


def expert_total_kernel(layers, counts, *refs):
    gate_up, down, *packed = refs[sum(counts) :]
    width, share = gate_up.shape[4], gate_up.shape[3]
    for l in range(layers):
        mine = refs[sum(counts[:l]) : sum(counts[: l + 1])]
        total = jnp.concatenate(
            [a[...].astype(full) + b[...].astype(full) for a, b in zip(mine[::2], mine[1::2])],
            axis=0,
        )
        for i in range(2):
            gate_up[l, 0, i] = total[0:share, i * width : (i + 1) * width]
        down[l, 0] = total[0:share, 2 * width : 3 * width]
        if packed and l < layers - 1:
            half = packed[l].shape[1]
            packed[l][...] = jnp.concatenate(
                [total[share:, 0:half], total[share:, half : 2 * half]], axis=0
            )


def attn_total_kernel(layers, counts, *refs):
    qkv, out = refs[sum(counts) :]
    pair = 2 * HDIM
    for l in range(layers):
        mine = refs[sum(counts[:l]) : sum(counts[: l + 1])]
        total = mine[0][...].astype(full)
        for ref in mine[1:]:
            total = total + ref[...].astype(full)
        third = total[:, 4 * pair :]
        for i in range(3):
            qkv[l, i, :, 0:pair] = total[:, i * pair : (i + 1) * pair]
            qkv[l, i, :, pair : pair + HDIM] = third[:, i * HDIM : (i + 1) * HDIM]
        out[l, 0:pair, :] = total[:, 3 * pair : 4 * pair].T
        out[l, pair : pair + HDIM, :] = third[:, 3 * HDIM :].T


def swap(x, axis, k):
    n = lax.axis_size(axis)
    return lax.ppermute(x, axis, [(i, i ^ k) for i in range(n)])


def swap_pair(x, k, j):
    experts_n = lax.axis_size("expert")
    tensor_n = lax.axis_size("tensor")
    if j == 0:
        return swap(x, "expert", k)
    if k == 0:
        return swap(x, "tensor", j)
    table = [
        (e * tensor_n + t, (e ^ k) * tensor_n + (t ^ j))
        for e in range(experts_n)
        for t in range(tensor_n)
    ]
    return lax.ppermute(x, ("expert", "tensor"), table)


def attend(blocks, call):
    results = []
    for m, block in enumerate(blocks):
        near = swap(block, "tensor", 1)
        far = swap(block, "tensor", 2)
        pack = [block, near, far, swap(far, "tensor", 1)]
        (keep, away, send, *rest), extra = call(m, pack, [])
        arrived = swap(send, "tensor", 1)
        (total,) = run_kernel(
            add_far_kernel, [shape_of(away.shape, low)], [away, arrived], "add_far", 8
        )
        results.append(([keep, arrived, swap(total, "tensor", 2)], extra))
    return results


def send_rows(bufs):
    experts_n = len(bufs)
    far = [swap_pair(buf, k, 2) for k, buf in enumerate(bufs)]
    near = [bufs[0]] + [swap_pair(bufs[k], k, 0) for k in range(1, experts_n)]
    held = near + far
    return held + [swap(x, "tensor", 1) for x in held]


def return_rows(keep, send, each):
    experts_n = lax.axis_size("expert")
    arrived = swap(send, "tensor", 1)
    sums = run_kernel(
        add_back_kernel,
        [shape_of((each, keep.shape[1]), low)] * (2 * experts_n),
        [keep, arrived],
        "add_back",
        8,
    )
    far = [swap_pair(sums[experts_n + k], k, 2) for k in range(experts_n)]
    near = [sums[0]] + [swap_pair(sums[k], k, 0) for k in range(1, experts_n)]
    return near + far, sums[0]


def small_pack_kernel(layers, micro, routes_n, *refs):
    smalls = [refs[l * micro : (l + 1) * micro] for l in range(layers)]
    at = layers * micro
    gains = [refs[at + l * micro : at + (l + 1) * micro] for l in range(layers - 1)]
    *first_gains, out = refs[at + (layers - 1) * micro :]
    pieces = []
    last_gain = sum(ref[0:1, :] for ref in first_gains)
    for l in range(layers):
        total = smalls[l][0][...]
        for ref in smalls[l][1:]:
            total = total + ref[...]
        if l < layers - 1:
            moe = gains[l][0][0:1, :]
            for ref in gains[l][1:]:
                moe = moe + ref[0:1, :]
        else:
            moe = total[26:27]
        pieces += [total[0 : routes_n + 4], total[24:26], moe, last_gain]
        last_gain = total[27:28]
    rows = sum(p.shape[0] for p in pieces)
    if out.shape[0] > rows:
        pieces.append(jnp.zeros((out.shape[0] - rows, out.shape[1]), full))
    out[...] = jnp.concatenate(pieces, axis=0).astype(low)


def sum_kernel(*refs):
    total = refs[0][...].astype(full)
    for ref in refs[1:-1]:
        total = total + ref[...].astype(full)
    refs[-1][...] = total


def small_out_kernel(layers, routes_n, parts, *refs):
    attn_gains, moe_gains, router, proj, vec = refs[parts:]
    total = refs[0][...]
    for ref in refs[1:parts]:
        total = total + ref[...]
    each = routes_n + 8
    for l in range(layers):
        mine = total[l * each : (l + 1) * each]
        for r in range(routes_n):
            router[r, l : l + 1, :] = mine[r : r + 1]
        proj[l] = mine[routes_n : routes_n + 4]
        vec[l] = mine[routes_n + 4 : routes_n + 6]
        moe_gains[l : l + 1, :] = mine[routes_n + 6 : routes_n + 7]
        attn_gains[l : l + 1, :] = mine[routes_n + 7 : routes_n + 8]


def sum_rows(parts):
    (out,) = run_kernel(sum_kernel, [shape_of(parts[0].shape, full)], parts, "sum", 8)
    return out


def sum_all(rows):
    over_dp = sum_rows([rows] + [swap(rows, "dp", k) for k in range(1, lax.axis_size("dp"))])
    over_cores = sum_rows([over_dp, swap(over_dp, "tensor", 1)])
    parts = [over_cores]
    for j in (0, 2):
        for k in range(lax.axis_size("expert")):
            if (j, k) != (0, 0):
                parts.append(swap_pair(over_cores, k, j))
    return parts, over_dp, over_cores


def pieces_of(grad, axis):
    n = lax.axis_size(axis)
    here = lax.axis_index(axis)

    def piece(k):
        return lax.dynamic_index_in_dim(grad, here ^ k, 0, keepdims=False)

    return [piece(0)] + [swap(piece(k), axis, k) for k in range(1, n)]


def local(
    tokens,
    cotangent,
    row_order,
    lengths,
    routes,
    norm_gains,
    w_qkv,
    w_out,
    w_gate_up,
    w_down,
    w_router,
    const_proj,
    const_vec,
):
    layers = w_qkv.shape[0]
    micro_n, rows_n, model = tokens.shape
    routes_n = w_router.shape[2]
    experts_n = lax.axis_size("expert")
    tensor_n = lax.axis_size("tensor")
    dp_n = lax.axis_size("dp")
    capacity = 9 * rows_n // (4 * (experts_n + 4))
    heads_width = w_qkv.shape[3]
    hidden_n = w_down.shape[2]
    seq = tensor_n * rows_n
    each = micro_n * capacity
    half_rows = 2 * experts_n * each
    blocks_n = 4 * experts_n
    arrivals_n = 2 * experts_n
    micro = range(micro_n)
    expert_limit = 12 if half_rows <= 384 else 40
    assert tensor_n == 4 and heads_width == 3 * HDIM and rows_n == 128 and micro_n == 2

    w_qkv = jnp.swapaxes(w_qkv, 2, 3)
    routes = jnp.swapaxes(routes, 2, 3)
    hs = [None] * micro_n
    (hs[0],) = run_kernel(
        functools.partial(norm_kernel, 0),
        [shape_of((rows_n, model), low)],
        [tokens, norm_gains],
        "norm",
        8,
        fetched=2,
    )
    place = jnp.stack([lax.axis_index(a) for a in ("tensor", "expert", "dp")]).astype(jnp.int32)
    cos, sin, bias, router_low, hs[1] = run_kernel(
        functools.partial(tables_kernel, tensor_n),
        [
            shape_of((micro_n, seq, 128), full),
            shape_of((micro_n, seq, 128), full),
            shape_of((micro_n, seq, seq), low),
            shape_of((layers, 384, model), low),
            shape_of((rows_n, model), low),
        ],
        [
            place, lengths, row_order, jnp.transpose(w_router, (2, 0, 1)),
            jnp.swapaxes(const_proj, 1, 2), tokens, norm_gains,
        ],
        "tables",
        12,
        scalars=2,
        fetched=5,
    )

    def attn_fwd(l, blocks):
        def call(m, heads, after):
            results = run_kernel(
                functools.partial(attn_fwd_kernel, l, m, tensor_n),
                [
                    shape_of((rows_n, model), low),
                    shape_of((rows_n, model), low),
                    shape_of((2 * rows_n, model), low),
                    shape_of((seq, 768), low),
                    shape_of((seq, heads_width), low),
                    shape_of((seq, 128), full),
                ],
                [*heads, w_qkv, w_out, cos, sin, bias],
                "attn_fwd",
                12,
                after=after,
            )
            saved, mixed, logsum = results[3:]
            return results, dict(heads=heads, saved=saved, mixed=mixed, logsum=logsum)

        return attend(blocks, call)

    first_gains = []

    def attn_bwd(l, blocks, kept, after):
        def call(m, grads, after_here):
            results = run_kernel(
                functools.partial(attn_bwd_kernel, l, m, tensor_n),
                [
                    shape_of((rows_n, model), low),
                    shape_of((rows_n, model), low),
                    shape_of((2 * rows_n, model), low),
                    shape_of((3, seq, heads_width), low),
                ]
                + [shape_of((8, model), full)] * (l == 0),
                [
                    *grads, w_qkv, w_out, cos, sin, bias, kept[m][l]["saved"],
                    kept[m][l]["logsum"], *([] if l else [*kept[m][l]["heads"], norm_gains]),
                ],
                "attn_bwd",
                12,
                after=[*after_here, *after[m]],
            )
            if not l:
                first_gains.append(results[4])
            return results, [*kept[m][l]["heads"], *grads, results[3], kept[m][l]["mixed"]]

        return attend(blocks, call)

    share = model // (dp_n * experts_n)

    woven = experts_n == 2 and dp_n == 4 and share % 32 == 0

    def attn_weights(ins, after, last):
        if last and woven:
            units = WOVEN
            outs = [shape_of((4 * share // 2, model), low)] * 4
        elif woven:
            units = [[(z, e, 0) for z in turned(dp_n)] for e in (0, 1)]
            outs = [shape_of((dp_n * share, model), low)] * 2
        else:
            units = []
            outs = [shape_of((model, model), low)]
        return run_kernel(
            functools.partial(attn_weights_kernel, tensor_n, micro_n, dp_n, experts_n, units),
            outs,
            [place, *ins],
            "attn_weights",
            12,
            scratch=[pltpu.VMEM((model, model), low)] if units else [],
            scalars=1,
            after=after,
        )

    def attn_sums(parts, after=(), after_last=()):
        if len(parts) == 1:
            grad = parts[0].reshape(dp_n, experts_n, share, model)
            mine = pieces_of(jnp.swapaxes(grad, 0, 1), "expert")
            total = sum(x.astype(full) for x in mine).astype(low)
            return pieces_of(total, "dp")
        one, one_out, two, two_out = parts
        two_in = swap(two_out, "dp", 1)
        one_in = swap(one_out, "expert", 1)
        one, one_out, two, two_out = halves([(one, one_in), (two, two_in)], after)
        one_in = swap(one_out, "dp", 1)
        two_in = swap(two_out, "expert", 1)
        keep, send = run_kernel(
            weave_kernel,
            [shape_of((share, model), low)] * 2,
            [one, one_in, two, two_in],
            "weave",
            8,
            after=after_last,
        )
        return [keep, swap(send, "dp", 2)]

    def expert_weights(blocks, hidden, dgu, apart, after, packed=()):
        unit = model // dp_n + sum(x.shape[0] // (2 * dp_n) for x in packed[:1])
        first = -(-unit // 32) * 16
        sizes = [first, unit - first] if packed else [unit]
        return run_kernel(
            functools.partial(
                expert_weights_kernel, blocks_n, apart, dp_n, bool(packed), len(sizes)
            ),
            [shape_of((dp_n // 2 * n, 3 * hidden_n), low) for n in sizes for _ in range(2)],
            [place, *blocks, hidden, dgu, *packed],
            "expert_weights",
            expert_limit,
            scratch=[pltpu.VMEM((model, 3 * hidden_n), low)],
            scalars=1,
            after=after,
        )

    def halves(pairs, after=()):
        return run_kernel(
            functools.partial(halves_kernel, len(pairs)),
            [
                shape_of((x.shape[0] // 2, x.shape[1]), low)
                for x, _ in pairs
                for _ in range(2)
            ],
            [x for pair in pairs for x in pair],
            "halves",
            12,
            after=after,
        )

    def halve_on(keep, came, after=()):
        bit = 1
        first = None
        while 2 * bit < dp_n:
            keep, send = halves([(keep, came)], after)
            after = ()
            bit *= 2
            first = send if first is None else first
            came = swap(send, "dp", bit)
        return [keep, came], first

    expert_outs = [
        shape_of((2 * half_rows, hidden_n), low),
        shape_of((2 * half_rows, 2 * hidden_n), low),
    ]

    stream = [tokens] * micro_n
    logits = [None] * micro_n
    kept = [[None] * layers for _ in micro]
    for l in range(layers):
        last = l == layers - 1
        kinds = 2 if last else 1
        bufs = []
        for m, (parts, k) in enumerate(attn_fwd(l, hs)):
            mid, h_moe, logits[m], aux, pick, *bufs = run_kernel(
                functools.partial(
                    mid_kernel, l, m, experts_n, routes_n, capacity, last, len(bufs)
                ),
                [
                    shape_of((rows_n, model), full),
                    shape_of((rows_n, model), low),
                    shape_of((rows_n, 128), full),
                    shape_of((rows_n, 128), full),
                    shape_of((experts_n * capacity, 2 * rows_n), low),
                ]
                + [shape_of(((m + 1) * kinds * capacity, model), low)] * experts_n,
                [place, *parts, stream[m], norm_gains, router_low, routes]
                + ([logits[m]] if l else [])
                + ([cotangent] if last else [])
                + bufs,
                "mid",
                12,
                scalars=1,
            )
            kept[m][l] = dict(
                k, mid=mid, h_moe=h_moe, aux=aux, pick=pick, stream=stream[m],
            )
        held = send_rows(bufs)
        if last:
            keep, send, hidden, dgu = run_kernel(
                functools.partial(expert_both_kernel, l, blocks_n),
                [shape_of((kinds * half_rows, model), low)] * 2 + expert_outs,
                [*held, w_gate_up, w_down],
                "expert_both",
                expert_limit,
            )
        else:
            keep, send = run_kernel(
                functools.partial(expert_fwd_kernel, l, blocks_n),
                [shape_of((half_rows, model), low)] * 2,
                [*held, w_gate_up, w_down],
                "expert_fwd",
                expert_limit,
            )
        arrivals, summed = return_rows(keep, send, kinds * each)
        for m in micro:
            kept[m][l]["held"] = held
            kept[m][l]["arrivals"] = arrivals
        if last:
            break
        for m in micro:
            k = kept[m][l]
            stream[m], hs[m] = run_kernel(
                functools.partial(combine_kernel, l, m, experts_n, capacity, arrivals_n),
                [shape_of((rows_n, model), full), shape_of((rows_n, model), low)],
                [
                    *arrivals, k["pick"], k["aux"], k["h_moe"], k["mid"], const_vec, norm_gains,
                ],
                "combine",
                12,
            )

    l = layers - 1
    expert_grads = [None] * layers
    expert_pieces = [None] * layers
    attn_pieces = [None] * layers
    smalls = [[None] * micro_n for _ in range(layers)]
    gains = [None] * (layers - 1)
    expert_grads[l] = expert_weights(held, hidden, dgu, False, [summed])
    expert_pieces[l], first = halve_on(
        expert_grads[l][0], swap(expert_grads[l][1], "dp", 1)
    )
    outputs = []
    dmid = [None] * micro_n
    dattn = [None] * micro_n
    dlogits = [None] * micro_n
    for m in micro:
        k = kept[m][l]
        out, dmid[m], dattn[m], dlogits[m], smalls[l][m] = run_kernel(
            functools.partial(
                turn_kernel, l, m, experts_n, routes_n, capacity, arrivals_n, len(outputs)
            ),
            [
                shape_of((micro_n, rows_n, model), low),
                shape_of((rows_n, model), full),
                shape_of((rows_n, model), low),
                shape_of((rows_n, 128), full),
                shape_of((32, model), full),
            ],
            [
                *arrivals, k["pick"], k["aux"], k["h_moe"], k["mid"], const_vec, norm_gains,
                router_low, cotangent, *outputs,
            ],
            "turn",
            12,
            after=[expert_grads[l][0]],
        )
        outputs = [out]
    (outputs,) = outputs
    before_bwd = [[], [first]]
    attn_in = None
    while True:
        parts = [None] * micro_n
        grads_in = []
        for m, (parts[m], more) in enumerate(attn_bwd(l, dattn, kept, before_bwd)):
            grads_in += more
        attn_in = grads_in
        if l == 0:
            break
        l -= 1
        grad = attn_weights(attn_in, [], False)
        packed = []
        if woven:
            packed = [grad[0], swap(grad[1], "expert", 1)]
        else:
            attn_pieces[l + 1] = attn_sums(grad)
        bufs = []
        dstream = [None] * micro_n
        dlocal = [None] * micro_n
        for m in micro:
            k = kept[m][l]
            dstream[m], dlogits[m], dlocal[m], smalls[l][m], *bufs = run_kernel(
                functools.partial(
                    next_back_kernel, l, m, experts_n, routes_n, capacity, arrivals_n, len(bufs)
                ),
                [
                    shape_of((rows_n, model), full),
                    shape_of((rows_n, 128), full),
                    shape_of((rows_n, model), full),
                    shape_of((32, model), full),
                ]
                + [shape_of(((m + 1) * capacity, model), low)] * experts_n,
                [
                    *k["arrivals"], *parts[m], kept[m][l + 1]["stream"], norm_gains, dmid[m],
                    k["pick"], k["aux"], k["h_moe"], const_vec, router_low, dlogits[m],
                    *bufs,
                ],
                "next_back",
                12,
                after=[] if m else [grad[0]],
            )
        held = kept[0][l]["held"]
        grads = send_rows(bufs)
        keep, send, hidden, dgu = run_kernel(
            functools.partial(expert_bwd_kernel, l, blocks_n),
            [shape_of((half_rows, model), low)] * 2 + expert_outs,
            [*held, *grads, w_gate_up, w_down],
            "expert_bwd",
            expert_limit,
            after=[expert_pieces[l + 1][1], *packed[1:]],
        )
        arrivals, summed = return_rows(keep, send, each)
        expert_grads[l] = expert_weights(
            [*held, *grads], hidden, dgu, True, [], packed
        )
        expert_came = [swap(x, "dp", 1) for x in expert_grads[l][1::2]]
        gains[l] = [None] * micro_n
        for m in micro:
            k = kept[m][l]
            dmid[m], dattn[m], dgain = run_kernel(
                functools.partial(expert_norm_back_kernel, l, m, capacity, arrivals_n),
                [
                    shape_of((rows_n, model), full),
                    shape_of((rows_n, model), low),
                    shape_of((8, model), full),
                ],
                [*arrivals, k["pick"], dlocal[m], k["mid"], norm_gains, dstream[m]],
                "expert_norm_back",
                12,
                after=[expert_grads[l][0]],
            )
            gains[l][m] = dgain
        pieces, first = halve_on(expert_grads[l][0], expert_came[0], [dattn[0]])
        expert_pieces[l] = pieces
        before_bwd = [[first], []]
        if len(expert_came) > 1 and l:
            pieces, first = halve_on(expert_grads[l][2], expert_came[1])
            expert_pieces[l] = expert_pieces[l] + pieces
            before_bwd[1].append(first)

    first = []
    if layers > 1 and len(expert_came) > 1:
        pieces, sent = halve_on(expert_grads[0][2], expert_came[1], [parts[-1][0]])
        expert_pieces[0] = expert_pieces[0] + pieces
        first = [sent]
    each_small = routes_n + 8
    (small,) = run_kernel(
        functools.partial(small_pack_kernel, layers, micro_n, routes_n),
        [shape_of((-(-layers * each_small // 16) * 16, model), low)],
        [x for xs in [*smalls, *gains, first_gains] for x in xs],
        "small_pack",
        8,
    )
    small, over_dp, over_cores = sum_all(small)
    grad = attn_weights(attn_in, first, True)
    attn_pieces[0] = attn_sums(grad, expert_pieces[0][1:2] if first else [], [over_cores])
    (grad_tokens,) = run_kernel(
        functools.partial(input_back_kernel, micro_n),
        [shape_of((micro_n, rows_n, model), full)],
        [x for m in micro for x in (*parts[m], dmid[m])] + [tokens, norm_gains],
        "input_back",
        12,
    )

    attn_gains, moe_gains, grad_router, grad_proj, grad_vec = run_kernel(
        functools.partial(small_out_kernel, layers, routes_n, len(small)),
        [
            shape_of((layers, model), full),
            shape_of((layers, model), full),
            shape_of((routes_n, layers, model), full),
            shape_of((layers, 4, model), full),
            shape_of((layers, 2, model), full),
        ],
        small,
        "small_out",
        8,
    )
    grad_gate_up, grad_down, *packed = run_kernel(
        functools.partial(expert_total_kernel, layers, [len(x) for x in expert_pieces]),
        [
            shape_of((layers, 1, 2, model // dp_n, hidden_n), full),
            shape_of((layers, 1, model // dp_n, hidden_n), full),
        ]
        + [shape_of((share, model), full)] * (layers - 1 if woven else 0),
        [x for pieces in expert_pieces for x in pieces],
        "expert_total",
        12,
        after=[grad[0]],
    )
    if woven:
        attn_pieces[1:] = [[x] for x in packed]
    grad_qkv, grad_out = run_kernel(
        functools.partial(attn_total_kernel, layers, [len(x) for x in attn_pieces]),
        [
            shape_of((layers, 3, share, heads_width), full),
            shape_of((layers, heads_width, share), full),
        ],
        [x for pieces in attn_pieces for x in pieces],
        "attn_total",
        12,
    )
    return (
        outputs,
        grad_tokens,
        attn_gains,
        moe_gains,
        grad_qkv,
        grad_out,
        grad_gate_up,
        jnp.swapaxes(grad_down, 2, 3),
        jnp.transpose(grad_router, (1, 2, 0)),
        jnp.swapaxes(grad_proj, 1, 2),
        grad_vec,
    )


def solution(mesh):
    return jax.shard_map(
        local,
        mesh=mesh,
        in_specs=(
            P(None, ("dp", "expert", "tensor"), None),
            P(None, ("dp", "expert", "tensor"), None),
            P(None, ("dp", "expert"), None),
            P(None, ("dp", "expert"), None),
            P(None, None, ("dp", "expert", "tensor"), None),
            P(),
            P(None, None, None, "tensor"),
            P(None, "tensor", None),
            P(None, "expert", None, None, "tensor"),
            P(None, "expert", "tensor", None),
            P(),
            P(),
            P(),
        ),
        out_specs=(
            P(None, ("dp", "expert", "tensor"), None),
            P(None, ("dp", "expert", "tensor"), None),
            P(),
            P(),
            P(None, None, ("dp", "expert"), "tensor"),
            P(None, "tensor", ("dp", "expert")),
            P(None, "expert", None, "dp", "tensor"),
            P(None, "expert", "tensor", "dp"),
            P(),
            P(),
            P(),
        ),
        check_vma=False,
    )
```

```python
import functools
import math

import jax
import jax.numpy as jnp
from jax import lax
from jax.experimental import pallas as pl
from jax.experimental.pallas import tpu as pltpu
from jax.sharding import PartitionSpec as P

HDIM = 64
epsilon = 1e-06
masked_value = -1e30
highest = lax.Precision.HIGHEST
low = jnp.bfloat16
full = jnp.float32
MIB = 1 << 20


FLOPS_PER_US = 1.1e9
MICROS = {"tables": 3.0}


def shape_of(shape, dtype):
    return jax.ShapeDtypeStruct(shape, dtype)


def run_kernel(body, outs, ins, name, limit, scratch=(), scalars=0, after=(), fetched=0):
    ins = list(ins)
    taken = len(ins)
    for i in range(taken - fetched, taken):
        ins[i] = pltpu.with_memory_space_constraint(ins[i], pltpu.HBM)
    vmem = pl.BlockSpec(memory_space=pltpu.VMEM)
    smem = pl.BlockSpec(memory_space=pltpu.SMEM)
    skip = len(after)

    scratch = list(scratch)
    buffers = [pltpu.VMEM(a.shape, a.dtype) for a in ins[taken - fetched :]] if fetched else []

    def kernel(*refs):
        given = refs[:taken]
        rest = refs[taken + skip :]
        if fetched:
            done = rest[-1]
            inside = rest[-1 - fetched : -1]
            rest = rest[: -1 - fetched]
            copies = [
                pltpu.make_async_copy(a, b, done.at[i])
                for i, (a, b) in enumerate(zip(given[taken - fetched :], inside))
            ]
            for copy in copies:
                copy.start()
            for copy in copies:
                copy.wait()
            given = (*given[: taken - fetched], *inside)
        body(*given, *rest)

    if fetched:
        scratch += [*buffers, pltpu.SemaphoreType.DMA((fetched,))]
    return pl.pallas_call(
        kernel,
        out_shape=tuple(outs),
        in_specs=[smem] * scalars
        + [vmem] * (taken - scalars - fetched)
        + [pl.BlockSpec(memory_space=pltpu.HBM)] * fetched
        + [pl.BlockSpec(memory_space=pl.ANY)] * skip,
        out_specs=tuple([vmem] * len(outs)),
        scratch_shapes=scratch,
        compiler_params=pltpu.CompilerParams(vmem_limit_bytes=limit * MIB),
        cost_estimate=pl.CostEstimate(
            flops=int(MICROS.get(name, 0.0) * FLOPS_PER_US), bytes_accessed=0, transcendentals=0
        ),
        name=name,
    )(*ins, *after)


def dot(a, b):
    return jnp.dot(a, b, preferred_element_type=full)


def dot_nt(a, b):
    return lax.dot_general(a, b, (((1,), (1,)), ((), ())), preferred_element_type=full)


def dot_tn(a, b):
    return lax.dot_general(a, b, (((0,), (0,)), ((), ())), preferred_element_type=full)


def lanes(rows, width=128):
    return lax.broadcasted_iota(jnp.int32, (rows, width), 1)


def sublanes(rows, width=128):
    return lax.broadcasted_iota(jnp.int32, (rows, width), 0)


def join(parts):
    if parts[0].shape[0] % 16:
        return jnp.concatenate([p.astype(full) for p in parts], axis=0).astype(low)
    return jnp.concatenate(parts, axis=0)


def stack_rows(refs, start=0, count=None):
    if count is None or count == refs[0].shape[0]:
        return join([r[...] for r in refs])
    if count % 16 or start % 16:
        return join([r[...].astype(full)[start : start + count].astype(low) for r in refs])
    return join([r[start : start + count, :] for r in refs])


def rms_scale(rows):
    return lax.rsqrt(jnp.mean(rows * rows, axis=-1, keepdims=True) + epsilon)


def split2(rows):
    top = rows.astype(low)
    return top, (rows - top.astype(full)).astype(low)


def as_column(row):
    n = row.shape[1]
    return jnp.sum(jnp.where(sublanes(n, n) == lanes(n, n), row, 0.0), axis=1, keepdims=True)


def norm_kernel(m, tokens, gains, out):
    rows = tokens[m].astype(full)
    out[...] = (rows * rms_scale(rows) * gains[0, 0:1, :]).astype(low)


def tables_kernel(tensor_n, place, lengths, order, w_router, const_proj, tokens, gains, cos, sin, bias, router_low,
                  normed):
    norm_kernel(1, tokens, gains, normed)
    micro_n, _, seq = order.shape
    rows_n = seq // tensor_n
    segments = lengths.shape[2]
    mine = place[0]
    half = HDIM // 2
    lane = lanes(rows_n)
    frequency = jnp.exp((lane % half).astype(full) * (-math.log(10000.0) / half))
    sign = jnp.where(lane % HDIM < half, -1.0, 1.0)
    for m in range(micro_n):
        row = order[m].astype(full)
        cuts = [row[:, j * rows_n : (j + 1) * rows_n] for j in range(tensor_n)]
        blocks = []
        for j in range(tensor_n):
            block = jnp.zeros((1, rows_n), full)
            for i in range(tensor_n):
                block = jnp.where((mine ^ j) == i, cuts[i], block)
            blocks.append(block)
        across = jnp.concatenate(blocks, axis=1)
        starts = []
        total = lengths[m, 0, 0]
        for s in range(1, segments):
            starts.append(total.astype(full))
            total = total + lengths[m, 0, s]
        for j in range(tensor_n):
            part = slice(j * rows_n, (j + 1) * rows_n)
            down = as_column(blocks[j])
            begin = jnp.zeros_like(down)
            for start in starts:
                begin = jnp.where(down >= start, start, begin)
            angle = (down - begin) * frequency
            cos[m, part, :] = jnp.cos(angle)
            sin[m, part, :] = jnp.sin(angle) * sign
            bias[m, part, :] = jnp.where(
                (begin <= across) & (across <= down), 0.0, masked_value
            ).astype(low)
    routes_n, layers, model = w_router.shape
    proj_n = const_proj.shape[1]
    for l in range(layers):
        both = jnp.concatenate(
            [w_router[r, l : l + 1, :] for r in range(routes_n)]
            + [const_proj[l], jnp.zeros((128 - routes_n - proj_n, model), full)],
            axis=0,
        )
        top = both.astype(low)
        rest = both - top.astype(full)
        middle = rest.astype(low)
        router_low[l, 0:128, :] = top
        router_low[l, 128:256, :] = middle
        router_low[l, 256:384, :] = (rest - middle.astype(full)).astype(low)


def swap_halves(rows):
    lane = lanes(rows.shape[0])
    half = HDIM // 2
    return jnp.where(
        lane % HDIM < half, pltpu.roll(rows, 128 - half, 1), pltpu.roll(rows, half, 1)
    )


def half_masks():
    lane = lanes(1)
    return (lane < HDIM).astype(full).astype(low), (lane >= HDIM).astype(full).astype(low)


def attn_fwd_kernel(l, m, blocks, *refs):
    heads = refs[:blocks]
    w, wo, cos, sin, bias, keep, far, send, saved, mixed, logsum = refs[blocks:]
    pair = 2 * HDIM
    h = stack_rows(heads)
    c = cos[m]
    s = sin[m]
    lane = lanes(h.shape[0])

    def turn(chunk):
        return chunk * c + swap_halves(chunk) * s

    q = dot_nt(h, w[l, 0])
    k = dot_nt(h, w[l, 1])
    v = dot_nt(h, w[l, 2])
    saved[:, 0:128] = (turn(q[:, 0:pair]) * 0.125).astype(low)
    saved[:, 128:256] = turn(k[:, 0:pair]).astype(low)
    saved[:, 256:384] = v[:, 0:pair].astype(low)
    third = turn(jnp.concatenate([q[:, pair:], k[:, pair:]], axis=1))
    saved[:, 384:512] = jnp.where(lane < HDIM, third * 0.125, 0.0).astype(low)
    saved[:, 512:640] = jnp.where(lane < HDIM, pltpu.roll(third, HDIM, 1), 0.0).astype(low)
    saved[:, 640:768] = jnp.concatenate(
        [v[:, pair:], jnp.zeros((h.shape[0], HDIM), full)], axis=1
    ).astype(low)
    first, second = half_masks()
    shift = bias[m].astype(full)
    q01 = saved[:, 0:128]
    heads = (
        (q01 * first, slice(128, 256), slice(256, 384)),
        (q01 * second, slice(128, 256), slice(256, 384)),
        (saved[:, 384:512], slice(512, 640), slice(640, 768)),
    )
    scores = [dot_nt(query, saved[:, keys]) + shift for query, keys, _ in heads]
    peaks = [jnp.max(x, axis=-1, keepdims=True) for x in scores]
    powers = [jnp.exp(x - peak) for x, peak in zip(scores, peaks)]
    totals = [jnp.sum(x, axis=-1, keepdims=True) for x in powers]
    results = [
        dot((x * (1.0 / total)).astype(low), saved[:, values])
        for x, total, (_, _, values) in zip(powers, totals, heads)
    ]
    sums = [peak + jnp.log(total) for peak, total in zip(peaks, totals)]
    logsum[...] = jnp.where(lane == 0, sums[0], jnp.where(lane == 1, sums[1], sums[2]))
    mixed[:, 0:pair] = jnp.where(lane < HDIM, results[0], results[1]).astype(low)
    mixed[:, pair : pair + HDIM] = results[2][:, 0:HDIM].astype(low)
    spread(dot(mixed[...], wo[l]).astype(low), keep, far, send)


def spread(value, keep, far, send):
    rows_n = keep.shape[0]
    keep[...] = value[0:rows_n]
    far[...] = value[2 * rows_n : 3 * rows_n]
    send[0:rows_n, :] = value[rows_n : 2 * rows_n]
    send[rows_n : 2 * rows_n, :] = value[3 * rows_n : 4 * rows_n]


def attn_bwd_kernel(l, m, blocks, *refs):
    grads = refs[:blocks]
    w, wo, cos, sin, bias, saved, logsum, *more = refs[blocks:]
    if not l:
        *rows, gains, dgain = more[: blocks + 1] + more[-1:]
        more = more[blocks + 1 : -1]
    keep, far, send, dqkv = more
    pair = 2 * HDIM
    c = cos[m]
    s = sin[m]
    dattn = stack_rows(grads)
    dmix = dot_nt(dattn, wo[l]).astype(low)
    seq = dmix.shape[0]
    d01 = dmix[:, 0:pair]
    d2 = jnp.concatenate([dmix[:, pair:], jnp.zeros((seq, HDIM), low)], axis=1)
    first, second = half_masks()
    q01 = saved[:, 0:128]
    k01 = saved[:, 128:256]
    v01 = saved[:, 256:384]
    q2 = saved[:, 384:512]
    k2 = saved[:, 512:640]
    v2 = saved[:, 640:768]
    heads = (
        (q01 * first, k01 * first, v01, d01 * first),
        (q01 * second, k01 * second, v01, d01 * second),
        (q2, k2, v2, d2),
    )
    shift = bias[m].astype(full)
    dqs, dks, dvs = [], [], []
    for n, (query, keys, values, dout) in enumerate(heads):
        probs = jnp.exp(dot_nt(query, keys) + shift - logsum[:, n : n + 1])
        dprobs = dot_nt(dout, values)
        inner = jnp.sum(probs * dprobs, axis=-1, keepdims=True)
        dscores = (probs * (dprobs - inner)).astype(low)
        dqs.append(dot(dscores, keys))
        dks.append(dot_tn(query, dscores))
        dvs.append(dot_tn(dout, probs.astype(low)))

    dks = [(dks[0] + dks[1]).T, dks[2].T]
    dvs = [(dvs[0] + dvs[1]).T, dvs[2].T]

    def turn_back(chunk):
        return chunk * c - swap_halves(chunk) * s

    third = turn_back(dqs[2] * 0.125 + pltpu.roll(dks[1], HDIM, 1)).astype(low)
    dq = jnp.concatenate([turn_back((dqs[0] + dqs[1]) * 0.125).astype(low), third[:, :HDIM]], axis=1)
    dk = jnp.concatenate([turn_back(dks[0]).astype(low), third[:, HDIM:]], axis=1)
    dv = jnp.concatenate([dvs[0], dvs[1][:, :HDIM]], axis=1).astype(low)
    dqkv[0] = dq
    dqkv[1] = dk
    dqkv[2] = dv
    dh = dot(dq, w[l, 0]) + dot(dk, w[l, 1]) + dot(dv, w[l, 2])
    spread(dh.astype(low), keep, far, send)
    if not l:
        along = jnp.sum(dh * stack_rows(rows).astype(full), axis=0, keepdims=True)
        dgain[...] = jnp.broadcast_to(along / gains[l, 0:1, :], dgain.shape)


def attn_weights_kernel(blocks, micro, dp_n, experts_n, units, *refs):
    place = refs[0]
    total = (2 * blocks + 2) * micro
    outs = refs[1 + total : -1]
    out = refs[-1]
    refs = refs[1 : 1 + total]
    per = 2 * blocks + 2
    pair = 2 * HDIM
    groups = [refs[m * per : (m + 1) * per] for m in range(micro)]
    h = jnp.concatenate([stack_rows(g[:blocks]) for g in groups], axis=0)
    d = jnp.concatenate([stack_rows(g[blocks : 2 * blocks]) for g in groups], axis=0)
    third = []
    for i in range(3):
        part = dot_tn(h, jnp.concatenate([g[2 * blocks][i] for g in groups], axis=0))
        out[:, i * pair : (i + 1) * pair] = part[:, :pair].astype(low)
        third.append(part[:, pair:])
    part = dot_tn(d, jnp.concatenate([g[2 * blocks + 1][...] for g in groups], axis=0))
    out[:, 3 * pair : 4 * pair] = part[:, :pair].astype(low)
    third.append(part[:, pair:])
    out[:, 4 * pair : 5 * pair] = jnp.concatenate(third[0:2], axis=1).astype(low)
    out[:, 5 * pair : 6 * pair] = jnp.concatenate(third[2:4], axis=1).astype(low)
    share = out.shape[0] // (dp_n * experts_n)
    for ref, mine in zip(outs, units):
        rows_n = ref.shape[0] // len(mine)
        for i, (zr, er, part) in enumerate(mine):
            owner = (place[2] ^ zr) * experts_n + (place[1] ^ er)
            at = pl.multiple_of(owner * share + part * rows_n, rows_n)
            ref[i * rows_n : (i + 1) * rows_n, :] = out[pl.ds(at, rows_n), :]


WOVEN = (
    [(z, 0, 0) for z in (0, 2, 1, 3)],
    [(z, 1, 0) for z in (0, 2, 1, 3)],
    [(z, e, 1) for e in (0, 1) for z in (0, 2)],
    [(z, e, 1) for e in (0, 1) for z in (1, 3)],
)


def halves_kernel(pairs, *refs):
    outs = list(refs[2 * pairs :])
    for n in range(pairs):
        one, two = refs[2 * n : 2 * n + 2]
        at = 0
        while at < one.shape[0]:
            out = outs.pop(0)
            rows_n = out.shape[0]
            part = slice(at, at + rows_n)
            out[...] = (one[part, :].astype(full) + two[part, :].astype(full)).astype(low)
            at += rows_n


def weave_kernel(one, one_in, two, two_in, keep, send):
    rows_n = one.shape[0] // 2
    for n, (a, b) in enumerate(((one, one_in), (two, two_in))):
        at = slice(n * rows_n, (n + 1) * rows_n)
        keep[at, :] = (a[0:rows_n, :].astype(full) + b[0:rows_n, :].astype(full)).astype(low)
        send[at, :] = (a[rows_n:, :].astype(full) + b[rows_n:, :].astype(full)).astype(low)


def add_far_kernel(far, arrived, out):
    rows_n = far.shape[0]
    out[...] = (far[...].astype(full) + arrived[rows_n : 2 * rows_n, :].astype(full)).astype(low)


def add_back_kernel(keep, arrived, *outs):
    rows_n = outs[0].shape[0]
    for i, out in enumerate(outs):
        part = slice(i * rows_n, (i + 1) * rows_n)
        out[...] = (keep[part, :].astype(full) + arrived[part, :].astype(full)).astype(low)


def fill_bufs(bufs, earlier, parts, capacity):
    for k, buf in enumerate(bufs):
        pieces = []
        for f, part in enumerate(parts):
            if earlier:
                before = earlier[k][...].astype(full)
                pieces.append(before[f * capacity : (f + 1) * capacity])
            pieces.append(part[k * capacity : (k + 1) * capacity])
        buf[...] = jnp.concatenate(pieces, axis=0).astype(low)


def mid_kernel(l, m, experts_n, routes_n, capacity, last, earlier_n, *refs):
    place, keep, arrived, across, stream, gains, router, routes = refs[:8]
    at = 8
    if l:
        previous = refs[at]
        at += 1
    if last:
        cotangent = refs[at]
        at += 1
    earlier = refs[at : at + earlier_n]
    at += earlier_n
    mid, h_moe, logits_out, aux, pick, *bufs = refs[at:]
    rows_n = keep.shape[0]
    rows = stream[m] if l == 0 else stream[...]
    rows = (
        rows.astype(full)
        + keep[...].astype(full)
        + arrived[0:rows_n, :].astype(full)
        + across[...].astype(full)
    )
    mid[...] = rows
    h = (rows * rms_scale(rows) * gains[l, 1:2, :]).astype(low)
    h_moe[...] = h
    parts = dot_nt(h, router[l])
    raw = parts[:, 0:128] + parts[:, 128:256] + parts[:, 256:384]
    lane = lanes(rows_n)
    logits = raw + previous[...] if l else raw
    logits_out[...] = jnp.where(lane < routes_n, logits, 0.0)
    columns = [as_column(routes[l, m, k : k + 1, :].astype(full)) for k in range(2)]
    picked = [
        jnp.sum(jnp.where(lane.astype(full) == column, logits, 0.0), axis=-1, keepdims=True)
        for column in columns
    ]
    peak = jnp.maximum(picked[0], picked[1])
    gate = [jnp.exp(p - peak) for p in picked]
    both = gate[0] + gate[1]
    gates = [gate[0] / both, gate[1] / both]
    numbers = list(gates)
    for j in range(2):
        two = [raw[:, routes_n + 2 * j + i : routes_n + 2 * j + i + 1] for i in range(2)]
        peak = jnp.maximum(two[0], two[1])
        power = [jnp.exp(p - peak) for p in two]
        both = power[0] + power[1]
        numbers += [power[0] / both, power[1] / both]
    numbers += columns
    value = jnp.zeros((rows_n, 128), full)
    for i, number in enumerate(numbers):
        value = jnp.where(lane == i, number, value)
    aux[...] = value
    here = place[1]
    along = []
    for k in range(2):
        route = routes[l, m, k : k + 1, :]
        along.append(jnp.where(route < experts_n, route ^ here, route).astype(full))
    index_rows = max(16, experts_n)
    expert = sublanes(index_rows, rows_n).astype(full)
    member = ((along[0] == expert) | (along[1] == expert)).astype(full).astype(low)
    before = (sublanes(rows_n, rows_n) < lanes(rows_n, rows_n)).astype(full).astype(low)
    rank = dot(member, before)
    slot = sublanes(capacity, rows_n).astype(full)
    picks = [
        jnp.concatenate(
            [
                ((slot == rank[k : k + 1, :]) & (route == k)).astype(full)
                for k in range(experts_n)
            ],
            axis=0,
        )
        for route in along
    ]
    pick[:, 0:rows_n] = picks[0].astype(low)
    pick[:, rows_n : 2 * rows_n] = picks[1].astype(low)
    sent = [dot((picks[0] + picks[1]).astype(low), h)]
    if last:
        dstream = cotangent[m].astype(full)
        sent.append(
            dot(picks[0].astype(low), (gates[0] * dstream).astype(low))
            + dot(picks[1].astype(low), (gates[1] * dstream).astype(low))
        )
    fill_bufs(bufs, earlier, sent, capacity)


def route_columns(aux):
    return [aux[:, 6 + k : 7 + k] for k in range(2)]


def route_values(experts_n, pick, values_low, aux, columns, h, vec):
    rows_n = h.shape[0]
    twice = jnp.concatenate([pick[...], pick[...]], axis=0)
    both = dot_tn(twice, values_low)
    values = []
    for k in range(2):
        route = columns[k]
        scale = (route == experts_n + 1).astype(full)
        value = both[k * rows_n : (k + 1) * rows_n]
        for j in range(2):
            here = (route == experts_n + 2 + j).astype(full)
            scale = scale + here * aux[:, 2 + 2 * j : 3 + 2 * j]
            value = value + (here * aux[:, 3 + 2 * j : 4 + 2 * j]) * vec[j : j + 1, :]
        values.append(value + scale * h)
    return values


def combine_kernel(l, m, experts_n, capacity, arrivals_n, *refs):
    arrivals = refs[:arrivals_n]
    pick, aux, h_moe, mid, vec, gains, stream, h_next = refs[arrivals_n:]
    columns = route_columns(aux)
    values = route_values(
        experts_n, pick, stack_rows(arrivals, m * capacity, capacity), aux, columns,
        h_moe[...].astype(full), vec[l],
    )
    rows = mid[...] + aux[:, 0:1] * values[0] + aux[:, 1:2] * values[1]
    stream[...] = rows
    h_next[...] = (rows * rms_scale(rows) * gains[l + 1, 0:1, :]).astype(low)


def route_back(
    l, experts_n, routes_n, dstream, values, pick, aux, columns, h_low, vec, router, dnext,
    small,
):
    lane = lanes(dstream.shape[0])
    h = h_low.astype(full)
    gates = [aux[:, k : k + 1] for k in range(2)]
    dgate = [jnp.sum(dstream * v, axis=-1, keepdims=True) for v in values]
    mean = gates[0] * dgate[0] + gates[1] * dgate[1]
    dlogits = dnext
    for k in range(2):
        dlogits = dlogits + jnp.where(lane.astype(full) == columns[k], gates[k] * (dgate[k] - mean), 0.0)

    def gate_of(route):
        return sum((columns[k] == route).astype(full) * gates[k] for k in range(2))

    along_h = jnp.sum(dstream * h, axis=-1, keepdims=True)
    scale = gate_of(experts_n + 1)
    both = dlogits
    for j in range(2):
        share = gate_of(experts_n + 2 + j)
        mix = [aux[:, 2 + 2 * j + i : 3 + 2 * j + i] for i in range(2)]
        along_v = jnp.sum(dstream * vec[l, j : j + 1, :], axis=-1, keepdims=True)
        dm = [share * along_h, share * along_v]
        inner = mix[0] * dm[0] + mix[1] * dm[1]
        for i in range(2):
            both = jnp.where(lane == routes_n + 2 * j + i, mix[i] * (dm[i] - inner), both)
        scale = scale + mix[0] * share
        small[24 + j : 25 + j, :] = jnp.sum((mix[1] * share) * dstream, axis=0, keepdims=True)
    top, rest = split2(both)
    dlocal = scale * dstream + (
        dot(top, router[l, 0:128, :])
        + dot(top, router[l, 128:256, :])
        + dot(rest, router[l, 0:128, :])
    )
    small[0:24, :] = (dot_tn(top, h_low) + dot_tn(rest, h_low))[0:24]
    return dlogits, dlocal


def norm_back(dh, rows, gain):
    scale = rms_scale(rows)
    unit = rows * scale
    dn = dh * gain
    drows = scale * (dn - unit * jnp.mean(dn * unit, axis=-1, keepdims=True))
    return drows, jnp.sum(dh * unit, axis=0, keepdims=True)


def turn_kernel(l, m, experts_n, routes_n, capacity, arrivals_n, earlier_n, *refs):
    arrivals = refs[:arrivals_n]
    pick, aux, h_moe, mid, vec, gains, router, cotangent = refs[
        arrivals_n : arrivals_n + 8
    ]
    at = arrivals_n + 8
    earlier = refs[at : at + earlier_n]
    out, dmid, dattn, dlogits_out, small = refs[at + earlier_n :]
    micro = len(earlier) + 1
    columns = route_columns(aux)
    h_low = h_moe[...]
    values = route_values(
        experts_n, pick, stack_rows(arrivals, m * capacity, capacity), aux, columns,
        h_low.astype(full), vec[l],
    )
    rows = mid[...]
    for i, ref in enumerate(earlier):
        out[i] = ref[i]
    out[m] = (rows + aux[:, 0:1] * values[0] + aux[:, 1:2] * values[1]).astype(low)
    for i in range(m + 1, out.shape[0]):
        out[i] = jnp.zeros(out.shape[1:], low)
    small[24:32, :] = jnp.zeros((8, small.shape[1]), full)
    dstream = cotangent[m].astype(full)
    dlogits, dlocal = route_back(
        l, experts_n, routes_n, dstream, values, pick, aux, columns, h_low, vec, router,
        jnp.zeros((dstream.shape[0], 128), full), small,
    )
    dlogits_out[...] = dlogits
    rows_n = rows.shape[0]
    both = pick[:, 0:rows_n] + pick[:, rows_n : 2 * rows_n]
    twice = jnp.concatenate([both, both], axis=0)
    at = (cotangent.shape[0] + m) * capacity
    dh = dlocal + dot_tn(twice, stack_rows(arrivals, at, capacity))
    drows, dgain = norm_back(dh, rows, gains[l, 1:2, :])
    small[26:27, :] = dgain
    value = dstream + drows
    dmid[...] = value
    dattn[...] = value.astype(low)


def next_back_kernel(l, m, experts_n, routes_n, capacity, arrivals_n, earlier_n, *refs):
    arrivals = refs[:arrivals_n]
    (keep, arrived, across, stream, gains, dmid, pick, aux, h_moe, vec, router,
     dnext) = refs[arrivals_n : arrivals_n + 12]
    at = arrivals_n + 12
    earlier = refs[at : at + earlier_n]
    dstream_out, dlogits_out, dlocal_out, small, *bufs = refs[at + earlier_n :]
    rows_n = keep.shape[0]
    dh = keep[...].astype(full) + arrived[0:rows_n, :].astype(full) + across[...].astype(full)
    drows, dgain = norm_back(dh, stream[...], gains[l + 1, 0:1, :])
    dstream = dmid[...] + drows
    dstream_out[...] = dstream
    small[24:32, :] = jnp.zeros((8, small.shape[1]), full)
    small[27:28, :] = dgain
    columns = route_columns(aux)
    h_low = h_moe[...]
    values = route_values(
        experts_n, pick, stack_rows(arrivals, m * capacity, capacity), aux, columns,
        h_low.astype(full), vec[l],
    )
    gates = [aux[:, k : k + 1] for k in range(2)]
    sent = dot(pick[:, 0:rows_n], (gates[0] * dstream).astype(low)) + dot(
        pick[:, rows_n : 2 * rows_n], (gates[1] * dstream).astype(low)
    )
    fill_bufs(bufs, earlier, [sent], capacity)
    dlogits, dlocal = route_back(
        l, experts_n, routes_n, dstream, values, pick, aux, columns, h_low, vec, router,
        dnext[...], small,
    )
    dlogits_out[...] = dlogits
    dlocal_out[...] = dlocal


def expert_norm_back_kernel(l, m, capacity, arrivals_n, *refs):
    arrivals = refs[:arrivals_n]
    pick, dlocal, mid, gains, dstream, dmid, dattn, dgain_out = refs[arrivals_n:]
    rows_n = mid.shape[0]
    both = pick[:, 0:rows_n] + pick[:, rows_n : 2 * rows_n]
    twice = jnp.concatenate([both, both], axis=0)
    dh = dlocal[...] + dot_tn(twice, stack_rows(arrivals, m * capacity, capacity))
    drows, dgain = norm_back(dh, mid[...], gains[l, 1:2, :])
    dgain_out[...] = jnp.broadcast_to(dgain, dgain_out.shape)
    value = dstream[...] + drows
    dmid[...] = value
    dattn[...] = value.astype(low)


def input_back_kernel(micro, *refs):
    tokens, gains, out = refs[4 * micro :]
    for m in range(micro):
        keep, arrived, across, dmid = refs[4 * m : 4 * m + 4]
        rows_n = keep.shape[0]
        dh = keep[...].astype(full) + arrived[0:rows_n, :].astype(full) + across[...].astype(full)
        drows, _ = norm_back(dh, tokens[m].astype(full), gains[0, 0:1, :])
        out[m] = dmid[...] + drows


def expert_fwd_kernel(l, blocks_n, *refs):
    gate_up, down, keep, send = refs[blocks_n:]
    rows = stack_rows(refs[:blocks_n])
    g = dot(rows, gate_up[l, 0, 0])
    u = dot(rows, gate_up[l, 0, 1])
    hidden = (g * jax.nn.sigmoid(g) * u).astype(low)
    value = dot(hidden, down[l, 0]).astype(low)
    half = keep.shape[0]
    keep[...] = value[0:half]
    send[...] = value[half:]


def expert_back(l, rows, grads, gate_up, down):
    g = dot(rows, gate_up[l, 0, 0])
    u = dot(rows, gate_up[l, 0, 1])
    dhidden = dot_nt(grads, down[l, 0])
    s = jax.nn.sigmoid(g)
    silu = g * s
    hidden = (silu * u).astype(low)
    dg = (dhidden * u * s * (1.0 + g * (1.0 - s))).astype(low)
    du = (dhidden * silu).astype(low)
    drows = (dot_nt(dg, gate_up[l, 0, 0]) + dot_nt(du, gate_up[l, 0, 1])).astype(low)
    return hidden, dg, du, drows


def expert_both_kernel(l, blocks_n, *refs):
    blocks = refs[:blocks_n]
    gate_up, down, keep, send, hidden_out, dgu_out = refs[blocks_n:]
    each = blocks[0].shape[0] // 2
    rows = stack_rows(blocks, 0, each)
    grads = stack_rows(blocks, each, each)
    hidden, dg, du, drows = expert_back(l, rows, grads, gate_up, down)
    hidden_out[...] = hidden
    width = dg.shape[1]
    dgu_out[:, 0:width] = dg
    dgu_out[:, width : 2 * width] = du
    value = dot(hidden, down[l, 0]).astype(low)
    for i in range(blocks_n):
        out = keep if i < blocks_n // 2 else send
        at = 2 * each * (i % (blocks_n // 2))
        out[at : at + each, :] = value[i * each : (i + 1) * each]
        out[at + each : at + 2 * each, :] = drows[i * each : (i + 1) * each]


def expert_bwd_kernel(l, blocks_n, *refs):
    gate_up, down, keep, send, hidden_out, dgu_out = refs[2 * blocks_n :]
    rows = stack_rows(refs[:blocks_n])
    grads = stack_rows(refs[blocks_n : 2 * blocks_n])
    hidden, dg, du, drows = expert_back(l, rows, grads, gate_up, down)
    hidden_out[...] = hidden
    width = dg.shape[1]
    dgu_out[:, 0:width] = dg
    dgu_out[:, width : 2 * width] = du
    half = keep.shape[0]
    keep[...] = drows[0:half]
    send[...] = drows[half:]


def turned(n):
    order = [0]
    bit = n // 2
    while bit:
        order = order + [k + bit for k in order]
        bit //= 2
    bits = n.bit_length() - 1
    return [int(format(i, "b").zfill(bits)[::-1], 2) for i in range(n)]


def expert_weights_kernel(blocks_n, apart, pieces, packed, parts, *refs):
    place = refs[0]
    refs = refs[1:]
    if packed:
        ends = refs[-1 - 2 * parts :]
        one, two = refs[-3 - 2 * parts : -1 - 2 * parts]
        extra = (one[...].astype(full) + two[...].astype(full)).astype(low)
        refs = (*refs[: -3 - 2 * parts], *ends)
    if apart:
        rows = stack_rows(refs[:blocks_n])
        grads = stack_rows(refs[blocks_n : 2 * blocks_n])
    else:
        each = refs[0].shape[0] // 2
        rows = stack_rows(refs[:blocks_n], 0, each)
        grads = stack_rows(refs[:blocks_n], each, each)
    hidden, dgu, *outs, total = refs[-3 - 2 * parts :]
    width = dgu.shape[1]
    total[:, 0:width] = dot_tn(rows, dgu[...]).astype(low)
    total[:, width : width + hidden.shape[1]] = dot_tn(grads, hidden[...]).astype(low)
    share = total.shape[0] // pieces
    for i, k in enumerate(turned(pieces)):
        at = pl.multiple_of((place[2] ^ k) * share, share)
        mine = [total[pl.ds(at, share), :]]
        if packed:
            more = extra.shape[0] // pieces // 2
            mine.append(
                jnp.concatenate(
                    [extra[(2 * i + n) * more : (2 * i + n + 1) * more] for n in range(2)], axis=1
                )
            )
        unit = jnp.concatenate(mine, axis=0)
        begin = 0
        for part in range(parts):
            out = outs[2 * part + 2 * i // pieces]
            rows_n = out.shape[0] // (pieces // 2)
            to = i % (pieces // 2) * rows_n
            out[to : to + rows_n, :] = unit[begin : begin + rows_n]
            begin += rows_n


def expert_total_kernel(layers, counts, *refs):
    gate_up, down, *packed = refs[sum(counts) :]
    width, share = gate_up.shape[4], gate_up.shape[3]
    for l in range(layers):
        mine = refs[sum(counts[:l]) : sum(counts[: l + 1])]
        total = jnp.concatenate(
            [a[...].astype(full) + b[...].astype(full) for a, b in zip(mine[::2], mine[1::2])],
            axis=0,
        )
        for i in range(2):
            gate_up[l, 0, i] = total[0:share, i * width : (i + 1) * width]
        down[l, 0] = total[0:share, 2 * width : 3 * width]
        if packed and l < layers - 1:
            half = packed[l].shape[1]
            packed[l][...] = jnp.concatenate(
                [total[share:, 0:half], total[share:, half : 2 * half]], axis=0
            )


def attn_total_kernel(layers, counts, *refs):
    qkv, out = refs[sum(counts) :]
    pair = 2 * HDIM
    for l in range(layers):
        mine = refs[sum(counts[:l]) : sum(counts[: l + 1])]
        total = mine[0][...].astype(full)
        for ref in mine[1:]:
            total = total + ref[...].astype(full)
        third = total[:, 4 * pair :]
        for i in range(3):
            qkv[l, i, :, 0:pair] = total[:, i * pair : (i + 1) * pair]
            qkv[l, i, :, pair : pair + HDIM] = third[:, i * HDIM : (i + 1) * HDIM]
        out[l, 0:pair, :] = total[:, 3 * pair : 4 * pair].T
        out[l, pair : pair + HDIM, :] = third[:, 3 * HDIM :].T


def swap(x, axis, k):
    n = lax.axis_size(axis)
    return lax.ppermute(x, axis, [(i, i ^ k) for i in range(n)])


def swap_pair(x, k, j):
    experts_n = lax.axis_size("expert")
    tensor_n = lax.axis_size("tensor")
    if j == 0:
        return swap(x, "expert", k)
    if k == 0:
        return swap(x, "tensor", j)
    table = [
        (e * tensor_n + t, (e ^ k) * tensor_n + (t ^ j))
        for e in range(experts_n)
        for t in range(tensor_n)
    ]
    return lax.ppermute(x, ("expert", "tensor"), table)


def attend(blocks, call):
    results = []
    for m, block in enumerate(blocks):
        near = swap(block, "tensor", 1)
        far = swap(block, "tensor", 2)
        pack = [block, near, far, swap(far, "tensor", 1)]
        (keep, away, send, *rest), extra = call(m, pack, [])
        arrived = swap(send, "tensor", 1)
        (total,) = run_kernel(
            add_far_kernel, [shape_of(away.shape, low)], [away, arrived], "add_far", 8
        )
        results.append(([keep, arrived, swap(total, "tensor", 2)], extra))
    return results


def send_rows(bufs):
    experts_n = len(bufs)
    far = [swap_pair(buf, k, 2) for k, buf in enumerate(bufs)]
    near = [bufs[0]] + [swap_pair(bufs[k], k, 0) for k in range(1, experts_n)]
    held = near + far
    return held + [swap(x, "tensor", 1) for x in held]


def return_rows(keep, send, each):
    experts_n = lax.axis_size("expert")
    arrived = swap(send, "tensor", 1)
    sums = run_kernel(
        add_back_kernel,
        [shape_of((each, keep.shape[1]), low)] * (2 * experts_n),
        [keep, arrived],
        "add_back",
        8,
    )
    far = [swap_pair(sums[experts_n + k], k, 2) for k in range(experts_n)]
    near = [sums[0]] + [swap_pair(sums[k], k, 0) for k in range(1, experts_n)]
    return near + far, sums[0]


def small_pack_kernel(layers, micro, routes_n, *refs):
    smalls = [refs[l * micro : (l + 1) * micro] for l in range(layers)]
    at = layers * micro
    gains = [refs[at + l * micro : at + (l + 1) * micro] for l in range(layers - 1)]
    *first_gains, out = refs[at + (layers - 1) * micro :]
    pieces = []
    last_gain = sum(ref[0:1, :] for ref in first_gains)
    for l in range(layers):
        total = smalls[l][0][...]
        for ref in smalls[l][1:]:
            total = total + ref[...]
        if l < layers - 1:
            moe = gains[l][0][0:1, :]
            for ref in gains[l][1:]:
                moe = moe + ref[0:1, :]
        else:
            moe = total[26:27]
        pieces += [total[0 : routes_n + 4], total[24:26], moe, last_gain]
        last_gain = total[27:28]
    rows = sum(p.shape[0] for p in pieces)
    if out.shape[0] > rows:
        pieces.append(jnp.zeros((out.shape[0] - rows, out.shape[1]), full))
    out[...] = jnp.concatenate(pieces, axis=0).astype(low)


def sum_kernel(*refs):
    total = refs[0][...].astype(full)
    for ref in refs[1:-1]:
        total = total + ref[...].astype(full)
    refs[-1][...] = total


def small_out_kernel(layers, routes_n, parts, *refs):
    attn_gains, moe_gains, router, proj, vec = refs[parts:]
    total = refs[0][...]
    for ref in refs[1:parts]:
        total = total + ref[...]
    each = routes_n + 8
    for l in range(layers):
        mine = total[l * each : (l + 1) * each]
        for r in range(routes_n):
            router[r, l : l + 1, :] = mine[r : r + 1]
        proj[l] = mine[routes_n : routes_n + 4]
        vec[l] = mine[routes_n + 4 : routes_n + 6]
        moe_gains[l : l + 1, :] = mine[routes_n + 6 : routes_n + 7]
        attn_gains[l : l + 1, :] = mine[routes_n + 7 : routes_n + 8]


def sum_rows(parts):
    (out,) = run_kernel(sum_kernel, [shape_of(parts[0].shape, full)], parts, "sum", 8)
    return out


def sum_all(rows):
    over_dp = sum_rows([rows] + [swap(rows, "dp", k) for k in range(1, lax.axis_size("dp"))])
    over_cores = sum_rows([over_dp, swap(over_dp, "tensor", 1)])
    parts = [over_cores]
    for j in (0, 2):
        for k in range(lax.axis_size("expert")):
            if (j, k) != (0, 0):
                parts.append(swap_pair(over_cores, k, j))
    return parts, over_dp, over_cores


def pieces_of(grad, axis):
    n = lax.axis_size(axis)
    here = lax.axis_index(axis)

    def piece(k):
        return lax.dynamic_index_in_dim(grad, here ^ k, 0, keepdims=False)

    return [piece(0)] + [swap(piece(k), axis, k) for k in range(1, n)]


def local(
    tokens,
    cotangent,
    row_order,
    lengths,
    routes,
    norm_gains,
    w_qkv,
    w_out,
    w_gate_up,
    w_down,
    w_router,
    const_proj,
    const_vec,
):
    layers = w_qkv.shape[0]
    micro_n, rows_n, model = tokens.shape
    routes_n = w_router.shape[2]
    experts_n = lax.axis_size("expert")
    tensor_n = lax.axis_size("tensor")
    dp_n = lax.axis_size("dp")
    capacity = 9 * rows_n // (4 * (experts_n + 4))
    heads_width = w_qkv.shape[3]
    hidden_n = w_down.shape[2]
    seq = tensor_n * rows_n
    each = micro_n * capacity
    half_rows = 2 * experts_n * each
    blocks_n = 4 * experts_n
    arrivals_n = 2 * experts_n
    micro = range(micro_n)
    expert_limit = 12 if half_rows <= 384 else 40
    assert tensor_n == 4 and heads_width == 3 * HDIM and rows_n == 128 and micro_n == 2

    w_qkv = jnp.swapaxes(w_qkv, 2, 3)
    routes = jnp.swapaxes(routes, 2, 3)
    hs = [None] * micro_n
    (hs[0],) = run_kernel(
        functools.partial(norm_kernel, 0),
        [shape_of((rows_n, model), low)],
        [tokens, norm_gains],
        "norm",
        8,
        fetched=2,
    )
    place = jnp.stack([lax.axis_index(a) for a in ("tensor", "expert", "dp")]).astype(jnp.int32)
    cos, sin, bias, router_low, hs[1] = run_kernel(
        functools.partial(tables_kernel, tensor_n),
        [
            shape_of((micro_n, seq, 128), full),
            shape_of((micro_n, seq, 128), full),
            shape_of((micro_n, seq, seq), low),
            shape_of((layers, 384, model), low),
            shape_of((rows_n, model), low),
        ],
        [
            place, lengths, row_order, jnp.transpose(w_router, (2, 0, 1)),
            jnp.swapaxes(const_proj, 1, 2), tokens, norm_gains,
        ],
        "tables",
        12,
        scalars=2,
        fetched=5,
    )

    def attn_fwd(l, blocks):
        def call(m, heads, after):
            results = run_kernel(
                functools.partial(attn_fwd_kernel, l, m, tensor_n),
                [
                    shape_of((rows_n, model), low),
                    shape_of((rows_n, model), low),
                    shape_of((2 * rows_n, model), low),
                    shape_of((seq, 768), low),
                    shape_of((seq, heads_width), low),
                    shape_of((seq, 128), full),
                ],
                [*heads, w_qkv, w_out, cos, sin, bias],
                "attn_fwd",
                12,
                after=after,
            )
            saved, mixed, logsum = results[3:]
            return results, dict(heads=heads, saved=saved, mixed=mixed, logsum=logsum)

        return attend(blocks, call)

    first_gains = []

    def attn_bwd(l, blocks, kept, after):
        def call(m, grads, after_here):
            results = run_kernel(
                functools.partial(attn_bwd_kernel, l, m, tensor_n),
                [
                    shape_of((rows_n, model), low),
                    shape_of((rows_n, model), low),
                    shape_of((2 * rows_n, model), low),
                    shape_of((3, seq, heads_width), low),
                ]
                + [shape_of((8, model), full)] * (l == 0),
                [
                    *grads, w_qkv, w_out, cos, sin, bias, kept[m][l]["saved"],
                    kept[m][l]["logsum"], *([] if l else [*kept[m][l]["heads"], norm_gains]),
                ],
                "attn_bwd",
                12,
                after=[*after_here, *after[m]],
            )
            if not l:
                first_gains.append(results[4])
            return results, [*kept[m][l]["heads"], *grads, results[3], kept[m][l]["mixed"]]

        return attend(blocks, call)

    share = model // (dp_n * experts_n)

    woven = experts_n == 2 and dp_n == 4 and share % 32 == 0

    def attn_weights(ins, after, last):
        if last and woven:
            units = WOVEN
            outs = [shape_of((4 * share // 2, model), low)] * 4
        elif woven:
            units = [[(z, e, 0) for z in turned(dp_n)] for e in (0, 1)]
            outs = [shape_of((dp_n * share, model), low)] * 2
        else:
            units = []
            outs = [shape_of((model, model), low)]
        return run_kernel(
            functools.partial(attn_weights_kernel, tensor_n, micro_n, dp_n, experts_n, units),
            outs,
            [place, *ins],
            "attn_weights",
            12,
            scratch=[pltpu.VMEM((model, model), low)] if units else [],
            scalars=1,
            after=after,
        )

    def weave(one, one_in, two, two_in, after=()):
        return run_kernel(
            weave_kernel,
            [shape_of(one.shape, low)] * 2,
            [one, one_in, two, two_in],
            "weave",
            12,
            after=after,
        )

    def attn_sums(parts, after=(), after_last=()):
        if len(parts) == 1:
            grad = parts[0].reshape(dp_n, experts_n, share, model)
            mine = pieces_of(jnp.swapaxes(grad, 0, 1), "expert")
            total = sum(x.astype(full) for x in mine).astype(low)
            return pieces_of(total, "dp")
        one, one_out, two, two_out = parts
        two_in = swap(two_out, "dp", 1)
        one_in = swap(one_out, "expert", 1)
        one, one_out, two, two_out = halves([(one, one_in), (two, two_in)], after)
        one_in = swap(one_out, "dp", 1)
        two_in = swap(two_out, "expert", 1)
        keep, send = weave(one, one_in, two, two_in, after_last)
        return [keep, swap(send, "dp", 2)]

    def expert_weights(blocks, hidden, dgu, apart, after, packed=(), split=False):
        unit = model // dp_n + sum(x.shape[0] // (2 * dp_n) for x in packed[:1])
        first = -(-unit // 32) * 16
        sizes = [first, unit - first] if packed or split else [unit]
        return run_kernel(
            functools.partial(
                expert_weights_kernel, blocks_n, apart, dp_n, bool(packed), len(sizes)
            ),
            [shape_of((dp_n // 2 * n, 3 * hidden_n), low) for n in sizes for _ in range(2)],
            [place, *blocks, hidden, dgu, *packed],
            "expert_weights",
            expert_limit,
            scratch=[pltpu.VMEM((model, 3 * hidden_n), low)],
            scalars=1,
            after=after,
        )

    def halves(pairs, after=()):
        return run_kernel(
            functools.partial(halves_kernel, len(pairs)),
            [
                shape_of((x.shape[0] // 2, x.shape[1]), low)
                for x, _ in pairs
                for _ in range(2)
            ],
            [x for pair in pairs for x in pair],
            "halves",
            12,
            after=after,
        )

    def halve_on(keep, came, after=()):
        bit = 1
        first = None
        while 2 * bit < dp_n:
            keep, send = halves([(keep, came)], after)
            after = ()
            bit *= 2
            first = send if first is None else first
            came = swap(send, "dp", bit)
        return [keep, came], first

    expert_outs = [
        shape_of((2 * half_rows, hidden_n), low),
        shape_of((2 * half_rows, 2 * hidden_n), low),
    ]

    stream = [tokens] * micro_n
    logits = [None] * micro_n
    kept = [[None] * layers for _ in micro]
    for l in range(layers):
        last = l == layers - 1
        kinds = 2 if last else 1
        bufs = []
        for m, (parts, k) in enumerate(attn_fwd(l, hs)):
            mid, h_moe, logits[m], aux, pick, *bufs = run_kernel(
                functools.partial(
                    mid_kernel, l, m, experts_n, routes_n, capacity, last, len(bufs)
                ),
                [
                    shape_of((rows_n, model), full),
                    shape_of((rows_n, model), low),
                    shape_of((rows_n, 128), full),
                    shape_of((rows_n, 128), full),
                    shape_of((experts_n * capacity, 2 * rows_n), low),
                ]
                + [shape_of(((m + 1) * kinds * capacity, model), low)] * experts_n,
                [place, *parts, stream[m], norm_gains, router_low, routes]
                + ([logits[m]] if l else [])
                + ([cotangent] if last else [])
                + bufs,
                "mid",
                12,
                scalars=1,
            )
            kept[m][l] = dict(
                k, mid=mid, h_moe=h_moe, aux=aux, pick=pick, stream=stream[m],
            )
        held = send_rows(bufs)
        if last:
            keep, send, hidden, dgu = run_kernel(
                functools.partial(expert_both_kernel, l, blocks_n),
                [shape_of((kinds * half_rows, model), low)] * 2 + expert_outs,
                [*held, w_gate_up, w_down],
                "expert_both",
                expert_limit,
            )
        else:
            keep, send = run_kernel(
                functools.partial(expert_fwd_kernel, l, blocks_n),
                [shape_of((half_rows, model), low)] * 2,
                [*held, w_gate_up, w_down],
                "expert_fwd",
                expert_limit,
            )
        arrivals, summed = return_rows(keep, send, kinds * each)
        for m in micro:
            kept[m][l]["held"] = held
            kept[m][l]["arrivals"] = arrivals
        if last:
            break
        for m in micro:
            k = kept[m][l]
            stream[m], hs[m] = run_kernel(
                functools.partial(combine_kernel, l, m, experts_n, capacity, arrivals_n),
                [shape_of((rows_n, model), full), shape_of((rows_n, model), low)],
                [
                    *arrivals, k["pick"], k["aux"], k["h_moe"], k["mid"], const_vec, norm_gains,
                ],
                "combine",
                12,
            )

    l = layers - 1
    expert_grads = [None] * layers
    expert_pieces = [None] * layers
    attn_pieces = [None] * layers
    smalls = [[None] * micro_n for _ in range(layers)]
    gains = [None] * (layers - 1)
    expert_grads[l] = expert_weights(held, hidden, dgu, False, [], split=woven)
    if woven:
        one, one_out, two, two_out = expert_grads[l]
        keep, first = weave(one, swap(one_out, "dp", 1), two, swap(two_out, "dp", 1))
        expert_pieces[l] = [keep, swap(first, "dp", 2)]
    else:
        expert_pieces[l], first = halve_on(
            expert_grads[l][0], swap(expert_grads[l][1], "dp", 1)
        )
    outputs = []
    dmid = [None] * micro_n
    dattn = [None] * micro_n
    dlogits = [None] * micro_n
    for m in micro:
        k = kept[m][l]
        out, dmid[m], dattn[m], dlogits[m], smalls[l][m] = run_kernel(
            functools.partial(
                turn_kernel, l, m, experts_n, routes_n, capacity, arrivals_n, len(outputs)
            ),
            [
                shape_of((micro_n, rows_n, model), low),
                shape_of((rows_n, model), full),
                shape_of((rows_n, model), low),
                shape_of((rows_n, 128), full),
                shape_of((32, model), full),
            ],
            [
                *arrivals, k["pick"], k["aux"], k["h_moe"], k["mid"], const_vec, norm_gains,
                router_low, cotangent, *outputs,
            ],
            "turn",
            12,
            after=[expert_grads[l][0]],
        )
        outputs = [out]
    (outputs,) = outputs
    before_bwd = [[], [first]]
    attn_in = None
    while True:
        parts = [None] * micro_n
        grads_in = []
        for m, (parts[m], more) in enumerate(attn_bwd(l, dattn, kept, before_bwd)):
            grads_in += more
        attn_in = grads_in
        if l == 0:
            break
        l -= 1
        grad = attn_weights(attn_in, [], False)
        packed = []
        if woven:
            packed = [grad[0], swap(grad[1], "expert", 1)]
        else:
            attn_pieces[l + 1] = attn_sums(grad)
        bufs = []
        dstream = [None] * micro_n
        dlocal = [None] * micro_n
        for m in micro:
            k = kept[m][l]
            dstream[m], dlogits[m], dlocal[m], smalls[l][m], *bufs = run_kernel(
                functools.partial(
                    next_back_kernel, l, m, experts_n, routes_n, capacity, arrivals_n, len(bufs)
                ),
                [
                    shape_of((rows_n, model), full),
                    shape_of((rows_n, 128), full),
                    shape_of((rows_n, model), full),
                    shape_of((32, model), full),
                ]
                + [shape_of(((m + 1) * capacity, model), low)] * experts_n,
                [
                    *k["arrivals"], *parts[m], kept[m][l + 1]["stream"], norm_gains, dmid[m],
                    k["pick"], k["aux"], k["h_moe"], const_vec, router_low, dlogits[m],
                    *bufs,
                ],
                "next_back",
                12,
                after=[] if m else [grad[0]],
            )
        held = kept[0][l]["held"]
        grads = send_rows(bufs)
        keep, send, hidden, dgu = run_kernel(
            functools.partial(expert_bwd_kernel, l, blocks_n),
            [shape_of((half_rows, model), low)] * 2 + expert_outs,
            [*held, *grads, w_gate_up, w_down],
            "expert_bwd",
            expert_limit,
            after=[expert_pieces[l + 1][1], *packed[1:]],
        )
        arrivals, summed = return_rows(keep, send, each)
        expert_grads[l] = expert_weights(
            [*held, *grads], hidden, dgu, True, [], packed
        )
        expert_came = [swap(x, "dp", 1) for x in expert_grads[l][1::2]]
        gains[l] = [None] * micro_n
        for m in micro:
            k = kept[m][l]
            dmid[m], dattn[m], dgain = run_kernel(
                functools.partial(expert_norm_back_kernel, l, m, capacity, arrivals_n),
                [
                    shape_of((rows_n, model), full),
                    shape_of((rows_n, model), low),
                    shape_of((8, model), full),
                ],
                [*arrivals, k["pick"], dlocal[m], k["mid"], norm_gains, dstream[m]],
                "expert_norm_back",
                12,
                after=[expert_grads[l][0]],
            )
            gains[l][m] = dgain
        pieces, first = halve_on(expert_grads[l][0], expert_came[0], [dattn[0]])
        expert_pieces[l] = pieces
        before_bwd = [[first], []]
        if len(expert_came) > 1 and l:
            pieces, first = halve_on(expert_grads[l][2], expert_came[1])
            expert_pieces[l] = expert_pieces[l] + pieces
            before_bwd[1].append(first)

    first = []
    if layers > 1 and len(expert_came) > 1:
        pieces, sent = halve_on(expert_grads[0][2], expert_came[1], [parts[-1][0]])
        expert_pieces[0] = expert_pieces[0] + pieces
        first = [sent]
    each_small = routes_n + 8
    (small,) = run_kernel(
        functools.partial(small_pack_kernel, layers, micro_n, routes_n),
        [shape_of((-(-layers * each_small // 16) * 16, model), low)],
        [x for xs in [*smalls, *gains, first_gains] for x in xs],
        "small_pack",
        8,
    )
    small, over_dp, over_cores = sum_all(small)
    grad = attn_weights(attn_in, first, True)
    attn_pieces[0] = attn_sums(grad, expert_pieces[0][1:2] if first else [], [over_cores])
    (grad_tokens,) = run_kernel(
        functools.partial(input_back_kernel, micro_n),
        [shape_of((micro_n, rows_n, model), full)],
        [x for m in micro for x in (*parts[m], dmid[m])] + [tokens, norm_gains],
        "input_back",
        12,
    )

    attn_gains, moe_gains, grad_router, grad_proj, grad_vec = run_kernel(
        functools.partial(small_out_kernel, layers, routes_n, len(small)),
        [
            shape_of((layers, model), full),
            shape_of((layers, model), full),
            shape_of((routes_n, layers, model), full),
            shape_of((layers, 4, model), full),
            shape_of((layers, 2, model), full),
        ],
        small,
        "small_out",
        8,
    )
    grad_gate_up, grad_down, *packed = run_kernel(
        functools.partial(expert_total_kernel, layers, [len(x) for x in expert_pieces]),
        [
            shape_of((layers, 1, 2, model // dp_n, hidden_n), full),
            shape_of((layers, 1, model // dp_n, hidden_n), full),
        ]
        + [shape_of((share, model), full)] * (layers - 1 if woven else 0),
        [x for pieces in expert_pieces for x in pieces],
        "expert_total",
        12,
        after=[grad[0]],
    )
    if woven:
        attn_pieces[1:] = [[x] for x in packed]
    grad_qkv, grad_out = run_kernel(
        functools.partial(attn_total_kernel, layers, [len(x) for x in attn_pieces]),
        [
            shape_of((layers, 3, share, heads_width), full),
            shape_of((layers, heads_width, share), full),
        ],
        [x for pieces in attn_pieces for x in pieces],
        "attn_total",
        12,
    )
    return (
        outputs,
        grad_tokens,
        attn_gains,
        moe_gains,
        grad_qkv,
        grad_out,
        grad_gate_up,
        jnp.swapaxes(grad_down, 2, 3),
        jnp.transpose(grad_router, (1, 2, 0)),
        jnp.swapaxes(grad_proj, 1, 2),
        grad_vec,
    )


def solution(mesh):
    return jax.shard_map(
        local,
        mesh=mesh,
        in_specs=(
            P(None, ("dp", "expert", "tensor"), None),
            P(None, ("dp", "expert", "tensor"), None),
            P(None, ("dp", "expert"), None),
            P(None, ("dp", "expert"), None),
            P(None, None, ("dp", "expert", "tensor"), None),
            P(),
            P(None, None, None, "tensor"),
            P(None, "tensor", None),
            P(None, "expert", None, None, "tensor"),
            P(None, "expert", "tensor", None),
            P(),
            P(),
            P(),
        ),
        out_specs=(
            P(None, ("dp", "expert", "tensor"), None),
            P(None, ("dp", "expert", "tensor"), None),
            P(),
            P(),
            P(None, None, ("dp", "expert"), "tensor"),
            P(None, "tensor", ("dp", "expert")),
            P(None, "expert", None, "dp", "tensor"),
            P(None, "expert", "tensor", "dp"),
            P(),
            P(),
            P(),
        ),
        check_vma=False,
    )
```

```python
import functools
import math

import jax
import jax.numpy as jnp
from jax import lax
from jax.experimental import pallas as pl
from jax.experimental.pallas import tpu as pltpu
from jax.sharding import PartitionSpec as P

HDIM = 64
epsilon = 1e-06
masked_value = -1e30
highest = lax.Precision.HIGHEST
low = jnp.bfloat16
full = jnp.float32
MIB = 1 << 20


FLOPS_PER_US = 1.1e9
MICROS = {"tables": 3.0}


def shape_of(shape, dtype):
    return jax.ShapeDtypeStruct(shape, dtype)


def run_kernel(body, outs, ins, name, limit, scratch=(), scalars=0, after=(), fetched=0):
    ins = list(ins)
    taken = len(ins)
    for i in range(taken - fetched, taken):
        ins[i] = pltpu.with_memory_space_constraint(ins[i], pltpu.HBM)
    vmem = pl.BlockSpec(memory_space=pltpu.VMEM)
    smem = pl.BlockSpec(memory_space=pltpu.SMEM)
    skip = len(after)

    scratch = list(scratch)
    buffers = [pltpu.VMEM(a.shape, a.dtype) for a in ins[taken - fetched :]] if fetched else []

    def kernel(*refs):
        given = refs[:taken]
        rest = refs[taken + skip :]
        if fetched:
            done = rest[-1]
            inside = rest[-1 - fetched : -1]
            rest = rest[: -1 - fetched]
            copies = [
                pltpu.make_async_copy(a, b, done.at[i])
                for i, (a, b) in enumerate(zip(given[taken - fetched :], inside))
            ]
            for copy in copies:
                copy.start()
            for copy in copies:
                copy.wait()
            given = (*given[: taken - fetched], *inside)
        body(*given, *rest)

    if fetched:
        scratch += [*buffers, pltpu.SemaphoreType.DMA((fetched,))]
    return pl.pallas_call(
        kernel,
        out_shape=tuple(outs),
        in_specs=[smem] * scalars
        + [vmem] * (taken - scalars - fetched)
        + [pl.BlockSpec(memory_space=pltpu.HBM)] * fetched
        + [pl.BlockSpec(memory_space=pl.ANY)] * skip,
        out_specs=tuple([vmem] * len(outs)),
        scratch_shapes=scratch,
        compiler_params=pltpu.CompilerParams(vmem_limit_bytes=limit * MIB),
        cost_estimate=pl.CostEstimate(
            flops=int(MICROS.get(name, 0.0) * FLOPS_PER_US), bytes_accessed=0, transcendentals=0
        ),
        name=name,
    )(*ins, *after)


def dot(a, b):
    return jnp.dot(a, b, preferred_element_type=full)


def dot_nt(a, b):
    return lax.dot_general(a, b, (((1,), (1,)), ((), ())), preferred_element_type=full)


def dot_tn(a, b):
    return lax.dot_general(a, b, (((0,), (0,)), ((), ())), preferred_element_type=full)


def lanes(rows, width=128):
    return lax.broadcasted_iota(jnp.int32, (rows, width), 1)


def sublanes(rows, width=128):
    return lax.broadcasted_iota(jnp.int32, (rows, width), 0)


def join(parts):
    if parts[0].shape[0] % 16:
        return jnp.concatenate([p.astype(full) for p in parts], axis=0).astype(low)
    return jnp.concatenate(parts, axis=0)


def stack_rows(refs, start=0, count=None):
    if count is None or count == refs[0].shape[0]:
        return join([r[...] for r in refs])
    if count % 16 or start % 16:
        return join([r[...].astype(full)[start : start + count].astype(low) for r in refs])
    return join([r[start : start + count, :] for r in refs])


def rms_scale(rows):
    return lax.rsqrt(jnp.mean(rows * rows, axis=-1, keepdims=True) + epsilon)


def split2(rows):
    top = rows.astype(low)
    return top, (rows - top.astype(full)).astype(low)


def as_column(row):
    n = row.shape[1]
    return jnp.sum(jnp.where(sublanes(n, n) == lanes(n, n), row, 0.0), axis=1, keepdims=True)


def norm_kernel(tokens, gains, *outs):
    for m, out in enumerate(outs):
        rows = tokens[m].astype(full)
        out[...] = (rows * rms_scale(rows) * gains[0, 0:1, :]).astype(low)


def tables_kernel(tensor_n, place, lengths, again, order, w_router, const_proj, cos, sin, bias, router_low,
                  normed):
    normed[...] = again[...]
    micro_n, _, seq = order.shape
    rows_n = seq // tensor_n
    segments = lengths.shape[2]
    mine = place[0]
    half = HDIM // 2
    lane = lanes(rows_n)
    frequency = jnp.exp((lane % half).astype(full) * (-math.log(10000.0) / half))
    sign = jnp.where(lane % HDIM < half, -1.0, 1.0)
    for m in range(micro_n):
        row = order[m].astype(full)
        cuts = [row[:, j * rows_n : (j + 1) * rows_n] for j in range(tensor_n)]
        blocks = []
        for j in range(tensor_n):
            block = jnp.zeros((1, rows_n), full)
            for i in range(tensor_n):
                block = jnp.where((mine ^ j) == i, cuts[i], block)
            blocks.append(block)
        across = jnp.concatenate(blocks, axis=1)
        starts = []
        total = lengths[m, 0, 0]
        for s in range(1, segments):
            starts.append(total.astype(full))
            total = total + lengths[m, 0, s]
        for j in range(tensor_n):
            part = slice(j * rows_n, (j + 1) * rows_n)
            down = as_column(blocks[j])
            begin = jnp.zeros_like(down)
            for start in starts:
                begin = jnp.where(down >= start, start, begin)
            angle = (down - begin) * frequency
            cos[m, part, :] = jnp.cos(angle)
            sin[m, part, :] = jnp.sin(angle) * sign
            bias[m, part, :] = jnp.where(
                (begin <= across) & (across <= down), 0.0, masked_value
            ).astype(low)
    routes_n, layers, model = w_router.shape
    proj_n = const_proj.shape[1]
    for l in range(layers):
        both = jnp.concatenate(
            [w_router[r, l : l + 1, :] for r in range(routes_n)]
            + [const_proj[l], jnp.zeros((128 - routes_n - proj_n, model), full)],
            axis=0,
        )
        top = both.astype(low)
        rest = both - top.astype(full)
        middle = rest.astype(low)
        router_low[l, 0:128, :] = top
        router_low[l, 128:256, :] = middle
        router_low[l, 256:384, :] = (rest - middle.astype(full)).astype(low)


def swap_halves(rows):
    lane = lanes(rows.shape[0])
    half = HDIM // 2
    return jnp.where(
        lane % HDIM < half, pltpu.roll(rows, 128 - half, 1), pltpu.roll(rows, half, 1)
    )


def half_masks():
    lane = lanes(1)
    return (lane < HDIM).astype(full).astype(low), (lane >= HDIM).astype(full).astype(low)


def attn_fwd_kernel(l, m, blocks, *refs):
    heads = refs[:blocks]
    w, wo, cos, sin, bias, keep, far, send, saved, mixed, logsum = refs[blocks:]
    pair = 2 * HDIM
    h = stack_rows(heads)
    c = cos[m]
    s = sin[m]
    lane = lanes(h.shape[0])

    def turn(chunk):
        return chunk * c + swap_halves(chunk) * s

    q = dot_nt(h, w[l, 0])
    k = dot_nt(h, w[l, 1])
    v = dot_nt(h, w[l, 2])
    saved[:, 0:128] = (turn(q[:, 0:pair]) * 0.125).astype(low)
    saved[:, 128:256] = turn(k[:, 0:pair]).astype(low)
    saved[:, 256:384] = v[:, 0:pair].astype(low)
    third = turn(jnp.concatenate([q[:, pair:], k[:, pair:]], axis=1))
    saved[:, 384:512] = jnp.where(lane < HDIM, third * 0.125, 0.0).astype(low)
    saved[:, 512:640] = jnp.where(lane < HDIM, pltpu.roll(third, HDIM, 1), 0.0).astype(low)
    saved[:, 640:768] = jnp.concatenate(
        [v[:, pair:], jnp.zeros((h.shape[0], HDIM), full)], axis=1
    ).astype(low)
    first, second = half_masks()
    shift = bias[m].astype(full)
    q01 = saved[:, 0:128]
    heads = (
        (q01 * first, slice(128, 256), slice(256, 384)),
        (q01 * second, slice(128, 256), slice(256, 384)),
        (saved[:, 384:512], slice(512, 640), slice(640, 768)),
    )
    scores = [dot_nt(query, saved[:, keys]) + shift for query, keys, _ in heads]
    peaks = [jnp.max(x, axis=-1, keepdims=True) for x in scores]
    powers = [jnp.exp(x - peak) for x, peak in zip(scores, peaks)]
    totals = [jnp.sum(x, axis=-1, keepdims=True) for x in powers]
    results = [
        dot((x * (1.0 / total)).astype(low), saved[:, values])
        for x, total, (_, _, values) in zip(powers, totals, heads)
    ]
    sums = [peak + jnp.log(total) for peak, total in zip(peaks, totals)]
    logsum[...] = jnp.where(lane == 0, sums[0], jnp.where(lane == 1, sums[1], sums[2]))
    mixed[:, 0:pair] = jnp.where(lane < HDIM, results[0], results[1]).astype(low)
    mixed[:, pair : pair + HDIM] = results[2][:, 0:HDIM].astype(low)
    spread(dot(mixed[...], wo[l]).astype(low), keep, far, send)


def spread(value, keep, far, send):
    rows_n = keep.shape[0]
    keep[...] = value[0:rows_n]
    far[...] = value[2 * rows_n : 3 * rows_n]
    send[0:rows_n, :] = value[rows_n : 2 * rows_n]
    send[rows_n : 2 * rows_n, :] = value[3 * rows_n : 4 * rows_n]


def attn_bwd_kernel(l, m, blocks, *refs):
    grads = refs[:blocks]
    w, wo, cos, sin, bias, saved, logsum, *more = refs[blocks:]
    if not l:
        *rows, gains, dgain = more[: blocks + 1] + more[-1:]
        more = more[blocks + 1 : -1]
    keep, far, send, dqkv = more
    pair = 2 * HDIM
    c = cos[m]
    s = sin[m]
    dattn = stack_rows(grads)
    dmix = dot_nt(dattn, wo[l]).astype(low)
    seq = dmix.shape[0]
    d01 = dmix[:, 0:pair]
    d2 = jnp.concatenate([dmix[:, pair:], jnp.zeros((seq, HDIM), low)], axis=1)
    first, second = half_masks()
    q01 = saved[:, 0:128]
    k01 = saved[:, 128:256]
    v01 = saved[:, 256:384]
    q2 = saved[:, 384:512]
    k2 = saved[:, 512:640]
    v2 = saved[:, 640:768]
    heads = (
        (q01 * first, k01 * first, v01, d01 * first),
        (q01 * second, k01 * second, v01, d01 * second),
        (q2, k2, v2, d2),
    )
    shift = bias[m].astype(full)
    dqs, dks, dvs = [], [], []
    for n, (query, keys, values, dout) in enumerate(heads):
        probs = jnp.exp(dot_nt(query, keys) + shift - logsum[:, n : n + 1])
        dprobs = dot_nt(dout, values)
        inner = jnp.sum(probs * dprobs, axis=-1, keepdims=True)
        dscores = (probs * (dprobs - inner)).astype(low)
        dqs.append(dot(dscores, keys))
        dks.append(dot_tn(query, dscores))
        dvs.append(dot_tn(dout, probs.astype(low)))

    dks = [(dks[0] + dks[1]).T, dks[2].T]
    dvs = [(dvs[0] + dvs[1]).T, dvs[2].T]

    def turn_back(chunk):
        return chunk * c - swap_halves(chunk) * s

    third = turn_back(dqs[2] * 0.125 + pltpu.roll(dks[1], HDIM, 1)).astype(low)
    dq = jnp.concatenate([turn_back((dqs[0] + dqs[1]) * 0.125).astype(low), third[:, :HDIM]], axis=1)
    dk = jnp.concatenate([turn_back(dks[0]).astype(low), third[:, HDIM:]], axis=1)
    dv = jnp.concatenate([dvs[0], dvs[1][:, :HDIM]], axis=1).astype(low)
    dqkv[0] = dq
    dqkv[1] = dk
    dqkv[2] = dv
    dh = dot(dq, w[l, 0]) + dot(dk, w[l, 1]) + dot(dv, w[l, 2])
    spread(dh.astype(low), keep, far, send)
    if not l:
        along = jnp.sum(dh * stack_rows(rows).astype(full), axis=0, keepdims=True)
        dgain[...] = jnp.broadcast_to(along / gains[l, 0:1, :], dgain.shape)


def attn_weights_kernel(blocks, micro, dp_n, experts_n, units, *refs):
    place = refs[0]
    total = (2 * blocks + 2) * micro
    outs = refs[1 + total : -1]
    out = refs[-1]
    refs = refs[1 : 1 + total]
    per = 2 * blocks + 2
    pair = 2 * HDIM
    groups = [refs[m * per : (m + 1) * per] for m in range(micro)]
    h = jnp.concatenate([stack_rows(g[:blocks]) for g in groups], axis=0)
    d = jnp.concatenate([stack_rows(g[blocks : 2 * blocks]) for g in groups], axis=0)
    third = []
    for i in range(3):
        part = dot_tn(h, jnp.concatenate([g[2 * blocks][i] for g in groups], axis=0))
        out[:, i * pair : (i + 1) * pair] = part[:, :pair].astype(low)
        third.append(part[:, pair:])
    part = dot_tn(d, jnp.concatenate([g[2 * blocks + 1][...] for g in groups], axis=0))
    out[:, 3 * pair : 4 * pair] = part[:, :pair].astype(low)
    third.append(part[:, pair:])
    out[:, 4 * pair : 5 * pair] = jnp.concatenate(third[0:2], axis=1).astype(low)
    out[:, 5 * pair : 6 * pair] = jnp.concatenate(third[2:4], axis=1).astype(low)
    share = out.shape[0] // (dp_n * experts_n)
    for ref, mine in zip(outs, units):
        rows_n = ref.shape[0] // len(mine)
        for i, (zr, er, part) in enumerate(mine):
            owner = (place[2] ^ zr) * experts_n + (place[1] ^ er)
            at = pl.multiple_of(owner * share + part * rows_n, rows_n)
            ref[i * rows_n : (i + 1) * rows_n, :] = out[pl.ds(at, rows_n), :]


WOVEN = (
    [(z, 0, 0) for z in (0, 2, 1, 3)],
    [(z, 1, 0) for z in (0, 2, 1, 3)],
    [(z, e, 1) for e in (0, 1) for z in (0, 2)],
    [(z, e, 1) for e in (0, 1) for z in (1, 3)],
)


def halves_kernel(pairs, *refs):
    outs = list(refs[2 * pairs :])
    for n in range(pairs):
        one, two = refs[2 * n : 2 * n + 2]
        at = 0
        while at < one.shape[0]:
            out = outs.pop(0)
            rows_n = out.shape[0]
            part = slice(at, at + rows_n)
            out[...] = (one[part, :].astype(full) + two[part, :].astype(full)).astype(low)
            at += rows_n


def weave_kernel(one, one_in, two, two_in, keep, send):
    rows_n = one.shape[0] // 2
    for n, (a, b) in enumerate(((one, one_in), (two, two_in))):
        at = slice(n * rows_n, (n + 1) * rows_n)
        keep[at, :] = (a[0:rows_n, :].astype(full) + b[0:rows_n, :].astype(full)).astype(low)
        send[at, :] = (a[rows_n:, :].astype(full) + b[rows_n:, :].astype(full)).astype(low)


def add_far_kernel(far, arrived, out):
    rows_n = far.shape[0]
    out[...] = (far[...].astype(full) + arrived[rows_n : 2 * rows_n, :].astype(full)).astype(low)


def add_back_kernel(keep, arrived, *outs):
    rows_n = outs[0].shape[0]
    for i, out in enumerate(outs):
        part = slice(i * rows_n, (i + 1) * rows_n)
        out[...] = (keep[part, :].astype(full) + arrived[part, :].astype(full)).astype(low)


def fill_bufs(bufs, earlier, parts, capacity):
    for k, buf in enumerate(bufs):
        pieces = []
        for f, part in enumerate(parts):
            if earlier:
                before = earlier[k][...].astype(full)
                pieces.append(before[f * capacity : (f + 1) * capacity])
            pieces.append(part[k * capacity : (k + 1) * capacity])
        buf[...] = jnp.concatenate(pieces, axis=0).astype(low)


def mid_kernel(l, m, experts_n, routes_n, capacity, last, earlier_n, *refs):
    place, keep, arrived, across, stream, gains, router, routes = refs[:8]
    at = 8
    if l:
        previous = refs[at]
        at += 1
    if last:
        cotangent = refs[at]
        at += 1
    earlier = refs[at : at + earlier_n]
    at += earlier_n
    mid, h_moe, logits_out, aux, pick, *bufs = refs[at:]
    rows_n = keep.shape[0]
    rows = stream[m] if l == 0 else stream[...]
    rows = (
        rows.astype(full)
        + keep[...].astype(full)
        + arrived[0:rows_n, :].astype(full)
        + across[...].astype(full)
    )
    mid[...] = rows
    h = (rows * rms_scale(rows) * gains[l, 1:2, :]).astype(low)
    h_moe[...] = h
    parts = dot_nt(h, router[l])
    raw = parts[:, 0:128] + parts[:, 128:256] + parts[:, 256:384]
    lane = lanes(rows_n)
    logits = raw + previous[...] if l else raw
    logits_out[...] = jnp.where(lane < routes_n, logits, 0.0)
    columns = [as_column(routes[l, m, k : k + 1, :].astype(full)) for k in range(2)]
    picked = [
        jnp.sum(jnp.where(lane.astype(full) == column, logits, 0.0), axis=-1, keepdims=True)
        for column in columns
    ]
    peak = jnp.maximum(picked[0], picked[1])
    gate = [jnp.exp(p - peak) for p in picked]
    both = gate[0] + gate[1]
    gates = [gate[0] / both, gate[1] / both]
    numbers = list(gates)
    for j in range(2):
        two = [raw[:, routes_n + 2 * j + i : routes_n + 2 * j + i + 1] for i in range(2)]
        peak = jnp.maximum(two[0], two[1])
        power = [jnp.exp(p - peak) for p in two]
        both = power[0] + power[1]
        numbers += [power[0] / both, power[1] / both]
    numbers += columns
    value = jnp.zeros((rows_n, 128), full)
    for i, number in enumerate(numbers):
        value = jnp.where(lane == i, number, value)
    aux[...] = value
    here = place[1]
    along = []
    for k in range(2):
        route = routes[l, m, k : k + 1, :]
        along.append(jnp.where(route < experts_n, route ^ here, route).astype(full))
    index_rows = max(16, experts_n)
    expert = sublanes(index_rows, rows_n).astype(full)
    member = ((along[0] == expert) | (along[1] == expert)).astype(full).astype(low)
    before = (sublanes(rows_n, rows_n) < lanes(rows_n, rows_n)).astype(full).astype(low)
    rank = dot(member, before)
    slot = sublanes(capacity, rows_n).astype(full)
    picks = [
        jnp.concatenate(
            [
                ((slot == rank[k : k + 1, :]) & (route == k)).astype(full)
                for k in range(experts_n)
            ],
            axis=0,
        )
        for route in along
    ]
    pick[:, 0:rows_n] = picks[0].astype(low)
    pick[:, rows_n : 2 * rows_n] = picks[1].astype(low)
    sent = [dot((picks[0] + picks[1]).astype(low), h)]
    if last:
        dstream = cotangent[m].astype(full)
        sent.append(
            dot(picks[0].astype(low), (gates[0] * dstream).astype(low))
            + dot(picks[1].astype(low), (gates[1] * dstream).astype(low))
        )
    fill_bufs(bufs, earlier, sent, capacity)


def route_columns(aux):
    return [aux[:, 6 + k : 7 + k] for k in range(2)]


def route_values(experts_n, pick, values_low, aux, columns, h, vec):
    rows_n = h.shape[0]
    twice = jnp.concatenate([pick[...], pick[...]], axis=0)
    both = dot_tn(twice, values_low)
    values = []
    for k in range(2):
        route = columns[k]
        scale = (route == experts_n + 1).astype(full)
        value = both[k * rows_n : (k + 1) * rows_n]
        for j in range(2):
            here = (route == experts_n + 2 + j).astype(full)
            scale = scale + here * aux[:, 2 + 2 * j : 3 + 2 * j]
            value = value + (here * aux[:, 3 + 2 * j : 4 + 2 * j]) * vec[j : j + 1, :]
        values.append(value + scale * h)
    return values


def combine_kernel(l, m, experts_n, capacity, arrivals_n, *refs):
    arrivals = refs[:arrivals_n]
    pick, aux, h_moe, mid, vec, gains, stream, h_next = refs[arrivals_n:]
    columns = route_columns(aux)
    values = route_values(
        experts_n, pick, stack_rows(arrivals, m * capacity, capacity), aux, columns,
        h_moe[...].astype(full), vec[l],
    )
    rows = mid[...] + aux[:, 0:1] * values[0] + aux[:, 1:2] * values[1]
    stream[...] = rows
    h_next[...] = (rows * rms_scale(rows) * gains[l + 1, 0:1, :]).astype(low)


def route_back(
    l, experts_n, routes_n, dstream, values, pick, aux, columns, h_low, vec, router, dnext,
    small,
):
    lane = lanes(dstream.shape[0])
    h = h_low.astype(full)
    gates = [aux[:, k : k + 1] for k in range(2)]
    dgate = [jnp.sum(dstream * v, axis=-1, keepdims=True) for v in values]
    mean = gates[0] * dgate[0] + gates[1] * dgate[1]
    dlogits = dnext
    for k in range(2):
        dlogits = dlogits + jnp.where(lane.astype(full) == columns[k], gates[k] * (dgate[k] - mean), 0.0)

    def gate_of(route):
        return sum((columns[k] == route).astype(full) * gates[k] for k in range(2))

    along_h = jnp.sum(dstream * h, axis=-1, keepdims=True)
    scale = gate_of(experts_n + 1)
    both = dlogits
    for j in range(2):
        share = gate_of(experts_n + 2 + j)
        mix = [aux[:, 2 + 2 * j + i : 3 + 2 * j + i] for i in range(2)]
        along_v = jnp.sum(dstream * vec[l, j : j + 1, :], axis=-1, keepdims=True)
        dm = [share * along_h, share * along_v]
        inner = mix[0] * dm[0] + mix[1] * dm[1]
        for i in range(2):
            both = jnp.where(lane == routes_n + 2 * j + i, mix[i] * (dm[i] - inner), both)
        scale = scale + mix[0] * share
        small[24 + j : 25 + j, :] = jnp.sum((mix[1] * share) * dstream, axis=0, keepdims=True)
    top, rest = split2(both)
    dlocal = scale * dstream + (
        dot(top, router[l, 0:128, :])
        + dot(top, router[l, 128:256, :])
        + dot(rest, router[l, 0:128, :])
    )
    small[0:24, :] = (dot_tn(top, h_low) + dot_tn(rest, h_low))[0:24]
    return dlogits, dlocal


def norm_back(dh, rows, gain):
    scale = rms_scale(rows)
    unit = rows * scale
    dn = dh * gain
    drows = scale * (dn - unit * jnp.mean(dn * unit, axis=-1, keepdims=True))
    return drows, jnp.sum(dh * unit, axis=0, keepdims=True)


def turn_kernel(l, m, experts_n, routes_n, capacity, arrivals_n, earlier_n, *refs):
    arrivals = refs[:arrivals_n]
    pick, aux, h_moe, mid, vec, gains, router, cotangent = refs[
        arrivals_n : arrivals_n + 8
    ]
    at = arrivals_n + 8
    earlier = refs[at : at + earlier_n]
    out, dmid, dattn, dlogits_out, small = refs[at + earlier_n :]
    micro = len(earlier) + 1
    columns = route_columns(aux)
    h_low = h_moe[...]
    values = route_values(
        experts_n, pick, stack_rows(arrivals, m * capacity, capacity), aux, columns,
        h_low.astype(full), vec[l],
    )
    rows = mid[...]
    for i, ref in enumerate(earlier):
        out[i] = ref[i]
    out[m] = (rows + aux[:, 0:1] * values[0] + aux[:, 1:2] * values[1]).astype(low)
    for i in range(m + 1, out.shape[0]):
        out[i] = jnp.zeros(out.shape[1:], low)
    small[24:32, :] = jnp.zeros((8, small.shape[1]), full)
    dstream = cotangent[m].astype(full)
    dlogits, dlocal = route_back(
        l, experts_n, routes_n, dstream, values, pick, aux, columns, h_low, vec, router,
        jnp.zeros((dstream.shape[0], 128), full), small,
    )
    dlogits_out[...] = dlogits
    rows_n = rows.shape[0]
    both = pick[:, 0:rows_n] + pick[:, rows_n : 2 * rows_n]
    twice = jnp.concatenate([both, both], axis=0)
    at = (cotangent.shape[0] + m) * capacity
    dh = dlocal + dot_tn(twice, stack_rows(arrivals, at, capacity))
    drows, dgain = norm_back(dh, rows, gains[l, 1:2, :])
    small[26:27, :] = dgain
    value = dstream + drows
    dmid[...] = value
    dattn[...] = value.astype(low)


def next_back_kernel(l, m, experts_n, routes_n, capacity, arrivals_n, earlier_n, *refs):
    arrivals = refs[:arrivals_n]
    (keep, arrived, across, stream, gains, dmid, pick, aux, h_moe, vec, router,
     dnext) = refs[arrivals_n : arrivals_n + 12]
    at = arrivals_n + 12
    earlier = refs[at : at + earlier_n]
    dstream_out, dlogits_out, dlocal_out, small, *bufs = refs[at + earlier_n :]
    rows_n = keep.shape[0]
    dh = keep[...].astype(full) + arrived[0:rows_n, :].astype(full) + across[...].astype(full)
    drows, dgain = norm_back(dh, stream[...], gains[l + 1, 0:1, :])
    dstream = dmid[...] + drows
    dstream_out[...] = dstream
    small[24:32, :] = jnp.zeros((8, small.shape[1]), full)
    small[27:28, :] = dgain
    columns = route_columns(aux)
    h_low = h_moe[...]
    values = route_values(
        experts_n, pick, stack_rows(arrivals, m * capacity, capacity), aux, columns,
        h_low.astype(full), vec[l],
    )
    gates = [aux[:, k : k + 1] for k in range(2)]
    sent = dot(pick[:, 0:rows_n], (gates[0] * dstream).astype(low)) + dot(
        pick[:, rows_n : 2 * rows_n], (gates[1] * dstream).astype(low)
    )
    fill_bufs(bufs, earlier, [sent], capacity)
    dlogits, dlocal = route_back(
        l, experts_n, routes_n, dstream, values, pick, aux, columns, h_low, vec, router,
        dnext[...], small,
    )
    dlogits_out[...] = dlogits
    dlocal_out[...] = dlocal


def expert_norm_back_kernel(l, m, capacity, arrivals_n, *refs):
    arrivals = refs[:arrivals_n]
    pick, dlocal, mid, gains, dstream, dmid, dattn, dgain_out = refs[arrivals_n:]
    rows_n = mid.shape[0]
    both = pick[:, 0:rows_n] + pick[:, rows_n : 2 * rows_n]
    twice = jnp.concatenate([both, both], axis=0)
    dh = dlocal[...] + dot_tn(twice, stack_rows(arrivals, m * capacity, capacity))
    drows, dgain = norm_back(dh, mid[...], gains[l, 1:2, :])
    dgain_out[...] = jnp.broadcast_to(dgain, dgain_out.shape)
    value = dstream[...] + drows
    dmid[...] = value
    dattn[...] = value.astype(low)


def input_back_kernel(micro, *refs):
    tokens, gains, out = refs[4 * micro :]
    for m in range(micro):
        keep, arrived, across, dmid = refs[4 * m : 4 * m + 4]
        rows_n = keep.shape[0]
        dh = keep[...].astype(full) + arrived[0:rows_n, :].astype(full) + across[...].astype(full)
        drows, _ = norm_back(dh, tokens[m].astype(full), gains[0, 0:1, :])
        out[m] = dmid[...] + drows


def expert_fwd_kernel(l, blocks_n, *refs):
    gate_up, down, keep, send = refs[blocks_n:]
    rows = stack_rows(refs[:blocks_n])
    g = dot(rows, gate_up[l, 0, 0])
    u = dot(rows, gate_up[l, 0, 1])
    hidden = (g * jax.nn.sigmoid(g) * u).astype(low)
    value = dot(hidden, down[l, 0]).astype(low)
    half = keep.shape[0]
    keep[...] = value[0:half]
    send[...] = value[half:]


def expert_back(l, rows, grads, gate_up, down):
    g = dot(rows, gate_up[l, 0, 0])
    u = dot(rows, gate_up[l, 0, 1])
    dhidden = dot_nt(grads, down[l, 0])
    s = jax.nn.sigmoid(g)
    silu = g * s
    hidden = (silu * u).astype(low)
    dg = (dhidden * u * s * (1.0 + g * (1.0 - s))).astype(low)
    du = (dhidden * silu).astype(low)
    drows = (dot_nt(dg, gate_up[l, 0, 0]) + dot_nt(du, gate_up[l, 0, 1])).astype(low)
    return hidden, dg, du, drows


def expert_both_kernel(l, blocks_n, *refs):
    blocks = refs[:blocks_n]
    gate_up, down, keep, send, hidden_out, dgu_out = refs[blocks_n:]
    each = blocks[0].shape[0] // 2
    rows = stack_rows(blocks, 0, each)
    grads = stack_rows(blocks, each, each)
    hidden, dg, du, drows = expert_back(l, rows, grads, gate_up, down)
    hidden_out[...] = hidden
    width = dg.shape[1]
    dgu_out[:, 0:width] = dg
    dgu_out[:, width : 2 * width] = du
    value = dot(hidden, down[l, 0]).astype(low)
    for i in range(blocks_n):
        out = keep if i < blocks_n // 2 else send
        at = 2 * each * (i % (blocks_n // 2))
        out[at : at + each, :] = value[i * each : (i + 1) * each]
        out[at + each : at + 2 * each, :] = drows[i * each : (i + 1) * each]


def expert_bwd_kernel(l, blocks_n, *refs):
    gate_up, down, keep, send, hidden_out, dgu_out = refs[2 * blocks_n :]
    rows = stack_rows(refs[:blocks_n])
    grads = stack_rows(refs[blocks_n : 2 * blocks_n])
    hidden, dg, du, drows = expert_back(l, rows, grads, gate_up, down)
    hidden_out[...] = hidden
    width = dg.shape[1]
    dgu_out[:, 0:width] = dg
    dgu_out[:, width : 2 * width] = du
    half = keep.shape[0]
    keep[...] = drows[0:half]
    send[...] = drows[half:]


def turned(n):
    order = [0]
    bit = n // 2
    while bit:
        order = order + [k + bit for k in order]
        bit //= 2
    bits = n.bit_length() - 1
    return [int(format(i, "b").zfill(bits)[::-1], 2) for i in range(n)]


def expert_weights_kernel(blocks_n, apart, pieces, packed, parts, *refs):
    place = refs[0]
    refs = refs[1:]
    if packed:
        ends = refs[-1 - 2 * parts :]
        one, two = refs[-3 - 2 * parts : -1 - 2 * parts]
        extra = (one[...].astype(full) + two[...].astype(full)).astype(low)
        refs = (*refs[: -3 - 2 * parts], *ends)
    if apart:
        rows = stack_rows(refs[:blocks_n])
        grads = stack_rows(refs[blocks_n : 2 * blocks_n])
    else:
        each = refs[0].shape[0] // 2
        rows = stack_rows(refs[:blocks_n], 0, each)
        grads = stack_rows(refs[:blocks_n], each, each)
    hidden, dgu, *outs, total = refs[-3 - 2 * parts :]
    width = dgu.shape[1]
    total[:, 0:width] = dot_tn(rows, dgu[...]).astype(low)
    total[:, width : width + hidden.shape[1]] = dot_tn(grads, hidden[...]).astype(low)
    share = total.shape[0] // pieces
    for i, k in enumerate(turned(pieces)):
        at = pl.multiple_of((place[2] ^ k) * share, share)
        mine = [total[pl.ds(at, share), :]]
        if packed:
            more = extra.shape[0] // pieces // 2
            mine.append(
                jnp.concatenate(
                    [extra[(2 * i + n) * more : (2 * i + n + 1) * more] for n in range(2)], axis=1
                )
            )
        unit = jnp.concatenate(mine, axis=0)
        begin = 0
        for part in range(parts):
            out = outs[2 * part + 2 * i // pieces]
            rows_n = out.shape[0] // (pieces // 2)
            to = i % (pieces // 2) * rows_n
            out[to : to + rows_n, :] = unit[begin : begin + rows_n]
            begin += rows_n


def expert_total_kernel(layers, counts, *refs):
    gate_up, down, *packed = refs[sum(counts) :]
    width, share = gate_up.shape[4], gate_up.shape[3]
    for l in range(layers):
        mine = refs[sum(counts[:l]) : sum(counts[: l + 1])]
        total = jnp.concatenate(
            [a[...].astype(full) + b[...].astype(full) for a, b in zip(mine[::2], mine[1::2])],
            axis=0,
        )
        for i in range(2):
            gate_up[l, 0, i] = total[0:share, i * width : (i + 1) * width]
        down[l, 0] = total[0:share, 2 * width : 3 * width]
        if packed and l < layers - 1:
            half = packed[l].shape[1]
            packed[l][...] = jnp.concatenate(
                [total[share:, 0:half], total[share:, half : 2 * half]], axis=0
            )


def attn_total_kernel(layers, counts, *refs):
    qkv, out = refs[sum(counts) :]
    pair = 2 * HDIM
    for l in range(layers):
        mine = refs[sum(counts[:l]) : sum(counts[: l + 1])]
        total = mine[0][...].astype(full)
        for ref in mine[1:]:
            total = total + ref[...].astype(full)
        third = total[:, 4 * pair :]
        for i in range(3):
            qkv[l, i, :, 0:pair] = total[:, i * pair : (i + 1) * pair]
            qkv[l, i, :, pair : pair + HDIM] = third[:, i * HDIM : (i + 1) * HDIM]
        out[l, 0:pair, :] = total[:, 3 * pair : 4 * pair].T
        out[l, pair : pair + HDIM, :] = third[:, 3 * HDIM :].T


def swap(x, axis, k):
    n = lax.axis_size(axis)
    return lax.ppermute(x, axis, [(i, i ^ k) for i in range(n)])


def swap_pair(x, k, j):
    experts_n = lax.axis_size("expert")
    tensor_n = lax.axis_size("tensor")
    if j == 0:
        return swap(x, "expert", k)
    if k == 0:
        return swap(x, "tensor", j)
    table = [
        (e * tensor_n + t, (e ^ k) * tensor_n + (t ^ j))
        for e in range(experts_n)
        for t in range(tensor_n)
    ]
    return lax.ppermute(x, ("expert", "tensor"), table)


def attend(blocks, call, nears=None):
    results = []
    for m, block in enumerate(blocks):
        near = swap(nears[m] if nears else block, "tensor", 1)
        far = swap(block, "tensor", 2)
        pack = [block, near, far, swap(far, "tensor", 1)]
        (keep, away, send, *rest), extra = call(m, pack, [])
        arrived = swap(send, "tensor", 1)
        (total,) = run_kernel(
            add_far_kernel, [shape_of(away.shape, low)], [away, arrived], "add_far", 8
        )
        results.append(([keep, arrived, swap(total, "tensor", 2)], extra))
    return results


def send_rows(bufs):
    experts_n = len(bufs)
    far = [swap_pair(buf, k, 2) for k, buf in enumerate(bufs)]
    near = [bufs[0]] + [swap_pair(bufs[k], k, 0) for k in range(1, experts_n)]
    held = near + far
    return held + [swap(x, "tensor", 1) for x in held]


def return_rows(keep, send, each):
    experts_n = lax.axis_size("expert")
    arrived = swap(send, "tensor", 1)
    sums = run_kernel(
        add_back_kernel,
        [shape_of((each, keep.shape[1]), low)] * (2 * experts_n),
        [keep, arrived],
        "add_back",
        8,
    )
    far = [swap_pair(sums[experts_n + k], k, 2) for k in range(experts_n)]
    near = [sums[0]] + [swap_pair(sums[k], k, 0) for k in range(1, experts_n)]
    return near + far, sums[0]


def small_pack_kernel(layers, micro, routes_n, *refs):
    smalls = [refs[l * micro : (l + 1) * micro] for l in range(layers)]
    at = layers * micro
    gains = [refs[at + l * micro : at + (l + 1) * micro] for l in range(layers - 1)]
    *first_gains, out = refs[at + (layers - 1) * micro :]
    pieces = []
    last_gain = sum(ref[0:1, :] for ref in first_gains)
    for l in range(layers):
        total = smalls[l][0][...]
        for ref in smalls[l][1:]:
            total = total + ref[...]
        if l < layers - 1:
            moe = gains[l][0][0:1, :]
            for ref in gains[l][1:]:
                moe = moe + ref[0:1, :]
        else:
            moe = total[26:27]
        pieces += [total[0 : routes_n + 4], total[24:26], moe, last_gain]
        last_gain = total[27:28]
    rows = sum(p.shape[0] for p in pieces)
    if out.shape[0] > rows:
        pieces.append(jnp.zeros((out.shape[0] - rows, out.shape[1]), full))
    out[...] = jnp.concatenate(pieces, axis=0).astype(low)


def sum_kernel(*refs):
    total = refs[0][...].astype(full)
    for ref in refs[1:-1]:
        total = total + ref[...].astype(full)
    refs[-1][...] = total


def small_out_kernel(layers, routes_n, parts, *refs):
    attn_gains, moe_gains, router, proj, vec = refs[parts:]
    total = refs[0][...]
    for ref in refs[1:parts]:
        total = total + ref[...]
    each = routes_n + 8
    for l in range(layers):
        mine = total[l * each : (l + 1) * each]
        for r in range(routes_n):
            router[r, l : l + 1, :] = mine[r : r + 1]
        proj[l] = mine[routes_n : routes_n + 4]
        vec[l] = mine[routes_n + 4 : routes_n + 6]
        moe_gains[l : l + 1, :] = mine[routes_n + 6 : routes_n + 7]
        attn_gains[l : l + 1, :] = mine[routes_n + 7 : routes_n + 8]


def sum_rows(parts):
    (out,) = run_kernel(sum_kernel, [shape_of(parts[0].shape, full)], parts, "sum", 8)
    return out


def sum_all(rows):
    over_dp = sum_rows([rows] + [swap(rows, "dp", k) for k in range(1, lax.axis_size("dp"))])
    over_cores = sum_rows([over_dp, swap(over_dp, "tensor", 1)])
    parts = [over_cores]
    for j in (0, 2):
        for k in range(lax.axis_size("expert")):
            if (j, k) != (0, 0):
                parts.append(swap_pair(over_cores, k, j))
    return parts, over_dp, over_cores


def pieces_of(grad, axis):
    n = lax.axis_size(axis)
    here = lax.axis_index(axis)

    def piece(k):
        return lax.dynamic_index_in_dim(grad, here ^ k, 0, keepdims=False)

    return [piece(0)] + [swap(piece(k), axis, k) for k in range(1, n)]


def local(
    tokens,
    cotangent,
    row_order,
    lengths,
    routes,
    norm_gains,
    w_qkv,
    w_out,
    w_gate_up,
    w_down,
    w_router,
    const_proj,
    const_vec,
):
    layers = w_qkv.shape[0]
    micro_n, rows_n, model = tokens.shape
    routes_n = w_router.shape[2]
    experts_n = lax.axis_size("expert")
    tensor_n = lax.axis_size("tensor")
    dp_n = lax.axis_size("dp")
    capacity = 9 * rows_n // (4 * (experts_n + 4))
    heads_width = w_qkv.shape[3]
    hidden_n = w_down.shape[2]
    seq = tensor_n * rows_n
    each = micro_n * capacity
    half_rows = 2 * experts_n * each
    blocks_n = 4 * experts_n
    arrivals_n = 2 * experts_n
    micro = range(micro_n)
    expert_limit = 12 if half_rows <= 384 else 40
    assert tensor_n == 4 and heads_width == 3 * HDIM and rows_n == 128 and micro_n == 2

    w_qkv = jnp.swapaxes(w_qkv, 2, 3)
    routes = jnp.swapaxes(routes, 2, 3)
    hs = list(
        run_kernel(
            norm_kernel,
            [shape_of((rows_n, model), low)] * micro_n,
            [tokens, norm_gains],
            "norm",
            8,
            fetched=2,
        )
    )
    place = jnp.stack([lax.axis_index(a) for a in ("tensor", "expert", "dp")]).astype(jnp.int32)
    cos, sin, bias, router_low, again = run_kernel(
        functools.partial(tables_kernel, tensor_n),
        [
            shape_of((micro_n, seq, 128), full),
            shape_of((micro_n, seq, 128), full),
            shape_of((micro_n, seq, seq), low),
            shape_of((layers, 384, model), low),
            shape_of((rows_n, model), low),
        ],
        [
            place, lengths, hs[1], row_order, jnp.transpose(w_router, (2, 0, 1)),
            jnp.swapaxes(const_proj, 1, 2),
        ],
        "tables",
        12,
        scalars=2,
        fetched=3,
    )

    def attn_fwd(l, blocks, nears):
        def call(m, heads, after):
            results = run_kernel(
                functools.partial(attn_fwd_kernel, l, m, tensor_n),
                [
                    shape_of((rows_n, model), low),
                    shape_of((rows_n, model), low),
                    shape_of((2 * rows_n, model), low),
                    shape_of((seq, 768), low),
                    shape_of((seq, heads_width), low),
                    shape_of((seq, 128), full),
                ],
                [*heads, w_qkv, w_out, cos, sin, bias],
                "attn_fwd",
                12,
                after=after,
            )
            saved, mixed, logsum = results[3:]
            return results, dict(heads=heads, saved=saved, mixed=mixed, logsum=logsum)

        return attend(blocks, call, nears)

    first_gains = []

    def attn_bwd(l, blocks, kept, after):
        def call(m, grads, after_here):
            results = run_kernel(
                functools.partial(attn_bwd_kernel, l, m, tensor_n),
                [
                    shape_of((rows_n, model), low),
                    shape_of((rows_n, model), low),
                    shape_of((2 * rows_n, model), low),
                    shape_of((3, seq, heads_width), low),
                ]
                + [shape_of((8, model), full)] * (l == 0),
                [
                    *grads, w_qkv, w_out, cos, sin, bias, kept[m][l]["saved"],
                    kept[m][l]["logsum"], *([] if l else [*kept[m][l]["heads"], norm_gains]),
                ],
                "attn_bwd",
                12,
                after=[*after_here, *after[m]],
            )
            if not l:
                first_gains.append(results[4])
            return results, [*kept[m][l]["heads"], *grads, results[3], kept[m][l]["mixed"]]

        return attend(blocks, call)

    share = model // (dp_n * experts_n)

    woven = experts_n == 2 and dp_n == 4 and share % 32 == 0

    def attn_weights(ins, after, last):
        if last and woven:
            units = WOVEN
            outs = [shape_of((4 * share // 2, model), low)] * 4
        elif woven:
            units = [[(z, e, 0) for z in turned(dp_n)] for e in (0, 1)]
            outs = [shape_of((dp_n * share, model), low)] * 2
        else:
            units = []
            outs = [shape_of((model, model), low)]
        return run_kernel(
            functools.partial(attn_weights_kernel, tensor_n, micro_n, dp_n, experts_n, units),
            outs,
            [place, *ins],
            "attn_weights",
            12,
            scratch=[pltpu.VMEM((model, model), low)] if units else [],
            scalars=1,
            after=after,
        )

    def weave(one, one_in, two, two_in, after=()):
        return run_kernel(
            weave_kernel,
            [shape_of(one.shape, low)] * 2,
            [one, one_in, two, two_in],
            "weave",
            12,
            after=after,
        )

    def attn_sums(parts, after=(), after_last=()):
        if len(parts) == 1:
            grad = parts[0].reshape(dp_n, experts_n, share, model)
            mine = pieces_of(jnp.swapaxes(grad, 0, 1), "expert")
            total = sum(x.astype(full) for x in mine).astype(low)
            return pieces_of(total, "dp")
        one, one_out, two, two_out = parts
        two_in = swap(two_out, "dp", 1)
        one_in = swap(one_out, "expert", 1)
        one, one_out, two, two_out = halves([(one, one_in), (two, two_in)], after)
        one_in = swap(one_out, "dp", 1)
        two_in = swap(two_out, "expert", 1)
        keep, send = weave(one, one_in, two, two_in, after_last)
        return [keep, swap(send, "dp", 2)]

    def expert_weights(blocks, hidden, dgu, apart, after, packed=(), split=False):
        unit = model // dp_n + sum(x.shape[0] // (2 * dp_n) for x in packed[:1])
        first = -(-unit // 32) * 16
        sizes = [first, unit - first] if packed or split else [unit]
        return run_kernel(
            functools.partial(
                expert_weights_kernel, blocks_n, apart, dp_n, bool(packed), len(sizes)
            ),
            [shape_of((dp_n // 2 * n, 3 * hidden_n), low) for n in sizes for _ in range(2)],
            [place, *blocks, hidden, dgu, *packed],
            "expert_weights",
            expert_limit,
            scratch=[pltpu.VMEM((model, 3 * hidden_n), low)],
            scalars=1,
            after=after,
        )

    def halves(pairs, after=()):
        return run_kernel(
            functools.partial(halves_kernel, len(pairs)),
            [
                shape_of((x.shape[0] // 2, x.shape[1]), low)
                for x, _ in pairs
                for _ in range(2)
            ],
            [x for pair in pairs for x in pair],
            "halves",
            12,
            after=after,
        )

    def halve_on(keep, came, after=()):
        bit = 1
        first = None
        while 2 * bit < dp_n:
            keep, send = halves([(keep, came)], after)
            after = ()
            bit *= 2
            first = send if first is None else first
            came = swap(send, "dp", bit)
        return [keep, came], first

    expert_outs = [
        shape_of((2 * half_rows, hidden_n), low),
        shape_of((2 * half_rows, 2 * hidden_n), low),
    ]

    stream = [tokens] * micro_n
    logits = [None] * micro_n
    kept = [[None] * layers for _ in micro]
    for l in range(layers):
        last = l == layers - 1
        kinds = 2 if last else 1
        bufs = []
        for m, (parts, k) in enumerate(attn_fwd(l, hs, None if l else [hs[0], again])):
            mid, h_moe, logits[m], aux, pick, *bufs = run_kernel(
                functools.partial(
                    mid_kernel, l, m, experts_n, routes_n, capacity, last, len(bufs)
                ),
                [
                    shape_of((rows_n, model), full),
                    shape_of((rows_n, model), low),
                    shape_of((rows_n, 128), full),
                    shape_of((rows_n, 128), full),
                    shape_of((experts_n * capacity, 2 * rows_n), low),
                ]
                + [shape_of(((m + 1) * kinds * capacity, model), low)] * experts_n,
                [place, *parts, stream[m], norm_gains, router_low, routes]
                + ([logits[m]] if l else [])
                + ([cotangent] if last else [])
                + bufs,
                "mid",
                12,
                scalars=1,
            )
            kept[m][l] = dict(
                k, mid=mid, h_moe=h_moe, aux=aux, pick=pick, stream=stream[m],
            )
        held = send_rows(bufs)
        if last:
            keep, send, hidden, dgu = run_kernel(
                functools.partial(expert_both_kernel, l, blocks_n),
                [shape_of((kinds * half_rows, model), low)] * 2 + expert_outs,
                [*held, w_gate_up, w_down],
                "expert_both",
                expert_limit,
            )
        else:
            keep, send = run_kernel(
                functools.partial(expert_fwd_kernel, l, blocks_n),
                [shape_of((half_rows, model), low)] * 2,
                [*held, w_gate_up, w_down],
                "expert_fwd",
                expert_limit,
            )
        arrivals, summed = return_rows(keep, send, kinds * each)
        for m in micro:
            kept[m][l]["held"] = held
            kept[m][l]["arrivals"] = arrivals
        if last:
            break
        for m in micro:
            k = kept[m][l]
            stream[m], hs[m] = run_kernel(
                functools.partial(combine_kernel, l, m, experts_n, capacity, arrivals_n),
                [shape_of((rows_n, model), full), shape_of((rows_n, model), low)],
                [
                    *arrivals, k["pick"], k["aux"], k["h_moe"], k["mid"], const_vec, norm_gains,
                ],
                "combine",
                12,
            )

    l = layers - 1
    expert_grads = [None] * layers
    expert_pieces = [None] * layers
    attn_pieces = [None] * layers
    smalls = [[None] * micro_n for _ in range(layers)]
    gains = [None] * (layers - 1)
    expert_grads[l] = expert_weights(held, hidden, dgu, False, [], split=woven)
    if woven:
        one, one_out, two, two_out = expert_grads[l]
        keep, first = weave(one, swap(one_out, "dp", 1), two, swap(two_out, "dp", 1))
        expert_pieces[l] = [keep, swap(first, "dp", 2)]
    else:
        expert_pieces[l], first = halve_on(
            expert_grads[l][0], swap(expert_grads[l][1], "dp", 1)
        )
    outputs = []
    dmid = [None] * micro_n
    dattn = [None] * micro_n
    dlogits = [None] * micro_n
    for m in micro:
        k = kept[m][l]
        out, dmid[m], dattn[m], dlogits[m], smalls[l][m] = run_kernel(
            functools.partial(
                turn_kernel, l, m, experts_n, routes_n, capacity, arrivals_n, len(outputs)
            ),
            [
                shape_of((micro_n, rows_n, model), low),
                shape_of((rows_n, model), full),
                shape_of((rows_n, model), low),
                shape_of((rows_n, 128), full),
                shape_of((32, model), full),
            ],
            [
                *arrivals, k["pick"], k["aux"], k["h_moe"], k["mid"], const_vec, norm_gains,
                router_low, cotangent, *outputs,
            ],
            "turn",
            12,
            after=[expert_grads[l][0]],
        )
        outputs = [out]
    (outputs,) = outputs
    before_bwd = [[], [first]]
    attn_in = None
    while True:
        parts = [None] * micro_n
        grads_in = []
        for m, (parts[m], more) in enumerate(attn_bwd(l, dattn, kept, before_bwd)):
            grads_in += more
        attn_in = grads_in
        if l == 0:
            break
        l -= 1
        grad = attn_weights(attn_in, [], False)
        packed = []
        if woven:
            packed = [grad[0], swap(grad[1], "expert", 1)]
        else:
            attn_pieces[l + 1] = attn_sums(grad)
        bufs = []
        dstream = [None] * micro_n
        dlocal = [None] * micro_n
        for m in micro:
            k = kept[m][l]
            dstream[m], dlogits[m], dlocal[m], smalls[l][m], *bufs = run_kernel(
                functools.partial(
                    next_back_kernel, l, m, experts_n, routes_n, capacity, arrivals_n, len(bufs)
                ),
                [
                    shape_of((rows_n, model), full),
                    shape_of((rows_n, 128), full),
                    shape_of((rows_n, model), full),
                    shape_of((32, model), full),
                ]
                + [shape_of(((m + 1) * capacity, model), low)] * experts_n,
                [
                    *k["arrivals"], *parts[m], kept[m][l + 1]["stream"], norm_gains, dmid[m],
                    k["pick"], k["aux"], k["h_moe"], const_vec, router_low, dlogits[m],
                    *bufs,
                ],
                "next_back",
                12,
                after=[] if m else [grad[0]],
            )
        held = kept[0][l]["held"]
        grads = send_rows(bufs)
        keep, send, hidden, dgu = run_kernel(
            functools.partial(expert_bwd_kernel, l, blocks_n),
            [shape_of((half_rows, model), low)] * 2 + expert_outs,
            [*held, *grads, w_gate_up, w_down],
            "expert_bwd",
            expert_limit,
            after=[expert_pieces[l + 1][1], *packed[1:]],
        )
        arrivals, summed = return_rows(keep, send, each)
        expert_grads[l] = expert_weights(
            [*held, *grads], hidden, dgu, True, [], packed
        )
        expert_came = [swap(x, "dp", 1) for x in expert_grads[l][1::2]]
        gains[l] = [None] * micro_n
        for m in micro:
            k = kept[m][l]
            dmid[m], dattn[m], dgain = run_kernel(
                functools.partial(expert_norm_back_kernel, l, m, capacity, arrivals_n),
                [
                    shape_of((rows_n, model), full),
                    shape_of((rows_n, model), low),
                    shape_of((8, model), full),
                ],
                [*arrivals, k["pick"], dlocal[m], k["mid"], norm_gains, dstream[m]],
                "expert_norm_back",
                12,
                after=[expert_grads[l][0]],
            )
            gains[l][m] = dgain
        pieces, first = halve_on(expert_grads[l][0], expert_came[0], [dattn[0]])
        expert_pieces[l] = pieces
        before_bwd = [[first], []]
        if len(expert_came) > 1 and l:
            pieces, first = halve_on(expert_grads[l][2], expert_came[1])
            expert_pieces[l] = expert_pieces[l] + pieces
            before_bwd[1].append(first)

    first = []
    if layers > 1 and len(expert_came) > 1:
        pieces, sent = halve_on(expert_grads[0][2], expert_came[1], [parts[-1][0]])
        expert_pieces[0] = expert_pieces[0] + pieces
        first = [sent]
    each_small = routes_n + 8
    (small,) = run_kernel(
        functools.partial(small_pack_kernel, layers, micro_n, routes_n),
        [shape_of((-(-layers * each_small // 16) * 16, model), low)],
        [x for xs in [*smalls, *gains, first_gains] for x in xs],
        "small_pack",
        8,
    )
    small, over_dp, over_cores = sum_all(small)
    grad = attn_weights(attn_in, first, True)
    attn_pieces[0] = attn_sums(grad, expert_pieces[0][1:2] if first else [], [over_cores])
    (grad_tokens,) = run_kernel(
        functools.partial(input_back_kernel, micro_n),
        [shape_of((micro_n, rows_n, model), full)],
        [x for m in micro for x in (*parts[m], dmid[m])] + [tokens, norm_gains],
        "input_back",
        12,
    )

    attn_gains, moe_gains, grad_router, grad_proj, grad_vec = run_kernel(
        functools.partial(small_out_kernel, layers, routes_n, len(small)),
        [
            shape_of((layers, model), full),
            shape_of((layers, model), full),
            shape_of((routes_n, layers, model), full),
            shape_of((layers, 4, model), full),
            shape_of((layers, 2, model), full),
        ],
        small,
        "small_out",
        8,
    )
    grad_gate_up, grad_down, *packed = run_kernel(
        functools.partial(expert_total_kernel, layers, [len(x) for x in expert_pieces]),
        [
            shape_of((layers, 1, 2, model // dp_n, hidden_n), full),
            shape_of((layers, 1, model // dp_n, hidden_n), full),
        ]
        + [shape_of((share, model), full)] * (layers - 1 if woven else 0),
        [x for pieces in expert_pieces for x in pieces],
        "expert_total",
        12,
        after=[grad[0]],
    )
    if woven:
        attn_pieces[1:] = [[x] for x in packed]
    grad_qkv, grad_out = run_kernel(
        functools.partial(attn_total_kernel, layers, [len(x) for x in attn_pieces]),
        [
            shape_of((layers, 3, share, heads_width), full),
            shape_of((layers, heads_width, share), full),
        ],
        [x for pieces in attn_pieces for x in pieces],
        "attn_total",
        12,
    )
    return (
        outputs,
        grad_tokens,
        attn_gains,
        moe_gains,
        grad_qkv,
        grad_out,
        grad_gate_up,
        jnp.swapaxes(grad_down, 2, 3),
        jnp.transpose(grad_router, (1, 2, 0)),
        jnp.swapaxes(grad_proj, 1, 2),
        grad_vec,
    )


def solution(mesh):
    return jax.shard_map(
        local,
        mesh=mesh,
        in_specs=(
            P(None, ("dp", "expert", "tensor"), None),
            P(None, ("dp", "expert", "tensor"), None),
            P(None, ("dp", "expert"), None),
            P(None, ("dp", "expert"), None),
            P(None, None, ("dp", "expert", "tensor"), None),
            P(),
            P(None, None, None, "tensor"),
            P(None, "tensor", None),
            P(None, "expert", None, None, "tensor"),
            P(None, "expert", "tensor", None),
            P(),
            P(),
            P(),
        ),
        out_specs=(
            P(None, ("dp", "expert", "tensor"), None),
            P(None, ("dp", "expert", "tensor"), None),
            P(),
            P(),
            P(None, None, ("dp", "expert"), "tensor"),
            P(None, "tensor", ("dp", "expert")),
            P(None, "expert", None, "dp", "tensor"),
            P(None, "expert", "tensor", "dp"),
            P(),
            P(),
            P(),
        ),
        check_vma=False,
    )
```
